256 devices in a mesh: mem: 8 (over x, core), state: 32 (over y, z).
Axes of the slice: x: 4, y: 4, z: 8, core: 2. Of those that a mesh axis runs over, the one named last changes fastest.
Arguments:
- ensemble: float32 [512, 1024, 256], P('mem', 'state'), may hold values from -12 to 12
- spreading_coefficient: float32 [1024, 256], P('state'), may hold values from 0.1 to 0.24
- obs_anom: bfloat16 [32, 128, 512], P('state'), may hold values from -6 to 6
- obs_weight: bfloat16 [32, 128, 512], P('state'), may hold values from -6 to 6
- taper_table: float32 [8, 128, 128], replicated, may hold values from 0.1 to 1
- obs_block: int32 [2048, 4], P('state'), may hold values from 0 to 31, as said below
- taper_id: int32 [2048, 4], P('state'), may hold values from 0 to 7
Outputs:
- forecast: float32 [512, 1024, 256], P('mem', 'state')
The draws below stay inside these ranges and needn't reach their ends.
Inputs may be any that keep to these rules, and one draw needn't show every extreme that they name: `obs_block`: the 4 block numbers of one tile are distinct.
All inputs are finite; a program needn't handle non-finite values.
Results may differ from the reference program's by a relative error of at most 0.00105.
Values may be sent and summed in bfloat16 or wider, within the bound.
No kernel may reach another device: no remote copies, remote signals or barrier semaphores. Data moves between devices by JAX's collectives and lax.ppermute only.
A program may use at most 64 MiB of HBM per device.

```python
import jax
import jax.numpy as jnp
from jax import lax

MEMBERS = 512
COLUMNS = 256
TILE = 128
SLOTS = 4
OBS_BLK = 128
PATTERNS = 8
FSTEPS = 4
NROWS = 1024
NBLK = 32
NTILES = 2048


def draw_obs_block(key, part):
    key = jax.random.fold_in(key, 11)
    scores = jax.random.randint(key, (NTILES, NBLK), 0, 1 << 20) * NBLK + jnp.arange(NBLK, dtype=jnp.int32)[None, :]
    values, chosen = lax.top_k(scores, SLOTS)
    return chosen.astype(jnp.int32)


def draw_ensemble(key, part):
    key = jax.random.fold_in(key, 5)
    base_key = jax.random.fold_in(key, 1)
    noise_key = jax.random.fold_in(key, 2)
    common = 2.0 * jax.random.normal(base_key, (NROWS, COLUMNS), jnp.float32)
    spread = jax.random.normal(noise_key, (MEMBERS, NROWS, COLUMNS), jnp.float32)
    return jnp.clip(common[None] + spread, -12.0, 12.0)


def place_ends(array, own_key, low, largest):
    spot = [jax.random.randint(jax.random.fold_in(own_key, axis), (), 0, length) for axis, length in enumerate(array.shape)]
    main_axis = array.shape.index(max(array.shape))
    neighbour = spot[:main_axis] + [(spot[main_axis] + 1) % array.shape[main_axis]] + spot[main_axis + 1:]
    return array.at[tuple(spot)].set(low).at[tuple(neighbour)].set(largest)


def steps_of(stream_key, dims, cuts, smallest, largest):
    loudness, own = 1.0, jax.random.fold_in(stream_key, 6)
    for position, parts in cuts:
        draws = jnp.exp(jax.random.uniform(jax.random.fold_in(own, position), (parts,), jnp.float32, smallest / len(cuts), largest / len(cuts)))
        loudness = loudness * jnp.repeat(draws, dims[position] // parts).reshape([-1 if axis == position else 1 for axis in range(len(dims))])
    return loudness


def noise(key, dims, scale, limit, shards=(), kind=jnp.bfloat16):
    values = scale * jax.random.normal(key, dims, jnp.float32)
    if shards:
        values = values * steps_of(key, dims, shards, -0.22, 0.18)
    return jnp.clip(values, -limit, limit).astype(kind)


def setup_inputs(seed: int = 0) -> dict:
    keys = jax.random.split(jax.random.key(seed), 8)
    return {
        "ensemble": draw_ensemble(jax.random.fold_in(keys[7], 71), 0),
        "spreading_coefficient": jnp.clip(0.1 + 0.13999999 * jax.random.uniform(keys[1], (NROWS, COLUMNS), jnp.float32) ** steps_of(keys[1], (NROWS, COLUMNS), ((0, 32),), -0.2, 0.2), 0.1, 0.24),
        "obs_anom": noise(keys[2], (NBLK, OBS_BLK, MEMBERS), 1.0, 6.0, ((0, 32),)),
        "obs_weight": noise(keys[3], (NBLK, OBS_BLK, MEMBERS), 1.0, 6.0, ((0, 32),)),
        "taper_table": jnp.clip(jax.random.uniform(keys[4], (PATTERNS, TILE, OBS_BLK), jnp.float32, 0.1, 1.0), 0.1, 1.0),
        "obs_block": draw_obs_block(jax.random.fold_in(keys[7], 71), 0),
        "taper_id": place_ends(jax.random.randint(keys[6], (NTILES, SLOTS), 0, PATTERNS), jax.random.fold_in(keys[6], 1), 0, PATTERNS - 1).astype(jnp.int32),
    }


def advance(model_variable, padded, smoothing_speed):
    beside_all = padded[:, 2:] + padded[:, :-2] + jnp.roll(model_variable, 1, 2) + jnp.roll(model_variable, -1, 2)
    return model_variable + smoothing_speed * (beside_all - 4.0 * model_variable)


def propagate_prior(model_variable, smoothing_speed):
    padded = jnp.pad(model_variable, ((0, 0), (1, 1), (0, 0)))
    return advance(model_variable, padded, smoothing_speed)


def reference(ensemble, spreading_coefficient, obs_anom, obs_weight, taper_table, obs_block, taper_id):
    model_variable = ensemble
    for number in range(FSTEPS):
        model_variable = propagate_prior(model_variable, spreading_coefficient)
    flat = model_variable.reshape(MEMBERS, NROWS * COLUMNS)

    def analyse(tile_index):
        start = (tile_index * TILE).astype(jnp.int32)
        local = lax.dynamic_slice_in_dim(flat, start, TILE, 1)
        centred = (local - jnp.mean(local, axis=0, keepdims=True)).astype(jnp.bfloat16)
        increment = jnp.zeros((TILE, MEMBERS), jnp.float32)
        for slot in range(SLOTS):
            block = obs_block[tile_index, slot]
            anom = obs_anom[block]
            cov = jnp.dot(centred.T, anom.T, preferred_element_type=jnp.float32)
            taper = taper_table[taper_id[tile_index, slot]]
            tapered_update = (taper * (cov / (MEMBERS - 1.0))).astype(jnp.bfloat16)
            increment = increment + jnp.dot(tapered_update, obs_weight[block], preferred_element_type=jnp.float32)
        return local + increment.T

    tiles = lax.map(analyse, jnp.arange(NTILES, dtype=jnp.int32))
    posterior_estimate = jnp.transpose(tiles, (1, 0, 2)).reshape(MEMBERS, NROWS, COLUMNS)
    return propagate_prior(posterior_estimate, spreading_coefficient)
```

```python
import jax
import jax.numpy as jnp
from jax import lax
from jax.experimental import pallas as pl
from jax.experimental.pallas import tpu as pltpu
from jax.sharding import PartitionSpec as P

F32, BF16 = jnp.float32, jnp.bfloat16
TILE = 128
SLOTS = 4
FSTEPS = 4
HALO = FSTEPS + 1
VMEM = pl.BlockSpec(memory_space=pltpu.VMEM)
SMEM = pl.BlockSpec(memory_space=pltpu.SMEM)


def pack_obs_kernel(anom_ref, weight_ref, out_ref):
    obs, members = anom_ref.shape[1:]
    for q in range(members // TILE):
        cols = slice(q * TILE, (q + 1) * TILE)
        out_ref[0, q * TILE : (q + 1) * TILE, :] = anom_ref[0, :, cols]
        out_ref[0, members + q * TILE : members + (q + 1) * TILE, :] = weight_ref[0, :, cols].T


def pack_halo_kernel(first_ref, last_ref, coef_ref, block_ref, taper_ref, up_ref, down_ref):
    members, depth, columns = first_ref.shape
    rows = coef_ref.shape[0]
    tiles = block_ref.shape[1]
    lane = lax.broadcasted_iota(jnp.int32, (8, columns), 1)
    for out_ref, x_ref, start, row0, tile0, far in (
        (up_ref, first_ref, 0, 0, 0, HALO - 1),
        (down_ref, last_ref, depth - HALO, rows - HALO, tiles - 2, 0),
    ):
        for r in range(HALO):
            out_ref[r, 0:members, :] = x_ref[:, start + r, :]
            out_ref[r, members : members + 8, :] = jnp.broadcast_to(coef_ref[row0 + r : row0 + r + 1, :], (8, columns))
        ids = jnp.zeros((8, columns), jnp.int32)
        for t in range(2):
            for k in range(SLOTS):
                ids = jnp.where(lane == t * SLOTS + k, block_ref[k, tile0 + t], ids)
                ids = jnp.where(lane == 8 + t * SLOTS + k, taper_ref[k, tile0 + t], ids)
        out_ref[far, members : members + 8, :] = ids.astype(F32)


def forecast_kernel(x_ref, above_ref, below_ref, coef_ref, prior_ref, pay_ref, a_ref, b_ref, c_ref, m_ref):
    members, rows, columns = x_ref.shape
    total = rows + 2 * HALO
    group = pay_ref.shape[0]
    per = rows // group
    tiles = 2 * per + 1
    for r in range(HALO):
        a_ref[r] = above_ref[r, 0:members, :]
        a_ref[HALO + rows + r] = below_ref[r, 0:members, :]
        c_ref[r] = above_ref[r, members : members + 8, :]
        c_ref[HALO + rows + r] = below_ref[r, members : members + 8, :]
    for r in range(rows):
        a_ref[HALO + r] = x_ref[:, r, :]
        c_ref[HALO + r] = jnp.broadcast_to(coef_ref[r : r + 1, :], (8, columns))
    src, dst = a_ref, b_ref
    for step in range(1, FSTEPS + 1):

        def one(r, carry, src=src, dst=dst):
            up, mid = carry
            down = src[r + 1]
            beside = up + down + pltpu.roll(mid, 1, 1) + pltpu.roll(mid, columns - 1, 1)
            delta = (beside - 4.0 * mid).reshape(members // 8, 8, columns)
            dst[r] = mid + (c_ref[r][None] * delta).reshape(members, columns)
            return mid, down

        lax.fori_loop(step, total - step, one, (src[step - 1], src[step]))
        src, dst = dst, src

    m_ref[...] = jnp.zeros_like(m_ref)

    def tile(index, dest, slot, half, keep):
        value = src[index, :, half * TILE : (half + 1) * TILE]
        mean = jnp.sum(value, axis=0, keepdims=True) * (1.0 / members)
        pay_ref[dest, slot * members : (slot + 1) * members, :] = (value - mean).astype(BF16)
        high = mean.astype(BF16).astype(F32)
        middle = (mean - high).astype(BF16).astype(F32)
        m_ref[dest, 3 * slot : 3 * slot + 1, :] = high
        m_ref[dest, 3 * slot + 1 : 3 * slot + 2, :] = middle
        m_ref[dest, 3 * slot + 2 : 3 * slot + 3, :] = mean - high - middle

    for j in range(group):
        for i in range(per):
            for half in range(2):
                tile(HALO + j * per + i, j, 2 * i + half, half, True)
    for half in range(2):
        tile(HALO - 1, half, tiles - 1, half, True)
        tile(HALO + rows, 2 + half, tiles - 1, half, True)
    for j in range(4, group):
        pay_ref[j, (tiles - 1) * members : tiles * members, :] = jnp.zeros((members, TILE), BF16)
    for j in range(group):
        pay_ref[j, tiles * members :, :] = m_ref[j].astype(BF16)
    prior_ref[...] = src[HALO - 1 : HALO + rows + 1]


def analysis_kernel(blocks_ref, tapers_ref, recv_ref, taper_ref, *rest):
    obs_refs, (ret_ref, shift_ref) = rest[:SLOTS], rest[SLOTS:]
    group, size, _ = recv_ref.shape
    tiles = pl.num_programs(0)
    count = ret_ref.shape[1]
    t = pl.program_id(0)
    members = group * count

    @pl.when(t == 0)
    def _():
        parts = recv_ref[:, size - 32 :, :].astype(F32)
        for i in range((size - 32) // count):
            own = parts[:, 3 * i, :] + parts[:, 3 * i + 1, :] + parts[:, 3 * i + 2, :]
            shift_ref[i] = own - jnp.mean(own, axis=0, keepdims=True)

    here = pl.ds(pl.multiple_of(t * count, count), count)
    delta = shift_ref[t]
    centred = (recv_ref[:, here, :].astype(F32) + delta[:, None, :]).astype(BF16).reshape(members, TILE)
    total = jnp.zeros((members, TILE), F32)
    for pair in range(SLOTS // 2):
        lhs, rhs = [], []
        for k in (2 * pair, 2 * pair + 1):
            anom = jnp.concatenate([obs_refs[k][0, q * TILE : (q + 1) * TILE, :] for q in range(members // TILE)], axis=1)
            cov = jnp.dot(anom, centred, preferred_element_type=F32)
            taper = taper_ref[tapers_ref[t, k]]
            rhs.append((taper * (cov * (1.0 / (members - 1.0)))).astype(BF16))
            lhs.append(obs_refs[k][0, members:, :])
        total += jnp.dot(jnp.concatenate(lhs, axis=1), jnp.concatenate(rhs, axis=0), preferred_element_type=F32)
    ret_ref[:, :, :] = total.astype(BF16).reshape(group, count, TILE)


def final_kernel(prior_ref, inc_ref, coef_ref, out_ref, v_ref):
    members, rows, columns = out_ref.shape
    group, size, _ = inc_ref.shape
    per = rows // group
    last = size // members - 1

    def put(index, j, slot, half):
        lanes = slice(half * TILE, (half + 1) * TILE)
        inc = inc_ref[j, slot * members : (slot + 1) * members, :].astype(F32)
        v_ref[index, :, lanes] = prior_ref[index, :, lanes] + inc

    for half in range(2):
        put(0, half, last, half)
        put(rows + 1, 2 + half, last, half)
    for r in range(rows):
        for half in range(2):
            put(r + 1, r // per, 2 * (r % per) + half, half)
    for r in range(rows):
        mid = v_ref[r + 1]
        beside = v_ref[r] + v_ref[r + 2] + pltpu.roll(mid, 1, 1) + pltpu.roll(mid, columns - 1, 1)
        out_ref[:, r, :] = mid + coef_ref[r : r + 1, :] * (beside - 4.0 * mid)


def body(ensemble, spreading_coefficient, obs_anom, obs_weight, taper_table, obs_block, taper_id):
    members, rows, columns = ensemble.shape
    group = lax.axis_size("mem")
    states = lax.axis_size("state")
    per = rows // group
    tiles = 2 * per + 1
    size = tiles * members + 32
    limit = pltpu.CompilerParams(vmem_limit_bytes=48 << 20)

    packed = pl.pallas_call(
        pack_obs_kernel,
        out_shape=jax.ShapeDtypeStruct((1, 2 * obs_anom.shape[2], TILE), BF16),
        in_specs=[VMEM] * 2,
        out_specs=VMEM,
        name="pack_obs",
    )(obs_anom, obs_weight)
    every = lax.all_gather(packed, "state", axis=0, tiled=True)

    up, down = pl.pallas_call(
        pack_halo_kernel,
        grid=(1,),
        out_shape=[jax.ShapeDtypeStruct((HALO, members + 8, columns), F32)] * 2,
        in_specs=[
            pl.BlockSpec((members, 8, columns), lambda i: (0, 0, 0)),
            pl.BlockSpec((members, 8, columns), lambda i: (0, rows // 8 - 1, 0)),
            VMEM,
            SMEM,
            SMEM,
        ],
        out_specs=[VMEM] * 2,
        name="pack_halo",
    )(ensemble, ensemble, spreading_coefficient, obs_block.T, taper_id.T)
    below = lax.ppermute(up, "state", [(i + 1, i) for i in range(states - 1)])
    above = lax.ppermute(down, "state", [(i, i + 1) for i in range(states - 1)])

    prior, payload = pl.pallas_call(
        forecast_kernel,
        out_shape=[
            jax.ShapeDtypeStruct((rows + 2, members, columns), F32),
            jax.ShapeDtypeStruct((group, size, TILE), BF16),
        ],
        in_specs=[VMEM] * 4,
        out_specs=[VMEM] * 2,
        scratch_shapes=[
            pltpu.VMEM((rows + 2 * HALO, members, columns), F32),
            pltpu.VMEM((rows + 2 * HALO, members, columns), F32),
            pltpu.VMEM((rows + 2 * HALO, 8, columns), F32),
            pltpu.VMEM((group, 32, TILE), F32),
        ],
        compiler_params=limit,
        name="forecast4",
    )(ensemble, above, below, spreading_coefficient)
    gathered = lax.all_to_all(payload, "mem", split_axis=0, concat_axis=0, tiled=True)

    j = lax.axis_index("mem")
    edge = jnp.where(j < 2, above[0, members, :16], below[HALO - 1, members, :16])
    edge = jnp.where(j % 2 == 0, edge.reshape(-1, 4)[:3:2], edge.reshape(-1, 4)[1:4:2]).astype(jnp.int32)
    mine = 2 * per * j
    blocks = jnp.concatenate([lax.dynamic_slice_in_dim(obs_block, mine, 2 * per, 0), edge[0:1]], axis=0)
    tapers = jnp.concatenate([lax.dynamic_slice_in_dim(taper_id, mine, 2 * per, 0), edge[1:2]], axis=0)

    increments = pl.pallas_call(
        analysis_kernel,
        out_shape=jax.ShapeDtypeStruct((group, tiles * members, TILE), BF16),
        grid_spec=pltpu.PrefetchScalarGridSpec(
            num_scalar_prefetch=2,
            grid=(tiles,),
            in_specs=[
                VMEM,
                VMEM,
                *(
                    pl.BlockSpec((1, every.shape[1], TILE), lambda t, b, p, k=k: (b[t, k], 0, 0))
                    for k in range(SLOTS)
                ),
            ],
            out_specs=pl.BlockSpec((group, members, TILE), lambda t, b, p: (0, t, 0)),
            scratch_shapes=[pltpu.VMEM((tiles, group, TILE), F32)],
        ),
        compiler_params=limit,
        name="analysis",
    )(blocks, tapers, gathered, jnp.swapaxes(taper_table, 1, 2), *([every] * SLOTS))
    returned = lax.all_to_all(increments, "mem", split_axis=0, concat_axis=0, tiled=True)

    return pl.pallas_call(
        final_kernel,
        out_shape=jax.ShapeDtypeStruct((members, rows, columns), F32),
        in_specs=[VMEM] * 3,
        out_specs=VMEM,
        scratch_shapes=[pltpu.VMEM((rows + 2, members, columns), F32)],
        compiler_params=limit,
        name="final_step",
    )(prior, returned, spreading_coefficient)


def solution(mesh):
    placed = (
        P("mem", "state", None),
        P("state", None),
        P("state", None, None),
        P("state", None, None),
        P(),
        P("state", None),
        P("state", None),
    )
    return jax.shard_map(
        body, mesh=mesh, in_specs=placed, out_specs=P("mem", "state", None), check_vma=False
    )
```

```python
import jax
import jax.numpy as jnp
from jax import lax
from jax.experimental import pallas as pl
from jax.experimental.pallas import tpu as pltpu
from jax.sharding import PartitionSpec as P

F32, BF16 = jnp.float32, jnp.bfloat16
TILE = 128
SLOTS = 4
FSTEPS = 4
HALO = FSTEPS + 1
VMEM = pl.BlockSpec(memory_space=pltpu.VMEM)
SMEM = pl.BlockSpec(memory_space=pltpu.SMEM)


def pack_obs_kernel(anom_ref, weight_ref, out_ref):
    members = anom_ref.shape[2]
    core = lax.rem(lax.axis_index("mem"), 2)

    @pl.when(core == 0)
    def _():
        for q in range(members // TILE):
            out_ref[0, q * TILE : (q + 1) * TILE, :] = anom_ref[0, :, q * TILE : (q + 1) * TILE]

    @pl.when(core == 1)
    def _():
        for q in range(members // TILE):
            out_ref[0, q * TILE : (q + 1) * TILE, :] = weight_ref[0, :, q * TILE : (q + 1) * TILE].T


def pack_halo_kernel(first_ref, last_ref, coef_ref, block_ref, taper_ref, up_ref, down_ref):
    members, depth, columns = first_ref.shape
    rows = coef_ref.shape[0]
    tiles = block_ref.shape[1]
    lane = lax.broadcasted_iota(jnp.int32, (8, columns), 1)
    for out_ref, x_ref, start, row0, tile0, far in (
        (up_ref, first_ref, 0, 0, 0, HALO - 1),
        (down_ref, last_ref, depth - HALO, rows - HALO, tiles - 2, 0),
    ):
        for r in range(HALO):
            out_ref[r, 0:members, :] = x_ref[:, start + r, :]
            out_ref[r, members : members + 8, :] = jnp.broadcast_to(coef_ref[row0 + r : row0 + r + 1, :], (8, columns))
        ids = jnp.zeros((8, columns), jnp.int32)
        for t in range(2):
            for k in range(SLOTS):
                ids = jnp.where(lane == t * SLOTS + k, block_ref[k, tile0 + t], ids)
                ids = jnp.where(lane == 8 + t * SLOTS + k, taper_ref[k, tile0 + t], ids)
        out_ref[far, members : members + 8, :] = ids.astype(F32)


def forecast_kernel(x_ref, above_ref, below_ref, coef_ref, prior_ref, pay_ref, a_ref, b_ref, c_ref, m_ref):
    members, rows, columns = x_ref.shape
    total = rows + 2 * HALO
    group = pay_ref.shape[0]
    per = rows // group
    tiles = 2 * per + 1
    for r in range(HALO):
        c_ref[r] = above_ref[r, members : members + 8, :]
        c_ref[HALO + rows + r] = below_ref[r, members : members + 8, :]
    for r in range(rows):
        c_ref[HALO + r] = jnp.broadcast_to(coef_ref[r : r + 1, :], (8, columns))
    chunk = 16

    def advance(number, carry):
        here = pl.ds(pl.multiple_of(number * chunk, chunk), chunk)
        for r in range(HALO):
            a_ref[r, here, :] = above_ref[r, here, :]
            a_ref[HALO + rows + r, here, :] = below_ref[r, here, :]
        for r in range(rows):
            a_ref[HALO + r, here, :] = x_ref[here, r, :]
        src, dst = a_ref, b_ref
        for step in range(1, FSTEPS + 1):
            for r in range(step, total - step):
                mid = src[r, here, :]
                beside = src[r - 1, here, :] + src[r + 1, here, :] + pltpu.roll(mid, 1, 1) + pltpu.roll(mid, columns - 1, 1)
                delta = (beside - 4.0 * mid).reshape(chunk // 8, 8, columns)
                dst[r, here, :] = mid + (c_ref[r][None] * delta).reshape(chunk, columns)
            src, dst = dst, src
        return carry

    lax.fori_loop(0, members // chunk, advance, 0)
    src = a_ref if FSTEPS % 2 == 0 else b_ref
    m_ref[...] = jnp.zeros_like(m_ref)

    def tile(index, dest, slot, half, keep):
        value = src[index, :, half * TILE : (half + 1) * TILE]
        mean = jnp.sum(value, axis=0, keepdims=True) * (1.0 / members)
        pay_ref[dest, slot * members : (slot + 1) * members, :] = (value - mean).astype(BF16)
        high = mean.astype(BF16).astype(F32)
        middle = (mean - high).astype(BF16).astype(F32)
        m_ref[dest, 3 * slot : 3 * slot + 1, :] = high
        m_ref[dest, 3 * slot + 1 : 3 * slot + 2, :] = middle
        m_ref[dest, 3 * slot + 2 : 3 * slot + 3, :] = mean - high - middle

    for j in range(group):
        for i in range(per):
            for half in range(2):
                tile(HALO + j * per + i, j, 2 * i + half, half, True)
    for half in range(2):
        tile(HALO - 1, half, tiles - 1, half, True)
        tile(HALO + rows, 2 + half, tiles - 1, half, True)
    for j in range(4, group):
        pay_ref[j, (tiles - 1) * members : tiles * members, :] = jnp.zeros((members, TILE), BF16)
    for j in range(group):
        pay_ref[j, tiles * members :, :] = m_ref[j].astype(BF16)
    prior_ref[...] = src[HALO - 1 : HALO + rows + 1]


def analysis_kernel(anom_at_ref, weight_at_ref, tapers_ref, recv_ref, taper_ref, *rest):
    pieces, (ret_ref, obs_ref, shift_ref, sems) = rest[:-4], rest[-4:]
    group, size, _ = recv_ref.shape
    count = ret_ref.shape[1] // anom_at_ref.shape[0]
    tiles = anom_at_ref.shape[0]
    members = group * count
    core = lax.rem(lax.axis_index("mem"), 2)
    copies = []
    for side in range(2):
        start = 0
        for piece in pieces[side * len(pieces) // 2 : (side + 1) * len(pieces) // 2]:
            length = piece.shape[0]
            to = obs_ref.at[core if side == 0 else 1 - core, pl.ds(start, length)]
            copies.append(pltpu.make_async_copy(piece, to, sems.at[len(copies)]))
            start += length
    for copy in copies:
        copy.start()

    parts = recv_ref[:, size - 32 :, :].astype(F32)
    for t in range(tiles):
        own = parts[:, 3 * t, :] + parts[:, 3 * t + 1, :] + parts[:, 3 * t + 2, :]
        shift_ref[t] = own - jnp.mean(own, axis=0, keepdims=True)
    for copy in copies:
        copy.wait()

    def one(t, carry):
        here = pl.ds(pl.multiple_of(t * count, count), count)
        delta = shift_ref[t]
        centred = (recv_ref[:, here, :].astype(F32) + delta[:, None, :]).astype(BF16).reshape(members, TILE)
        total = jnp.zeros((members, TILE), F32)
        for pair in range(SLOTS // 2):
            lhs, rhs = [], []
            for k in (2 * pair, 2 * pair + 1):
                at = anom_at_ref[t, k]
                anom = jnp.concatenate([obs_ref[0, at, q * TILE : (q + 1) * TILE, :] for q in range(members // TILE)], axis=1)
                cov = jnp.dot(anom, centred, preferred_element_type=F32)
                taper = taper_ref[tapers_ref[t, k]]
                rhs.append((taper * (cov * (1.0 / (members - 1.0)))).astype(BF16))
                lhs.append(obs_ref[1, weight_at_ref[t, k]])
            total += jnp.dot(jnp.concatenate(lhs, axis=1), jnp.concatenate(rhs, axis=0), preferred_element_type=F32)
        ret_ref[:, here, :] = total.astype(BF16).reshape(group, count, TILE)
        return carry

    lax.fori_loop(0, tiles, one, 0, unroll=3)


def final_kernel(prior_ref, inc_ref, coef_ref, out_ref, v_ref):
    members, rows, columns = out_ref.shape
    group, size, _ = inc_ref.shape
    per = rows // group
    last = size // members - 1

    def put(index, j, slot, half):
        lanes = slice(half * TILE, (half + 1) * TILE)
        inc = inc_ref[j, slot * members : (slot + 1) * members, :].astype(F32)
        v_ref[index, :, lanes] = prior_ref[index, :, lanes] + inc

    for half in range(2):
        put(0, half, last, half)
        put(rows + 1, 2 + half, last, half)
    for r in range(rows):
        for half in range(2):
            put(r + 1, r // per, 2 * (r % per) + half, half)
    for r in range(rows):
        mid = v_ref[r + 1]
        beside = v_ref[r] + v_ref[r + 2] + pltpu.roll(mid, 1, 1) + pltpu.roll(mid, columns - 1, 1)
        out_ref[:, r, :] = mid + coef_ref[r : r + 1, :] * (beside - 4.0 * mid)


AXES = ("mem", "state")


def fetch(value, mesh, source):
    xs, ys, zs = mesh
    pairs = []
    for x in range(xs):
        for c in range(2):
            for y in range(ys):
                for z in range(zs):
                    a, b, d, e = source(x, c, y, z)
                    pairs.append((((a * 2 + b) * ys + d % ys) * zs + e % zs, ((x * 2 + c) * ys + y) * zs + z))
    return lax.ppermute(value, AXES, pairs)


def ring(first, step):
    return lambda x, c, y, z: (x, c, y + step, z) if (c == 0) == first else (x, c, y, z + step)


def other_core(x, c, y, z):
    return (x, 1 - c, y, z)


def move(outs, plan, operands, name, after=()):
    def kernel(*refs):
        sources, targets, sems = refs[: len(operands)], refs[len(operands) + len(after) : -1], refs[-1]
        core = lax.rem(lax.axis_index("mem"), 2)
        copies = []
        for i, (a, first, b, to, length) in enumerate(plan):
            first = first(core) if callable(first) else first
            copies.append(pltpu.make_async_copy(sources[a].at[pl.ds(first, length)], targets[b].at[pl.ds(to, length)], sems.at[i]))
        for copy in copies:
            copy.start()
        for copy in copies:
            copy.wait()

    anywhere = pl.BlockSpec(memory_space=pl.ANY)
    return pl.pallas_call(
        kernel,
        out_shape=[jax.ShapeDtypeStruct((n, *operands[0].shape[1:]), operands[0].dtype) for n in outs],
        in_specs=[anywhere] * (len(operands) + len(after)),
        out_specs=[anywhere] * len(outs),
        scratch_shapes=[pltpu.SemaphoreType.DMA((len(plan),))],
        name=name,
    )(*operands, *after)


def gather_obs(own, mesh, after_first, after_second, after_third):
    far = fetch(own, mesh, lambda x, c, y, z: (x, c, y, z + 4))
    (held,) = move([2], [(0, 0, 0, 0, 1), (1, 0, 0, 1, 1)], [own, far], "merge_two", after_first)
    p, m, q = (fetch(held, mesh, ring(True, step)) for step in (1, -1, 2))
    plan = [(a, i, 0, 4 * i + a, 1) for i in range(2) for a in range(4)]
    (held,) = move([8], plan, [held, p, m, q], "merge_eight", after_second())
    p, m = (fetch(held, mesh, ring(False, step)) for step in (1, -1))
    swapped = [fetch(held, mesh, other_core)]
    plan = [(0, 0, 0, 0, 4), (1, lambda core: 4 * core, 1, 0, 4)]
    q, r = move([4, 4], plan, [p, m], "halves", after_third())
    q = fetch(q, mesh, ring(False, 1))
    r = fetch(r, mesh, ring(False, -1))
    swapped += [fetch(v, mesh, other_core) for v in (p, m, q, r)]
    return [held, p, m, q, r], swapped


def places(block, y, z):
    dy, dz = (block // 8 - y) % 4, (block % 8 - z) % 8
    low = dz % 4
    gray_y, gray_z = dy ^ (dy >> 1), low ^ (low >> 1)
    high = 4 * ((dz // 4) ^ (low == 3).astype(jnp.int32))
    return 8 * gray_z + high + gray_y, 8 * gray_y + high + gray_z


def body(ensemble, spreading_coefficient, obs_anom, obs_weight, taper_table, obs_block, taper_id):
    members, rows, columns = ensemble.shape
    group = lax.axis_size("mem")
    states = lax.axis_size("state")
    per = rows // group
    tiles = 2 * per + 1
    size = tiles * members + 32
    limit = pltpu.CompilerParams(vmem_limit_bytes=48 << 20)

    j, at = lax.axis_index("mem"), lax.axis_index("state")
    packed = pl.pallas_call(
        pack_obs_kernel,
        out_shape=jax.ShapeDtypeStruct((1, obs_anom.shape[2], TILE), BF16),
        in_specs=[VMEM] * 2,
        out_specs=VMEM,
        name="pack_obs",
    )(obs_anom, obs_weight)
    up, down = pl.pallas_call(
        pack_halo_kernel,
        grid=(1,),
        out_shape=[jax.ShapeDtypeStruct((HALO, members + 8, columns), F32)] * 2,
        in_specs=[
            pl.BlockSpec((members, 8, columns), lambda i: (0, 0, 0)),
            pl.BlockSpec((members, 8, columns), lambda i: (0, rows // 8 - 1, 0)),
            VMEM,
            SMEM,
            SMEM,
        ],
        out_specs=[VMEM] * 2,
        name="pack_halo",
    )(ensemble, ensemble, spreading_coefficient, obs_block.T, taper_id.T)
    below = lax.ppermute(up, "state", [(i + 1, i) for i in range(states - 1)])
    above = lax.ppermute(down, "state", [(i, i + 1) for i in range(states - 1)])

    prior, payload = pl.pallas_call(
        forecast_kernel,
        out_shape=[
            jax.ShapeDtypeStruct((rows + 2, members, columns), F32),
            jax.ShapeDtypeStruct((group, size, TILE), BF16),
        ],
        in_specs=[VMEM] * 4,
        out_specs=[VMEM] * 2,
        scratch_shapes=[
            pltpu.VMEM((rows + 2 * HALO, members, columns), F32),
            pltpu.VMEM((rows + 2 * HALO, members, columns), F32),
            pltpu.VMEM((rows + 2 * HALO, 8, columns), F32),
            pltpu.VMEM((group, 32, TILE), F32),
        ],
        compiler_params=limit,
        name="forecast4",
    )(ensemble, above, below, spreading_coefficient)
    own, swapped = gather_obs(
        packed, (group // 2, states // 8, 8), [up, down], lambda: [above, below], lambda: [payload]
    )
    gathered = lax.all_to_all(payload, "mem", split_axis=0, concat_axis=0, tiled=True)

    edge = jnp.where(j < 2, above[0, members, :16], below[HALO - 1, members, :16])
    edge = jnp.where(j % 2 == 0, edge.reshape(-1, 4)[:3:2], edge.reshape(-1, 4)[1:4:2]).astype(jnp.int32)
    mine = 2 * per * j
    blocks = jnp.concatenate([lax.dynamic_slice_in_dim(obs_block, mine, 2 * per, 0), edge[0:1]], axis=0)
    tapers = jnp.concatenate([lax.dynamic_slice_in_dim(taper_id, mine, 2 * per, 0), edge[1:2]], axis=0)

    anom_at, weight_at = places(blocks, at // 8, at % 8)
    increments = pl.pallas_call(
        analysis_kernel,
        out_shape=jax.ShapeDtypeStruct((group, tiles * members, TILE), BF16),
        in_specs=[SMEM] * 3 + [VMEM] * 2 + [pl.BlockSpec(memory_space=pl.ANY)] * (len(own) + len(swapped)),
        out_specs=VMEM,
        scratch_shapes=[
            pltpu.VMEM((2, states, *packed.shape[1:]), BF16),
            pltpu.VMEM((tiles, group, TILE), F32),
            pltpu.SemaphoreType.DMA((len(own) + len(swapped),)),
        ],
        compiler_params=limit,
        name="analysis",
    )(anom_at, weight_at, tapers, gathered, jnp.swapaxes(taper_table, 1, 2), *own, *swapped)
    returned = lax.all_to_all(increments, "mem", split_axis=0, concat_axis=0, tiled=True)

    return pl.pallas_call(
        final_kernel,
        out_shape=jax.ShapeDtypeStruct((members, rows, columns), F32),
        in_specs=[VMEM] * 3,
        out_specs=VMEM,
        scratch_shapes=[pltpu.VMEM((rows + 2, members, columns), F32)],
        compiler_params=limit,
        name="final_step",
    )(prior, returned, spreading_coefficient)


def solution(mesh):
    placed = (
        P("mem", "state", None),
        P("state", None),
        P("state", None, None),
        P("state", None, None),
        P(),
        P("state", None),
        P("state", None),
    )
    return jax.shard_map(
        body, mesh=mesh, in_specs=placed, out_specs=P("mem", "state", None), check_vma=False
    )
```

```python
import jax
import jax.numpy as jnp
from jax import lax
from jax.experimental import pallas as pl
from jax.experimental.pallas import tpu as pltpu
from jax.sharding import PartitionSpec as P

F32, BF16 = jnp.float32, jnp.bfloat16
TILE = 128
SLOTS = 4
FSTEPS = 4
HALO = FSTEPS + 1
VMEM = pl.BlockSpec(memory_space=pltpu.VMEM)
SMEM = pl.BlockSpec(memory_space=pltpu.SMEM)


def pack_obs_kernel(anom_ref, weight_ref, out_ref):
    members = anom_ref.shape[2]
    core = lax.rem(lax.axis_index("mem"), 2)

    @pl.when(core == 0)
    def _():
        for q in range(members // TILE):
            out_ref[0, q * TILE : (q + 1) * TILE, :] = anom_ref[0, :, q * TILE : (q + 1) * TILE]

    @pl.when(core == 1)
    def _():
        for q in range(members // TILE):
            out_ref[0, q * TILE : (q + 1) * TILE, :] = weight_ref[0, :, q * TILE : (q + 1) * TILE].T


def pack_halo_kernel(first_ref, last_ref, coef_ref, block_ref, taper_ref, up_ref, down_ref):
    members, depth, columns = first_ref.shape
    rows = coef_ref.shape[0]
    tiles = block_ref.shape[1]
    lane = lax.broadcasted_iota(jnp.int32, (8, columns), 1)
    for out_ref, x_ref, start, row0, tile0, far in (
        (up_ref, first_ref, 0, 0, 0, HALO - 1),
        (down_ref, last_ref, depth - HALO, rows - HALO, tiles - 2, 0),
    ):
        for r in range(HALO):
            out_ref[r, 0:members, :] = x_ref[:, start + r, :]
            out_ref[r, members : members + 8, :] = jnp.broadcast_to(coef_ref[row0 + r : row0 + r + 1, :], (8, columns))
        ids = jnp.zeros((8, columns), jnp.int32)
        for t in range(2):
            for k in range(SLOTS):
                ids = jnp.where(lane == t * SLOTS + k, block_ref[k, tile0 + t], ids)
                ids = jnp.where(lane == 8 + t * SLOTS + k, taper_ref[k, tile0 + t], ids)
        out_ref[far, members : members + 8, :] = ids.astype(F32)


def forecast_kernel(x_ref, above_ref, below_ref, coef_ref, prior_ref, pay_ref, a_ref, b_ref, c_ref, m_ref):
    members, rows, columns = x_ref.shape
    total = rows + 2 * HALO
    group = pay_ref.shape[0]
    per = rows // group
    tiles = 2 * per + 1
    for r in range(HALO):
        c_ref[r] = above_ref[r, members : members + 8, :]
        c_ref[HALO + rows + r] = below_ref[r, members : members + 8, :]
    for r in range(rows):
        c_ref[HALO + r] = jnp.broadcast_to(coef_ref[r : r + 1, :], (8, columns))
    chunk = 16

    def advance(number, carry):
        here = pl.ds(pl.multiple_of(number * chunk, chunk), chunk)
        for r in range(HALO):
            a_ref[r, here, :] = above_ref[r, here, :]
            a_ref[HALO + rows + r, here, :] = below_ref[r, here, :]
        for r in range(rows):
            a_ref[HALO + r, here, :] = x_ref[here, r, :]
        src, dst = a_ref, b_ref
        for step in range(1, FSTEPS + 1):
            for r in range(step, total - step):
                mid = src[r, here, :]
                beside = src[r - 1, here, :] + src[r + 1, here, :] + pltpu.roll(mid, 1, 1) + pltpu.roll(mid, columns - 1, 1)
                delta = (beside - 4.0 * mid).reshape(chunk // 8, 8, columns)
                dst[r, here, :] = mid + (c_ref[r][None] * delta).reshape(chunk, columns)
            src, dst = dst, src
        return carry

    lax.fori_loop(0, members // chunk, advance, 0)
    src = a_ref if FSTEPS % 2 == 0 else b_ref
    m_ref[...] = jnp.zeros_like(m_ref)

    def tile(index, dest, slot, half, keep):
        value = src[index, :, half * TILE : (half + 1) * TILE]
        mean = jnp.sum(value, axis=0, keepdims=True) * (1.0 / members)
        pay_ref[dest, slot * members : (slot + 1) * members, :] = (value - mean).astype(BF16)
        high = mean.astype(BF16).astype(F32)
        middle = (mean - high).astype(BF16).astype(F32)
        m_ref[dest, 3 * slot : 3 * slot + 1, :] = high
        m_ref[dest, 3 * slot + 1 : 3 * slot + 2, :] = middle
        m_ref[dest, 3 * slot + 2 : 3 * slot + 3, :] = mean - high - middle

    for j in range(group):
        for i in range(per):
            for half in range(2):
                tile(HALO + j * per + i, j, 2 * i + half, half, True)
    for half in range(2):
        tile(HALO - 1, half, tiles - 1, half, True)
        tile(HALO + rows, 2 + half, tiles - 1, half, True)
    for j in range(4, group):
        pay_ref[j, (tiles - 1) * members : tiles * members, :] = jnp.zeros((members, TILE), BF16)
    for j in range(group):
        pay_ref[j, tiles * members :, :] = m_ref[j].astype(BF16)
    prior_ref[...] = src[HALO - 1 : HALO + rows + 1]


def analysis_kernel(anom_at_ref, weight_at_ref, tapers_ref, recv_ref, taper_ref, *rest):
    pieces, (ret_ref, obs_ref, shift_ref, sems) = rest[:-4], rest[-4:]
    group, size, _ = recv_ref.shape
    count = ret_ref.shape[1] // anom_at_ref.shape[0]
    tiles = anom_at_ref.shape[0]
    members = group * count
    core = lax.rem(lax.axis_index("mem"), 2)
    copies = []
    for side in range(2):
        start = 0
        for piece in pieces[side * len(pieces) // 2 : (side + 1) * len(pieces) // 2]:
            length = piece.shape[0]
            to = obs_ref.at[core if side == 0 else 1 - core, pl.ds(start, length)]
            copies.append(pltpu.make_async_copy(piece, to, sems.at[len(copies)]))
            start += length
    for copy in copies:
        copy.start()

    parts = recv_ref[:, size - 32 :, :].astype(F32)
    for t in range(tiles):
        own = parts[:, 3 * t, :] + parts[:, 3 * t + 1, :] + parts[:, 3 * t + 2, :]
        shift_ref[t] = own - jnp.mean(own, axis=0, keepdims=True)
    for copy in copies:
        copy.wait()

    def one(t, carry):
        here = pl.ds(pl.multiple_of(t * count, count), count)
        delta = shift_ref[t]
        centred = (recv_ref[:, here, :].astype(F32) + delta[:, None, :]).astype(BF16).reshape(members, TILE)
        total = jnp.zeros((members, TILE), F32)
        for pair in range(SLOTS // 2):
            lhs, rhs = [], []
            for k in (2 * pair, 2 * pair + 1):
                at = anom_at_ref[t, k]
                anom = jnp.concatenate([obs_ref[0, at, q * TILE : (q + 1) * TILE, :] for q in range(members // TILE)], axis=1)
                cov = jnp.dot(anom, centred, preferred_element_type=F32)
                taper = taper_ref[tapers_ref[t, k]]
                rhs.append((taper * (cov * (1.0 / (members - 1.0)))).astype(BF16))
                lhs.append(obs_ref[1, weight_at_ref[t, k]])
            total += jnp.dot(jnp.concatenate(lhs, axis=1), jnp.concatenate(rhs, axis=0), preferred_element_type=F32)
        ret_ref[:, here, :] = total.astype(BF16).reshape(group, count, TILE)
        return carry

    lax.fori_loop(0, tiles, one, 0, unroll=3)


def final_kernel(prior_ref, inc_ref, coef_ref, out_ref, v_ref):
    members, rows, columns = out_ref.shape
    group, size, _ = inc_ref.shape
    per = rows // group
    last = size // members - 1

    def put(index, j, slot, half):
        lanes = slice(half * TILE, (half + 1) * TILE)
        inc = inc_ref[j, slot * members : (slot + 1) * members, :].astype(F32)
        v_ref[index, :, lanes] = prior_ref[index, :, lanes] + inc

    for half in range(2):
        put(0, half, last, half)
        put(rows + 1, 2 + half, last, half)
    for r in range(rows):
        for half in range(2):
            put(r + 1, r // per, 2 * (r % per) + half, half)
    for r in range(rows):
        mid = v_ref[r + 1]
        beside = v_ref[r] + v_ref[r + 2] + pltpu.roll(mid, 1, 1) + pltpu.roll(mid, columns - 1, 1)
        out_ref[:, r, :] = mid + coef_ref[r : r + 1, :] * (beside - 4.0 * mid)


AXES = ("mem", "state")


def fetch(value, mesh, source):
    xs, ys, zs = mesh
    pairs = []
    for x in range(xs):
        for c in range(2):
            for y in range(ys):
                for z in range(zs):
                    a, b, d, e = source(x, c, y, z)
                    pairs.append((((a * 2 + b) * ys + d % ys) * zs + e % zs, ((x * 2 + c) * ys + y) * zs + z))
    return lax.ppermute(value, AXES, pairs)


def ring(first, step):
    return lambda x, c, y, z: (x, c, y + step, z) if (c == 0) == first else (x, c, y, z + step)


def other_core(x, c, y, z):
    return (x, 1 - c, y, z)


def whole(value):
    return pl.BlockSpec(value.shape, lambda i, c: (0,) * len(value.shape))


def join(operands, core, name, after=()):
    count, blocks = len(operands), operands[0].shape[0]

    def kernel(core_ref, *refs):
        out_ref = refs[-1]
        for i in range(blocks):
            for a in range(count):
                out_ref[i * count + a] = refs[a][i]

    return pl.pallas_call(
        kernel,
        out_shape=jax.ShapeDtypeStruct((count * blocks, *operands[0].shape[1:]), BF16),
        grid_spec=pltpu.PrefetchScalarGridSpec(
            num_scalar_prefetch=1,
            grid=(1,),
            in_specs=[whole(v) for v in operands] + [pl.BlockSpec((1, 16, TILE), lambda i, c: (0, 0, 0))] * len(after),
            out_specs=pl.BlockSpec((count * blocks, *operands[0].shape[1:]), lambda i, c: (0, 0, 0)),
        ),
        name=name,
    )(core, *operands, *after)


def halves(p, m, core, after):
    def kernel(core_ref, p_ref, m_ref, after_ref, q_ref, r_ref):
        q_ref[...] = p_ref[...]
        r_ref[...] = m_ref[...]

    shape = (p.shape[0] // 2, *p.shape[1:])
    first = pl.BlockSpec(shape, lambda i, c: (0, 0, 0))
    return pl.pallas_call(
        kernel,
        out_shape=[jax.ShapeDtypeStruct(shape, BF16)] * 2,
        grid_spec=pltpu.PrefetchScalarGridSpec(
            num_scalar_prefetch=1,
            grid=(1,),
            in_specs=[first, pl.BlockSpec(shape, lambda i, c: (c[0], 0, 0)), pl.BlockSpec((1, 16, TILE), lambda i, c: (0, 0, 0))],
            out_specs=[first] * 2,
        ),
        name="halves",
    )(core, p, m, after)


def gather_obs(own, mesh, core, edges, arrived, payload):
    far = fetch(own, mesh, lambda x, c, y, z: (x, c, y, z + 4))
    held = join([own, far], core, "join_two", edges)
    p, m, q = (fetch(held, mesh, ring(True, step)) for step in (1, -1, 2))
    held = join([held, p, m, q], core, "join_eight", arrived)
    p, m = (fetch(held, mesh, ring(False, step)) for step in (1, -1))
    swapped = [fetch(held, mesh, other_core)]
    q, r = halves(p, m, core, payload)
    q = fetch(q, mesh, ring(False, 1))
    r = fetch(r, mesh, ring(False, -1))
    swapped += [fetch(v, mesh, other_core) for v in (p, m, q, r)]
    return [held, p, m, q, r], swapped


def places(block, y, z):
    dy, dz = (block // 8 - y) % 4, (block % 8 - z) % 8
    low = dz % 4
    gray_y, gray_z = dy ^ (dy >> 1), low ^ (low >> 1)
    high = 4 * ((dz // 4) ^ (low == 3).astype(jnp.int32))
    return 8 * gray_z + high + gray_y, 8 * gray_y + high + gray_z


def body(ensemble, spreading_coefficient, obs_anom, obs_weight, taper_table, obs_block, taper_id):
    members, rows, columns = ensemble.shape
    group = lax.axis_size("mem")
    states = lax.axis_size("state")
    per = rows // group
    tiles = 2 * per + 1
    size = tiles * members + 32
    limit = pltpu.CompilerParams(vmem_limit_bytes=48 << 20)

    j, at = lax.axis_index("mem"), lax.axis_index("state")
    packed = pl.pallas_call(
        pack_obs_kernel,
        out_shape=jax.ShapeDtypeStruct((1, obs_anom.shape[2], TILE), BF16),
        in_specs=[VMEM] * 2,
        out_specs=VMEM,
        name="pack_obs",
    )(obs_anom, obs_weight)
    up, down = pl.pallas_call(
        pack_halo_kernel,
        grid=(1,),
        out_shape=[jax.ShapeDtypeStruct((HALO, members + 8, columns), F32)] * 2,
        in_specs=[
            pl.BlockSpec((members, 8, columns), lambda i: (0, 0, 0)),
            pl.BlockSpec((members, 8, columns), lambda i: (0, rows // 8 - 1, 0)),
            VMEM,
            SMEM,
            SMEM,
        ],
        out_specs=[VMEM] * 2,
        name="pack_halo",
    )(ensemble, ensemble, spreading_coefficient, obs_block.T, taper_id.T)
    below = lax.ppermute(up, "state", [(i + 1, i) for i in range(states - 1)])
    above = lax.ppermute(down, "state", [(i, i + 1) for i in range(states - 1)])

    prior, payload = pl.pallas_call(
        forecast_kernel,
        out_shape=[
            jax.ShapeDtypeStruct((rows + 2, members, columns), F32),
            jax.ShapeDtypeStruct((group, size, TILE), BF16),
        ],
        in_specs=[VMEM] * 4,
        out_specs=[VMEM] * 2,
        scratch_shapes=[
            pltpu.VMEM((rows + 2 * HALO, members, columns), F32),
            pltpu.VMEM((rows + 2 * HALO, members, columns), F32),
            pltpu.VMEM((rows + 2 * HALO, 8, columns), F32),
            pltpu.VMEM((group, 32, TILE), F32),
        ],
        compiler_params=limit,
        name="forecast4",
    )(ensemble, above, below, spreading_coefficient)
    core = (j % 2).reshape(1)
    own, swapped = gather_obs(packed, (group // 2, states // 8, 8), core, [up, down], [above, below], payload)
    gathered = lax.all_to_all(payload, "mem", split_axis=0, concat_axis=0, tiled=True)

    edge = jnp.where(j < 2, above[0, members, :16], below[HALO - 1, members, :16])
    edge = jnp.where(j % 2 == 0, edge.reshape(-1, 4)[:3:2], edge.reshape(-1, 4)[1:4:2]).astype(jnp.int32)
    mine = 2 * per * j
    blocks = jnp.concatenate([lax.dynamic_slice_in_dim(obs_block, mine, 2 * per, 0), edge[0:1]], axis=0)
    tapers = jnp.concatenate([lax.dynamic_slice_in_dim(taper_id, mine, 2 * per, 0), edge[1:2]], axis=0)

    anom_at, weight_at = places(blocks, at // 8, at % 8)
    increments = pl.pallas_call(
        analysis_kernel,
        out_shape=jax.ShapeDtypeStruct((group, tiles * members, TILE), BF16),
        in_specs=[SMEM] * 3 + [VMEM] * 2 + [pl.BlockSpec(memory_space=pl.ANY)] * (len(own) + len(swapped)),
        out_specs=VMEM,
        scratch_shapes=[
            pltpu.VMEM((2, states, *packed.shape[1:]), BF16),
            pltpu.VMEM((tiles, group, TILE), F32),
            pltpu.SemaphoreType.DMA((len(own) + len(swapped),)),
        ],
        compiler_params=limit,
        name="analysis",
    )(anom_at, weight_at, tapers, gathered, jnp.swapaxes(taper_table, 1, 2), *own, *swapped)
    returned = lax.all_to_all(increments, "mem", split_axis=0, concat_axis=0, tiled=True)

    return pl.pallas_call(
        final_kernel,
        out_shape=jax.ShapeDtypeStruct((members, rows, columns), F32),
        in_specs=[VMEM] * 3,
        out_specs=VMEM,
        scratch_shapes=[pltpu.VMEM((rows + 2, members, columns), F32)],
        compiler_params=limit,
        name="final_step",
    )(prior, returned, spreading_coefficient)


def solution(mesh):
    placed = (
        P("mem", "state", None),
        P("state", None),
        P("state", None, None),
        P("state", None, None),
        P(),
        P("state", None),
        P("state", None),
    )
    return jax.shard_map(
        body, mesh=mesh, in_specs=placed, out_specs=P("mem", "state", None), check_vma=False
    )
```

```python
import jax
import jax.numpy as jnp
from jax import lax
from jax.experimental import pallas as pl
from jax.experimental.pallas import tpu as pltpu
from jax.sharding import PartitionSpec as P

F32, BF16 = jnp.float32, jnp.bfloat16
TILE = 128
SLOTS = 4
FSTEPS = 4
HALO = FSTEPS + 1
VMEM = pl.BlockSpec(memory_space=pltpu.VMEM)
SMEM = pl.BlockSpec(memory_space=pltpu.SMEM)


def pack_obs_kernel(anom_ref, weight_ref, out_ref):
    members = anom_ref.shape[2]
    core = lax.rem(lax.axis_index("mem"), 2)

    @pl.when(core == 0)
    def _():
        for q in range(members // TILE):
            out_ref[0, q * TILE : (q + 1) * TILE, :] = anom_ref[0, :, q * TILE : (q + 1) * TILE]

    @pl.when(core == 1)
    def _():
        for q in range(members // TILE):
            out_ref[0, q * TILE : (q + 1) * TILE, :] = weight_ref[0, :, q * TILE : (q + 1) * TILE].T


def pack_halo_kernel(first_ref, last_ref, coef_ref, block_ref, taper_ref, up_ref, down_ref):
    members, depth, columns = first_ref.shape
    rows = coef_ref.shape[0]
    tiles = block_ref.shape[1]
    lane = lax.broadcasted_iota(jnp.int32, (8, columns), 1)
    for out_ref, x_ref, start, row0, tile0, far in (
        (up_ref, first_ref, 0, 0, 0, HALO - 1),
        (down_ref, last_ref, depth - HALO, rows - HALO, tiles - 2, 0),
    ):
        for r in range(HALO):
            out_ref[r, 0:members, :] = x_ref[:, start + r, :]
            out_ref[r, members : members + 8, :] = jnp.broadcast_to(coef_ref[row0 + r : row0 + r + 1, :], (8, columns))
        ids = jnp.zeros((8, columns), jnp.int32)
        for t in range(2):
            for k in range(SLOTS):
                ids = jnp.where(lane == t * SLOTS + k, block_ref[k, tile0 + t], ids)
                ids = jnp.where(lane == 8 + t * SLOTS + k, taper_ref[k, tile0 + t], ids)
        out_ref[far, members : members + 8, :] = ids.astype(F32)


def forecast_kernel(x_ref, above_ref, below_ref, coef_ref, prior_ref, pay_ref, a_ref, b_ref, c_ref, m_ref):
    members, rows, columns = x_ref.shape
    total = rows + 2 * HALO
    group = pay_ref.shape[0]
    per = rows // group
    tiles = 2 * per + 1
    for r in range(HALO):
        c_ref[r] = above_ref[r, members : members + 8, :]
        c_ref[HALO + rows + r] = below_ref[r, members : members + 8, :]
    for r in range(rows):
        c_ref[HALO + r] = jnp.broadcast_to(coef_ref[r : r + 1, :], (8, columns))
    chunk = 16

    def advance(number, carry):
        here = pl.ds(pl.multiple_of(number * chunk, chunk), chunk)
        for r in range(HALO):
            a_ref[r, here, :] = above_ref[r, here, :]
            a_ref[HALO + rows + r, here, :] = below_ref[r, here, :]
        for r in range(rows):
            a_ref[HALO + r, here, :] = x_ref[here, r, :]
        src, dst = a_ref, b_ref
        for step in range(1, FSTEPS + 1):
            for r in range(step, total - step):
                mid = src[r, here, :]
                beside = src[r - 1, here, :] + src[r + 1, here, :] + pltpu.roll(mid, 1, 1) + pltpu.roll(mid, columns - 1, 1)
                delta = (beside - 4.0 * mid).reshape(chunk // 8, 8, columns)
                dst[r, here, :] = mid + (c_ref[r][None] * delta).reshape(chunk, columns)
            src, dst = dst, src
        return carry

    lax.fori_loop(0, members // chunk, advance, 0)
    src = a_ref if FSTEPS % 2 == 0 else b_ref
    m_ref[...] = jnp.zeros_like(m_ref)

    def tile(index, dest, slot, half, keep):
        value = src[index, :, half * TILE : (half + 1) * TILE]
        mean = jnp.sum(value, axis=0, keepdims=True) * (1.0 / members)
        pay_ref[dest, slot * members : (slot + 1) * members, :] = (value - mean).astype(BF16)
        high = mean.astype(BF16).astype(F32)
        middle = (mean - high).astype(BF16).astype(F32)
        m_ref[dest, 3 * slot : 3 * slot + 1, :] = high
        m_ref[dest, 3 * slot + 1 : 3 * slot + 2, :] = middle
        m_ref[dest, 3 * slot + 2 : 3 * slot + 3, :] = mean - high - middle

    for j in range(group):
        for i in range(per):
            for half in range(2):
                tile(HALO + j * per + i, j, 2 * i + half, half, True)
    for half in range(2):
        tile(HALO - 1, half, tiles - 1, half, True)
        tile(HALO + rows, 2 + half, tiles - 1, half, True)
    for j in range(4, group):
        pay_ref[j, (tiles - 1) * members : tiles * members, :] = jnp.zeros((members, TILE), BF16)
    for j in range(group):
        pay_ref[j, tiles * members :, :] = m_ref[j].astype(BF16)
    prior_ref[...] = src[HALO - 1 : HALO + rows + 1]


def analysis_kernel(anom_at_ref, weight_at_ref, tapers_ref, recv_ref, taper_ref, *rest):
    pieces, (ret_ref, obs_ref, centred_ref, sems) = rest[:-4], rest[-4:]
    group, size, _ = recv_ref.shape
    count = ret_ref.shape[1] // anom_at_ref.shape[0]
    tiles = anom_at_ref.shape[0]
    members = group * count
    core = lax.rem(lax.axis_index("mem"), 2)
    copies = []
    for side in range(2):
        start = 0
        for piece in pieces[side * len(pieces) // 2 : (side + 1) * len(pieces) // 2]:
            length = piece.shape[0]
            to = obs_ref.at[core if side == 0 else 1 - core, pl.ds(start, length)]
            copies.append(pltpu.make_async_copy(piece, to, sems.at[len(copies)]))
            start += length
    for copy in copies:
        copy.start()

    parts = recv_ref[:, size - 32 :, :].astype(F32)
    for t in range(tiles):
        own = parts[:, 3 * t, :] + parts[:, 3 * t + 1, :] + parts[:, 3 * t + 2, :]
        delta = own - jnp.mean(own, axis=0, keepdims=True)
        local = recv_ref[:, t * count : (t + 1) * count, :].astype(F32)
        centred_ref[t] = (local + delta[:, None, :]).astype(BF16).reshape(members, TILE)
    for copy in copies:
        copy.wait()

    def one(t, carry):
        anoms, weights = [], []
        for k in range(SLOTS):
            at = anom_at_ref[t, k]
            anoms.append(jnp.concatenate([obs_ref[0, at, q * TILE : (q + 1) * TILE, :] for q in range(members // TILE)], axis=1))
            weights.append(obs_ref[1, weight_at_ref[t, k]])
        cov = jnp.dot(jnp.concatenate(anoms, axis=0), centred_ref[t], preferred_element_type=F32) * (1.0 / (members - 1.0))
        tapered = [
            (taper_ref[tapers_ref[t, k]] * cov[k * TILE : (k + 1) * TILE]).astype(BF16) for k in range(SLOTS)
        ]
        total = jnp.dot(jnp.concatenate(weights, axis=1), jnp.concatenate(tapered, axis=0), preferred_element_type=F32)
        here = pl.ds(pl.multiple_of(t * count, count), count)
        ret_ref[:, here, :] = total.astype(BF16).reshape(group, count, TILE)
        return carry

    lax.fori_loop(0, tiles, one, 0, unroll=3)


def final_kernel(prior_ref, inc_ref, coef_ref, out_ref, v_ref):
    members, depth, columns = out_ref.shape
    group, size, _ = inc_ref.shape
    rows = prior_ref.shape[0] - 2
    per = rows // group
    extra = size // members - 1
    i, steps = pl.program_id(0), pl.num_programs(0)

    def put(index, j, slot, half):
        lanes = slice(half * TILE, (half + 1) * TILE)
        here = pl.ds(pl.multiple_of(slot * members, members), members)
        v_ref[index, :, lanes] = prior_ref[i * depth + index, :, lanes] + inc_ref[j, here, :].astype(F32)

    first = i * (depth // per)
    for half in range(2):
        top, bottom = i == 0, i == steps - 1
        put(0, jnp.where(top, half, first - 1), jnp.where(top, extra, 2 * (per - 1) + half), half)
        put(depth + 1, jnp.where(bottom, 2 + half, first + depth // per), jnp.where(bottom, extra, half), half)
        for r in range(depth):
            put(r + 1, first + r // per, 2 * (r % per) + half, half)
    coef = coef_ref[...]
    for r in range(depth):
        mid = v_ref[r + 1]
        beside = v_ref[r] + v_ref[r + 2] + pltpu.roll(mid, 1, 1) + pltpu.roll(mid, columns - 1, 1)
        out_ref[:, r, :] = mid + coef[r : r + 1, :] * (beside - 4.0 * mid)


AXES = ("mem", "state")


def fetch(value, mesh, source):
    xs, ys, zs = mesh
    pairs = []
    for x in range(xs):
        for c in range(2):
            for y in range(ys):
                for z in range(zs):
                    a, b, d, e = source(x, c, y, z)
                    pairs.append((((a * 2 + b) * ys + d % ys) * zs + e % zs, ((x * 2 + c) * ys + y) * zs + z))
    return lax.ppermute(value, AXES, pairs)


def ring(first, step):
    return lambda x, c, y, z: (x, c, y + step, z) if (c == 0) == first else (x, c, y, z + step)


def other_core(x, c, y, z):
    return (x, 1 - c, y, z)


def whole(value):
    return pl.BlockSpec(value.shape, lambda i, c: (0,) * len(value.shape))


def join(operands, core, name, after=(), split=False):
    count, blocks = len(operands), operands[0].shape[0]

    def kernel(core_ref, *refs):
        outs = refs[count + len(after) :]
        for i in range(blocks):
            for a in range(count):
                outs[0][i * count + a] = refs[a][i]
        if split:
            for a in range(count):
                outs[1][a] = refs[a][0]
                outs[2][a] = refs[a][core_ref[0]]

    shapes = [(count * blocks, *operands[0].shape[1:])] + [(count, *operands[0].shape[1:])] * (2 * split)
    return pl.pallas_call(
        kernel,
        out_shape=[jax.ShapeDtypeStruct(shape, BF16) for shape in shapes],
        grid_spec=pltpu.PrefetchScalarGridSpec(
            num_scalar_prefetch=1,
            grid=(1,),
            in_specs=[whole(v) for v in operands] + [pl.BlockSpec((1, 16, TILE), lambda i, c: (0, 0, 0))] * len(after),
            out_specs=[pl.BlockSpec(shape, lambda i, c: (0, 0, 0)) for shape in shapes],
        ),
        name=name,
    )(core, *operands, *after)


def gather_obs(own, mesh, core, edges, payload):
    far = fetch(own, mesh, lambda x, c, y, z: (x, c, y, z + 4))
    (held,) = join([own, far], core, "join_two", edges)
    p, m, q = (fetch(held, mesh, ring(True, step)) for step in (1, -1, 2))
    held, first, second = join([held, p, m, q], core, "join_eight", [payload], split=True)
    p, m = (fetch(held, mesh, ring(False, step)) for step in (1, -1))
    q = fetch(first, mesh, ring(False, 2))
    r = fetch(second, mesh, ring(False, -2))
    own = [held, p, m, q, r]
    return own, [fetch(v, mesh, other_core) for v in own]


def places(block, y, z):
    dy, dz = (block // 8 - y) % 4, (block % 8 - z) % 8
    low = dz % 4
    gray_y, gray_z = dy ^ (dy >> 1), low ^ (low >> 1)
    high = 4 * ((dz // 4) ^ (low == 3).astype(jnp.int32))
    return 8 * gray_z + high + gray_y, 8 * gray_y + high + gray_z


def body(ensemble, spreading_coefficient, obs_anom, obs_weight, taper_table, obs_block, taper_id):
    members, rows, columns = ensemble.shape
    group = lax.axis_size("mem")
    states = lax.axis_size("state")
    per = rows // group
    tiles = 2 * per + 1
    size = tiles * members + 32
    limit = pltpu.CompilerParams(vmem_limit_bytes=48 << 20)

    j, at = lax.axis_index("mem"), lax.axis_index("state")
    packed = pl.pallas_call(
        pack_obs_kernel,
        out_shape=jax.ShapeDtypeStruct((1, obs_anom.shape[2], TILE), BF16),
        in_specs=[VMEM] * 2,
        out_specs=VMEM,
        name="pack_obs",
    )(obs_anom, obs_weight)
    up, down = pl.pallas_call(
        pack_halo_kernel,
        grid=(1,),
        out_shape=[jax.ShapeDtypeStruct((HALO, members + 8, columns), F32)] * 2,
        in_specs=[
            pl.BlockSpec((members, 8, columns), lambda i: (0, 0, 0)),
            pl.BlockSpec((members, 8, columns), lambda i: (0, rows // 8 - 1, 0)),
            VMEM,
            SMEM,
            SMEM,
        ],
        out_specs=[VMEM] * 2,
        name="pack_halo",
    )(ensemble, ensemble, spreading_coefficient, obs_block.T, taper_id.T)
    below = lax.ppermute(up, "state", [(i + 1, i) for i in range(states - 1)])
    above = lax.ppermute(down, "state", [(i, i + 1) for i in range(states - 1)])

    prior, payload = pl.pallas_call(
        forecast_kernel,
        out_shape=[
            jax.ShapeDtypeStruct((rows + 2, members, columns), F32),
            jax.ShapeDtypeStruct((group, size, TILE), BF16),
        ],
        in_specs=[VMEM] * 4,
        out_specs=[VMEM] * 2,
        scratch_shapes=[
            pltpu.VMEM((rows + 2 * HALO, members, columns), F32),
            pltpu.VMEM((rows + 2 * HALO, members, columns), F32),
            pltpu.VMEM((rows + 2 * HALO, 8, columns), F32),
            pltpu.VMEM((group, 32, TILE), F32),
        ],
        compiler_params=limit,
        name="forecast4",
    )(ensemble, above, below, spreading_coefficient)
    core = (j % 2).reshape(1)
    own, swapped = gather_obs(packed, (group // 2, states // 8, 8), core, [up, down], payload)
    gathered = lax.all_to_all(payload, "mem", split_axis=0, concat_axis=0, tiled=True)

    edge = jnp.where(j < 2, above[0, members, :16], below[HALO - 1, members, :16])
    edge = jnp.where(j % 2 == 0, edge.reshape(-1, 4)[:3:2], edge.reshape(-1, 4)[1:4:2]).astype(jnp.int32)
    mine = 2 * per * j
    blocks = jnp.concatenate([lax.dynamic_slice_in_dim(obs_block, mine, 2 * per, 0), edge[0:1]], axis=0)
    tapers = jnp.concatenate([lax.dynamic_slice_in_dim(taper_id, mine, 2 * per, 0), edge[1:2]], axis=0)

    anom_at, weight_at = places(blocks, at // 8, at % 8)
    increments = pl.pallas_call(
        analysis_kernel,
        out_shape=jax.ShapeDtypeStruct((group, tiles * members, TILE), BF16),
        in_specs=[SMEM] * 3 + [VMEM] * 2 + [pl.BlockSpec(memory_space=pl.ANY)] * (len(own) + len(swapped)),
        out_specs=VMEM,
        scratch_shapes=[
            pltpu.VMEM((2, states, *packed.shape[1:]), BF16),
            pltpu.VMEM((tiles, group * members, TILE), BF16),
            pltpu.SemaphoreType.DMA((len(own) + len(swapped),)),
        ],
        compiler_params=limit,
        name="analysis",
    )(anom_at, weight_at, tapers, gathered, jnp.swapaxes(taper_table, 1, 2), *own, *swapped)
    returned = lax.all_to_all(increments, "mem", split_axis=0, concat_axis=0, tiled=True)

    return pl.pallas_call(
        final_kernel,
        grid=(rows // 8,),
        out_shape=jax.ShapeDtypeStruct((members, rows, columns), F32),
        in_specs=[VMEM] * 2 + [pl.BlockSpec((8, columns), lambda i: (i, 0))],
        out_specs=pl.BlockSpec((members, 8, columns), lambda i: (0, i, 0)),
        scratch_shapes=[pltpu.VMEM((10, members, columns), F32)],
        compiler_params=limit,
        name="final_step",
    )(prior, returned, spreading_coefficient)


def solution(mesh):
    placed = (
        P("mem", "state", None),
        P("state", None),
        P("state", None, None),
        P("state", None, None),
        P(),
        P("state", None),
        P("state", None),
    )
    return jax.shard_map(
        body, mesh=mesh, in_specs=placed, out_specs=P("mem", "state", None), check_vma=False
    )
```

```python
import jax
import jax.numpy as jnp
from jax import lax
from jax.experimental import pallas as pl
from jax.experimental.pallas import tpu as pltpu
from jax.sharding import PartitionSpec as P

F32, BF16 = jnp.float32, jnp.bfloat16
TILE = 128
SLOTS = 4
FSTEPS = 4
HALO = FSTEPS + 1
VMEM = pl.BlockSpec(memory_space=pltpu.VMEM)
SMEM = pl.BlockSpec(memory_space=pltpu.SMEM)


def pack_obs_kernel(anom_ref, weight_ref, out_ref):
    members = anom_ref.shape[2]
    core = lax.rem(lax.axis_index("mem"), 2)

    @pl.when(core == 0)
    def _():
        for q in range(members // TILE):
            out_ref[0, q * TILE : (q + 1) * TILE, :] = anom_ref[0, :, q * TILE : (q + 1) * TILE]

    @pl.when(core == 1)
    def _():
        for q in range(members // TILE):
            out_ref[0, q * TILE : (q + 1) * TILE, :] = weight_ref[0, :, q * TILE : (q + 1) * TILE].T


def pack_halo_kernel(first_ref, last_ref, coef_ref, block_ref, taper_ref, up_ref, down_ref, token_ref):
    members, depth, columns = first_ref.shape
    rows = coef_ref.shape[0]
    tiles = block_ref.shape[1]
    lane = lax.broadcasted_iota(jnp.int32, (8, columns), 1)
    for out_ref, x_ref, start, row0, tile0, far in (
        (up_ref, first_ref, 0, 0, 0, HALO - 1),
        (down_ref, last_ref, depth - HALO, rows - HALO, tiles - 2, 0),
    ):
        for r in range(HALO):
            out_ref[r, 0:members, :] = x_ref[:, start + r, :]
            out_ref[r, members : members + 8, :] = jnp.broadcast_to(coef_ref[row0 + r : row0 + r + 1, :], (8, columns))
        ids = jnp.zeros((8, columns), jnp.int32)
        for t in range(2):
            for k in range(SLOTS):
                ids = jnp.where(lane == t * SLOTS + k, block_ref[k, tile0 + t], ids)
                ids = jnp.where(lane == 8 + t * SLOTS + k, taper_ref[k, tile0 + t], ids)
        out_ref[far, members : members + 8, :] = ids.astype(F32)
    token_ref[...] = jnp.zeros(TOKEN.shape, F32)


def forecast_kernel(x_ref, above_ref, below_ref, coef_ref, token_ref, prior_ref, pay_ref, a_ref, b_ref, c_ref, m_ref):
    members, rows, columns = x_ref.shape
    total = rows + 2 * HALO
    group = pay_ref.shape[0]
    per = rows // group
    tiles = 2 * per + 1
    for r in range(HALO):
        c_ref[r] = above_ref[r, members : members + 8, :]
        c_ref[HALO + rows + r] = below_ref[r, members : members + 8, :]
    for r in range(rows):
        c_ref[HALO + r] = jnp.broadcast_to(coef_ref[r : r + 1, :], (8, columns))
    chunk = 16

    def advance(number, carry):
        here = pl.ds(pl.multiple_of(number * chunk, chunk), chunk)
        for r in range(HALO):
            a_ref[r, here, :] = above_ref[r, here, :]
            a_ref[HALO + rows + r, here, :] = below_ref[r, here, :]
        for r in range(rows):
            a_ref[HALO + r, here, :] = x_ref[here, r, :]
        src, dst = a_ref, b_ref
        for step in range(1, FSTEPS + 1):
            for r in range(step, total - step):
                mid = src[r, here, :]
                beside = src[r - 1, here, :] + src[r + 1, here, :] + pltpu.roll(mid, 1, 1) + pltpu.roll(mid, columns - 1, 1)
                delta = (beside - 4.0 * mid).reshape(chunk // 8, 8, columns)
                dst[r, here, :] = mid + (c_ref[r][None] * delta).reshape(chunk, columns)
            src, dst = dst, src
        return carry

    lax.fori_loop(0, members // chunk, advance, 0)
    src = a_ref if FSTEPS % 2 == 0 else b_ref
    m_ref[...] = jnp.zeros_like(m_ref)

    def tile(index, dest, slot, half, keep):
        value = src[index, :, half * TILE : (half + 1) * TILE]
        mean = jnp.sum(value, axis=0, keepdims=True) * (1.0 / members)
        pay_ref[dest, slot * members : (slot + 1) * members, :] = (value - mean).astype(BF16)
        high = mean.astype(BF16).astype(F32)
        middle = (mean - high).astype(BF16).astype(F32)
        m_ref[dest, 3 * slot : 3 * slot + 1, :] = high
        m_ref[dest, 3 * slot + 1 : 3 * slot + 2, :] = middle
        m_ref[dest, 3 * slot + 2 : 3 * slot + 3, :] = mean - high - middle

    for j in range(group):
        for i in range(per):
            for half in range(2):
                tile(HALO + j * per + i, j, 2 * i + half, half, True)
    for half in range(2):
        tile(HALO - 1, half, tiles - 1, half, True)
        tile(HALO + rows, 2 + half, tiles - 1, half, True)
    for j in range(4, group):
        pay_ref[j, (tiles - 1) * members : tiles * members, :] = jnp.zeros((members, TILE), BF16)
    for j in range(group):
        pay_ref[j, tiles * members :, :] = m_ref[j].astype(BF16)
    prior_ref[...] = src[HALO - 1 : HALO + rows + 1]


def analysis_kernel(anom_at_ref, weight_at_ref, tapers_ref, recv_ref, taper_ref, *rest):
    pieces, (ret_ref, obs_ref, centred_ref) = rest[:-3], rest[-3:]
    group, size, _ = recv_ref.shape
    count = ret_ref.shape[1] // anom_at_ref.shape[0]
    tiles = anom_at_ref.shape[0]
    members = group * count
    core = lax.rem(lax.axis_index("mem"), 2)
    for side in range(2):
        start = 0
        kind = core if side == 0 else 1 - core
        for piece in pieces[side * len(pieces) // 2 : (side + 1) * len(pieces) // 2]:

            def keep(i, carry, piece=piece, start=start, kind=kind):
                obs_ref[kind, start + i] = piece[i]
                return carry

            lax.fori_loop(0, piece.shape[0], keep, 0)
            start += piece.shape[0]

    parts = recv_ref[:, size - 32 :, :].astype(F32)
    for t in range(tiles):
        own = parts[:, 3 * t, :] + parts[:, 3 * t + 1, :] + parts[:, 3 * t + 2, :]
        delta = own - jnp.mean(own, axis=0, keepdims=True)
        local = recv_ref[:, t * count : (t + 1) * count, :].astype(F32)
        centred_ref[t] = (local + delta[:, None, :]).astype(BF16).reshape(members, TILE)
    def one(t, carry):
        anoms, weights = [], []
        for k in range(SLOTS):
            at = anom_at_ref[t, k]
            anoms.append(jnp.concatenate([obs_ref[0, at, q * TILE : (q + 1) * TILE, :] for q in range(members // TILE)], axis=1))
            weights.append(obs_ref[1, weight_at_ref[t, k]])
        cov = jnp.dot(jnp.concatenate(anoms, axis=0), centred_ref[t], preferred_element_type=F32) * (1.0 / (members - 1.0))
        tapered = [
            (taper_ref[tapers_ref[t, k]] * cov[k * TILE : (k + 1) * TILE]).astype(BF16) for k in range(SLOTS)
        ]
        total = jnp.dot(jnp.concatenate(weights, axis=1), jnp.concatenate(tapered, axis=0), preferred_element_type=F32)
        here = pl.ds(pl.multiple_of(t * count, count), count)
        ret_ref[:, here, :] = total.astype(BF16).reshape(group, count, TILE)
        return carry

    lax.fori_loop(0, tiles, one, 0, unroll=3)


def final_kernel(prior_ref, inc_ref, coef_ref, out_ref, v_ref):
    members, depth, columns = out_ref.shape
    group, size, _ = inc_ref.shape
    rows = prior_ref.shape[0] - 2
    per = rows // group
    extra = size // members - 1
    i, steps = pl.program_id(0), pl.num_programs(0)

    def put(index, j, slot, half):
        lanes = slice(half * TILE, (half + 1) * TILE)
        here = pl.ds(pl.multiple_of(slot * members, members), members)
        v_ref[index, :, lanes] = prior_ref[i * depth + index, :, lanes] + inc_ref[j, here, :].astype(F32)

    first = i * (depth // per)
    for half in range(2):
        top, bottom = i == 0, i == steps - 1
        put(0, jnp.where(top, half, first - 1), jnp.where(top, extra, 2 * (per - 1) + half), half)
        put(depth + 1, jnp.where(bottom, 2 + half, first + depth // per), jnp.where(bottom, extra, half), half)
        for r in range(depth):
            put(r + 1, first + r // per, 2 * (r % per) + half, half)
    coef = coef_ref[...]
    for r in range(depth):
        mid = v_ref[r + 1]
        beside = v_ref[r] + v_ref[r + 2] + pltpu.roll(mid, 1, 1) + pltpu.roll(mid, columns - 1, 1)
        out_ref[:, r, :] = mid + coef[r : r + 1, :] * (beside - 4.0 * mid)


AXES = ("mem", "state")


def fetch(value, mesh, source):
    xs, ys, zs = mesh
    pairs = []
    for x in range(xs):
        for c in range(2):
            for y in range(ys):
                for z in range(zs):
                    a, b, d, e = source(x, c, y, z)
                    pairs.append((((a * 2 + b) * ys + d % ys) * zs + e % zs, ((x * 2 + c) * ys + y) * zs + z))
    return lax.ppermute(value, AXES, pairs)


def ring(first, step):
    return lambda x, c, y, z: (x, c, y + step, z) if (c == 0) == first else (x, c, y, z + step)


def other_core(x, c, y, z):
    return (x, 1 - c, y, z)


TOKEN = jax.ShapeDtypeStruct((8, TILE), F32)


def join(operands, name, after=(), split=False):
    count, blocks = len(operands), operands[0].shape[0]

    def kernel(*refs):
        outs = refs[count + len(after) :]
        core = lax.rem(lax.axis_index("mem"), 2)
        for i in range(blocks):
            for a in range(count):
                outs[0][i * count + a] = refs[a][i]
        if split:
            for a in range(count):
                outs[1][a] = refs[a][0]
                outs[2][a] = refs[a][core]
        outs[-1][...] = jnp.zeros(TOKEN.shape, F32)

    shapes = [(count * blocks, *operands[0].shape[1:])] + [(count, *operands[0].shape[1:])] * (2 * split)
    return pl.pallas_call(
        kernel,
        out_shape=[jax.ShapeDtypeStruct(shape, BF16) for shape in shapes] + [TOKEN],
        in_specs=[VMEM] * (count + len(after)),
        out_specs=[VMEM] * (len(shapes) + 1),
        compiler_params=pltpu.CompilerParams(vmem_limit_bytes=6 << 20),
        name=name,
    )(*operands, *after)


def gather_start(own, mesh, packed_halo, arrived):
    far = fetch(own, mesh, lambda x, c, y, z: (x, c, y, z + 4))
    held, _ = join([own, far], "join_two", [packed_halo])
    p, m, q = (fetch(held, mesh, ring(True, step)) for step in (1, -1, 2))
    return join([held, p, m, q], "join_eight", arrived, split=True)


def gather_rest(held, first, second, mesh):
    p, m = (fetch(held, mesh, ring(False, step)) for step in (1, -1))
    q = fetch(first, mesh, ring(False, 2))
    r = fetch(second, mesh, ring(False, -2))
    own = [held, p, m, q, r]
    return own, [fetch(v, mesh, other_core) for v in own]


def places(block, y, z):
    dy, dz = (block // 8 - y) % 4, (block % 8 - z) % 8
    low = dz % 4
    gray_y, gray_z = dy ^ (dy >> 1), low ^ (low >> 1)
    high = 4 * ((dz // 4) ^ (low == 3).astype(jnp.int32))
    return 8 * gray_z + high + gray_y, 8 * gray_y + high + gray_z


def body(ensemble, spreading_coefficient, obs_anom, obs_weight, taper_table, obs_block, taper_id):
    members, rows, columns = ensemble.shape
    group = lax.axis_size("mem")
    states = lax.axis_size("state")
    per = rows // group
    tiles = 2 * per + 1
    size = tiles * members + 32

    j, at = lax.axis_index("mem"), lax.axis_index("state")
    packed = pl.pallas_call(
        pack_obs_kernel,
        out_shape=jax.ShapeDtypeStruct((1, obs_anom.shape[2], TILE), BF16),
        in_specs=[VMEM] * 2,
        out_specs=VMEM,
        name="pack_obs",
    )(obs_anom, obs_weight)
    up, down, packed_halo = pl.pallas_call(
        pack_halo_kernel,
        grid=(1,),
        out_shape=[jax.ShapeDtypeStruct((HALO, members + 8, columns), F32)] * 2 + [TOKEN],
        in_specs=[
            pl.BlockSpec((members, 8, columns), lambda i: (0, 0, 0)),
            pl.BlockSpec((members, 8, columns), lambda i: (0, rows // 8 - 1, 0)),
            VMEM,
            SMEM,
            SMEM,
        ],
        out_specs=[VMEM] * 3,
        name="pack_halo",
    )(ensemble, ensemble, spreading_coefficient, obs_block.T, taper_id.T)
    below = lax.ppermute(up, "state", [(i + 1, i) for i in range(states - 1)])
    above = lax.ppermute(down, "state", [(i, i + 1) for i in range(states - 1)])

    chips = (group // 2, states // 8, 8)
    held, first, second, joined = gather_start(packed, chips, packed_halo, [above, below])
    own, swapped = gather_rest(held, first, second, chips)
    prior, payload = pl.pallas_call(
        forecast_kernel,
        out_shape=[
            jax.ShapeDtypeStruct((rows + 2, members, columns), F32),
            jax.ShapeDtypeStruct((group, size, TILE), BF16),
        ],
        in_specs=[VMEM] * 5,
        out_specs=[VMEM] * 2,
        scratch_shapes=[
            pltpu.VMEM((rows + 2 * HALO, members, columns), F32),
            pltpu.VMEM((rows + 2 * HALO, members, columns), F32),
            pltpu.VMEM((rows + 2 * HALO, 8, columns), F32),
            pltpu.VMEM((group, 32, TILE), F32),
        ],
        compiler_params=pltpu.CompilerParams(vmem_limit_bytes=14 << 20),
        name="forecast4",
    )(ensemble, above, below, spreading_coefficient, joined)
    gathered = lax.all_to_all(payload, "mem", split_axis=0, concat_axis=0, tiled=True)

    edge = jnp.where(j < 2, above[0, members, :16], below[HALO - 1, members, :16])
    edge = jnp.where(j % 2 == 0, edge.reshape(-1, 4)[:3:2], edge.reshape(-1, 4)[1:4:2]).astype(jnp.int32)
    mine = 2 * per * j
    blocks = jnp.concatenate([lax.dynamic_slice_in_dim(obs_block, mine, 2 * per, 0), edge[0:1]], axis=0)
    tapers = jnp.concatenate([lax.dynamic_slice_in_dim(taper_id, mine, 2 * per, 0), edge[1:2]], axis=0)

    anom_at, weight_at = places(blocks, at // 8, at % 8)
    increments = pl.pallas_call(
        analysis_kernel,
        out_shape=jax.ShapeDtypeStruct((group, tiles * members, TILE), BF16),
        in_specs=[SMEM] * 3 + [VMEM] * (2 + len(own) + len(swapped)),
        out_specs=VMEM,
        scratch_shapes=[
            pltpu.VMEM((2, states, *packed.shape[1:]), BF16),
            pltpu.VMEM((tiles, group * members, TILE), BF16),
        ],
        compiler_params=pltpu.CompilerParams(vmem_limit_bytes=22 << 20),
        name="analysis",
    )(anom_at, weight_at, tapers, gathered, jnp.swapaxes(taper_table, 1, 2), *own, *swapped)
    returned = lax.all_to_all(increments, "mem", split_axis=0, concat_axis=0, tiled=True)

    return pl.pallas_call(
        final_kernel,
        grid=(rows // 8,),
        out_shape=jax.ShapeDtypeStruct((members, rows, columns), F32),
        in_specs=[VMEM] * 2 + [pl.BlockSpec((8, columns), lambda i: (i, 0))],
        out_specs=pl.BlockSpec((members, 8, columns), lambda i: (0, i, 0)),
        scratch_shapes=[pltpu.VMEM((10, members, columns), F32)],
        compiler_params=pltpu.CompilerParams(vmem_limit_bytes=10 << 20),
        name="final_step",
    )(prior, returned, spreading_coefficient)


def solution(mesh):
    placed = (
        P("mem", "state", None),
        P("state", None),
        P("state", None, None),
        P("state", None, None),
        P(),
        P("state", None),
        P("state", None),
    )
    return jax.shard_map(
        body, mesh=mesh, in_specs=placed, out_specs=P("mem", "state", None), check_vma=False
    )
```

```python
import jax
import jax.numpy as jnp
from jax import lax
from jax.experimental import pallas as pl
from jax.experimental.pallas import tpu as pltpu
from jax.sharding import PartitionSpec as P

F32, BF16 = jnp.float32, jnp.bfloat16
TILE = 128
SLOTS = 4
FSTEPS = 4
HALO = FSTEPS + 1
VMEM = pl.BlockSpec(memory_space=pltpu.VMEM)
SMEM = pl.BlockSpec(memory_space=pltpu.SMEM)
HBM = pl.BlockSpec(memory_space=pltpu.HBM)


def pack_obs(anom_ref, weight_ref, out_ref):
    members = anom_ref.shape[2]
    core = lax.rem(lax.axis_index("mem"), 2)

    @pl.when(core == 0)
    def _():
        for q in range(members // TILE):
            out_ref[0, q * TILE : (q + 1) * TILE, :] = anom_ref[0, :, q * TILE : (q + 1) * TILE]

    @pl.when(core == 1)
    def _():
        for q in range(members // TILE):
            out_ref[0, q * TILE : (q + 1) * TILE, :] = weight_ref[0, :, q * TILE : (q + 1) * TILE].T


def pack_kernel(first_ref, last_ref, coef_ref, block_ref, taper_ref, anom_ref, weight_ref, up_ref, down_ref, own_ref):
    pack_obs(anom_ref, weight_ref, own_ref)
    members, depth, columns = first_ref.shape
    rows = coef_ref.shape[0]
    tiles = block_ref.shape[1]
    lane = lax.broadcasted_iota(jnp.int32, (8, columns), 1)
    for out_ref, x_ref, start, row0, tile0, far in (
        (up_ref, first_ref, 0, 0, 0, HALO - 1),
        (down_ref, last_ref, depth - HALO, rows - HALO, tiles - 2, 0),
    ):
        for r in range(HALO):
            out_ref[r, 0:members, :] = x_ref[:, start + r, :]
            out_ref[r, members : members + 8, :] = jnp.broadcast_to(coef_ref[row0 + r : row0 + r + 1, :], (8, columns))
        ids = jnp.zeros((8, columns), jnp.int32)
        for t in range(2):
            for k in range(SLOTS):
                ids = jnp.where(lane == t * SLOTS + k, block_ref[k, tile0 + t], ids)
                ids = jnp.where(lane == 8 + t * SLOTS + k, taper_ref[k, tile0 + t], ids)
        out_ref[far, members : members + 8, :] = ids.astype(F32)


def forecast_kernel(x_ref, above_ref, below_ref, coef_ref, prior_ref, out_ref, token_ref, a_ref, b_ref, c_ref, m_ref, pay_ref, sems):
    members, rows, columns = x_ref.shape
    total = rows + 2 * HALO
    group = pay_ref.shape[0]
    per = rows // group
    tiles = 2 * per + 1
    for r in range(HALO):
        c_ref[r] = above_ref[r, members : members + 8, :]
        c_ref[HALO + rows + r] = below_ref[r, members : members + 8, :]
    for r in range(rows):
        c_ref[HALO + r] = jnp.broadcast_to(coef_ref[r : r + 1, :], (8, columns))
    chunk = 16

    def advance(number, carry):
        here = pl.ds(pl.multiple_of(number * chunk, chunk), chunk)
        for r in range(HALO):
            a_ref[r, here, :] = above_ref[r, here, :]
            a_ref[HALO + rows + r, here, :] = below_ref[r, here, :]
        for r in range(rows):
            a_ref[HALO + r, here, :] = x_ref[here, r, :]
        src, dst = a_ref, b_ref
        for step in range(1, FSTEPS + 1):
            for r in range(step, total - step):
                mid = src[r, here, :]
                beside = src[r - 1, here, :] + src[r + 1, here, :] + pltpu.roll(mid, 1, 1) + pltpu.roll(mid, columns - 1, 1)
                delta = (beside - 4.0 * mid).reshape(chunk // 8, 8, columns)
                dst[r, here, :] = mid + (c_ref[r][None] * delta).reshape(chunk, columns)
            src, dst = dst, src
        return carry

    lax.fori_loop(0, members // chunk, advance, 0)
    src = a_ref if FSTEPS % 2 == 0 else b_ref
    copies = [pltpu.make_async_copy(src.at[pl.ds(HALO - 1, rows + 2)], prior_ref, sems.at[group])]
    copies[0].start()
    m_ref[...] = jnp.zeros_like(m_ref)

    def tile(index, dest, slot, half):
        value = src[index, :, half * TILE : (half + 1) * TILE]
        mean = jnp.sum(value, axis=0, keepdims=True) * (1.0 / members)
        pay_ref[dest, slot * members : (slot + 1) * members, :] = (value - mean).astype(BF16)
        high = mean.astype(BF16).astype(F32)
        middle = (mean - high).astype(BF16).astype(F32)
        m_ref[dest, 3 * slot : 3 * slot + 1, :] = high
        m_ref[dest, 3 * slot + 1 : 3 * slot + 2, :] = middle
        m_ref[dest, 3 * slot + 2 : 3 * slot + 3, :] = mean - high - middle

    for j in range(group):
        for i in range(per):
            for half in range(2):
                tile(HALO + j * per + i, j, 2 * i + half, half)
        if j < 2:
            tile(HALO - 1, j, tiles - 1, j)
        elif j < 4:
            tile(HALO + rows, j, tiles - 1, j - 2)
        else:
            pay_ref[j, (tiles - 1) * members : tiles * members, :] = jnp.zeros((members, TILE), BF16)
        pay_ref[j, tiles * members :, :] = m_ref[j].astype(BF16)
        copies.append(pltpu.make_async_copy(pay_ref.at[j], out_ref.at[j], sems.at[j]))
        copies[-1].start()
    for copy in copies:
        copy.wait()


def fill(pieces, obs_ref):
    core = lax.rem(lax.axis_index("mem"), 2)
    for side in range(2):
        start = 0
        kind = core if side == 0 else 1 - core
        for piece in pieces[side * len(pieces) // 2 : (side + 1) * len(pieces) // 2]:

            def keep(i, carry, piece=piece, start=start, kind=kind):
                obs_ref[kind, start + i] = piece[i]
                return carry

            lax.fori_loop(0, piece.shape[0], keep, 0)
            start += piece.shape[0]


def collect_kernel(recv_ref, *rest):
    pieces, (obs_ref, centred_ref) = rest[:-2], rest[-2:]
    group, size, _ = recv_ref.shape
    tiles, members, _ = centred_ref.shape
    count = members // group
    fill(pieces, obs_ref)
    parts = recv_ref[:, size - 32 :, :].astype(F32)
    for t in range(tiles):
        own = parts[:, 3 * t, :] + parts[:, 3 * t + 1, :] + parts[:, 3 * t + 2, :]
        delta = own - jnp.mean(own, axis=0, keepdims=True)
        local = recv_ref[:, t * count : (t + 1) * count, :].astype(F32)
        centred_ref[t] = (local + delta[:, None, :]).astype(BF16).reshape(members, TILE)


def analysis_kernel(anom_at_ref, weight_at_ref, tapers_ref, taper_ref, centred_ref, early_ref, *rest):
    pieces, (ret_ref, late_ref) = rest[:-2], rest[-2:]
    tiles, members, _ = centred_ref.shape
    group = ret_ref.shape[0]
    count = members // group
    early = early_ref.shape[1]
    fill(pieces, late_ref)

    def block(kind, at):
        near = early_ref[kind, jnp.minimum(at, early - 1)]
        far = late_ref[kind, jnp.maximum(at - early, 0)]
        return jnp.where(at < early, near, far)

    def one(t, carry):
        anoms, weights = [], []
        for k in range(SLOTS):
            anom = block(0, anom_at_ref[t, k])
            anoms.append(jnp.concatenate([anom[q * TILE : (q + 1) * TILE] for q in range(members // TILE)], axis=1))
            weights.append(block(1, weight_at_ref[t, k]))
        cov = jnp.dot(jnp.concatenate(anoms, axis=0), centred_ref[t], preferred_element_type=F32) * (1.0 / (members - 1.0))
        tapered = [
            (taper_ref[tapers_ref[t, k]] * cov[k * TILE : (k + 1) * TILE]).astype(BF16) for k in range(SLOTS)
        ]
        total = jnp.dot(jnp.concatenate(weights, axis=1), jnp.concatenate(tapered, axis=0), preferred_element_type=F32)
        here = pl.ds(pl.multiple_of(t * count, count), count)
        ret_ref[:, here, :] = total.astype(BF16).reshape(group, count, TILE)
        return carry

    lax.fori_loop(0, tiles, one, 0, unroll=3)


def final_kernel(prior_ref, inc_ref, coef_ref, out_ref, v_ref):
    members, depth, columns = out_ref.shape
    group, size, _ = inc_ref.shape
    rows = prior_ref.shape[0] - 2
    per = rows // group
    extra = size // members - 1
    i, steps = pl.program_id(0), pl.num_programs(0)

    def put(index, j, slot, half):
        lanes = slice(half * TILE, (half + 1) * TILE)
        here = pl.ds(pl.multiple_of(slot * members, members), members)
        v_ref[index, :, lanes] = prior_ref[i * depth + index, :, lanes] + inc_ref[j, here, :].astype(F32)

    first = i * (depth // per)
    for half in range(2):
        top, bottom = i == 0, i == steps - 1
        put(0, jnp.where(top, half, first - 1), jnp.where(top, extra, 2 * (per - 1) + half), half)
        put(depth + 1, jnp.where(bottom, 2 + half, first + depth // per), jnp.where(bottom, extra, half), half)
        for r in range(depth):
            put(r + 1, first + r // per, 2 * (r % per) + half, half)
    coef = coef_ref[...]
    for r in range(depth):
        mid = v_ref[r + 1]
        beside = v_ref[r] + v_ref[r + 2] + pltpu.roll(mid, 1, 1) + pltpu.roll(mid, columns - 1, 1)
        out_ref[:, r, :] = mid + coef[r : r + 1, :] * (beside - 4.0 * mid)


AXES = ("mem", "state")


def fetch(value, mesh, source):
    xs, ys, zs = mesh
    pairs = []
    for x in range(xs):
        for c in range(2):
            for y in range(ys):
                for z in range(zs):
                    a, b, d, e = source(x, c, y, z)
                    pairs.append((((a * 2 + b) * ys + d % ys) * zs + e % zs, ((x * 2 + c) * ys + y) * zs + z))
    return lax.ppermute(value, AXES, pairs)


def ring(first, step):
    return lambda x, c, y, z: (x, c, y + step, z) if (c == 0) == first else (x, c, y, z + step)


def other_core(x, c, y, z):
    return (x, 1 - c, y, z)


TOKEN = jax.ShapeDtypeStruct((8, TILE), F32)


def join(operands, name, after=(), split=False):
    count, blocks = len(operands), operands[0].shape[0]

    def kernel(*refs):
        outs = refs[count + len(after) :]
        core = lax.rem(lax.axis_index("mem"), 2)
        for i in range(blocks):
            for a in range(count):
                outs[0][i * count + a] = refs[a][i]
        if split:
            for a in range(count):
                outs[1][a] = refs[a][0]
                outs[2][a] = refs[a][core]

    shapes = [(count * blocks, *operands[0].shape[1:])] + [(count, *operands[0].shape[1:])] * (2 * split)
    return pl.pallas_call(
        kernel,
        out_shape=[jax.ShapeDtypeStruct(shape, BF16) for shape in shapes],
        in_specs=[VMEM] * count + [HBM] * len(after),
        out_specs=[VMEM] * len(shapes),
        compiler_params=pltpu.CompilerParams(vmem_limit_bytes=6 << 20),
        name=name,
    )(*operands, *after)


def gather_start(own, mesh, after):
    far = fetch(own, mesh, lambda x, c, y, z: (x, c, y, z + 4))
    (held,) = join([own, far], "join_two")
    p, m, q = (fetch(held, mesh, ring(True, step)) for step in (1, -1, 2))
    return join([held, p, m, q], "join_eight", after, split=True)


def gather_rest(held, first, second, mesh):
    p, m = (fetch(held, mesh, ring(False, step)) for step in (1, -1))
    q = fetch(first, mesh, ring(False, 2))
    r = fetch(second, mesh, ring(False, -2))
    own = [held, p, m, q, r]
    return own, [fetch(v, mesh, other_core) for v in own]


def places(block, y, z):
    dy, dz = (block // 8 - y) % 4, (block % 8 - z) % 8
    low = dz % 4
    gray_y, gray_z = dy ^ (dy >> 1), low ^ (low >> 1)
    high = 4 * ((dz // 4) ^ (low == 3).astype(jnp.int32))
    return 8 * gray_z + high + gray_y, 8 * gray_y + high + gray_z


def body(ensemble, spreading_coefficient, obs_anom, obs_weight, taper_table, obs_block, taper_id):
    members, rows, columns = ensemble.shape
    group = lax.axis_size("mem")
    states = lax.axis_size("state")
    per = rows // group
    tiles = 2 * per + 1
    size = tiles * members + 32

    j, at = lax.axis_index("mem"), lax.axis_index("state")
    up, down, packed = pl.pallas_call(
        pack_kernel,
        grid=(1,),
        out_shape=[jax.ShapeDtypeStruct((HALO, members + 8, columns), F32)] * 2
        + [jax.ShapeDtypeStruct((1, obs_anom.shape[2], TILE), BF16)],
        in_specs=[
            pl.BlockSpec((members, 8, columns), lambda i: (0, 0, 0)),
            pl.BlockSpec((members, 8, columns), lambda i: (0, rows // 8 - 1, 0)),
            VMEM,
            SMEM,
            SMEM,
            VMEM,
            VMEM,
        ],
        out_specs=[VMEM] * 3,
        name="pack",
    )(ensemble, ensemble, spreading_coefficient, obs_block.T, taper_id.T, obs_anom, obs_weight)
    below = lax.ppermute(up, "state", [(i + 1, i) for i in range(states - 1)])
    above = lax.ppermute(down, "state", [(i, i + 1) for i in range(states - 1)])

    chips = (group // 2, states // 8, 8)
    prior, payload, forecast_done = pl.pallas_call(
        forecast_kernel,
        out_shape=[
            jax.ShapeDtypeStruct((rows + 2, members, columns), F32),
            jax.ShapeDtypeStruct((group, size, TILE), BF16),
            TOKEN,
        ],
        in_specs=[VMEM] * 4,
        out_specs=[HBM] * 3,
        scratch_shapes=[
            pltpu.VMEM((rows + 2 * HALO, members, columns), F32),
            pltpu.VMEM((rows + 2 * HALO, members, columns), F32),
            pltpu.VMEM((rows + 2 * HALO, 8, columns), F32),
            pltpu.VMEM((group, 32, TILE), F32),
            pltpu.VMEM((group, size, TILE), BF16),
            pltpu.SemaphoreType.DMA((group + 1,)),
        ],
        compiler_params=pltpu.CompilerParams(vmem_limit_bytes=14 << 20),
        name="forecast4",
    )(ensemble, above, below, spreading_coefficient)
    held, first, second = gather_start(packed, chips, [forecast_done])
    own, swapped = gather_rest(held, first, second, chips)
    gathered = lax.all_to_all(payload, "mem", split_axis=0, concat_axis=0, tiled=True)

    edge = jnp.where(j < 2, above[0, members, :16], below[HALO - 1, members, :16])
    edge = jnp.where(j % 2 == 0, edge.reshape(-1, 4)[:3:2], edge.reshape(-1, 4)[1:4:2]).astype(jnp.int32)
    mine = 2 * per * j
    blocks = jnp.concatenate([lax.dynamic_slice_in_dim(obs_block, mine, 2 * per, 0), edge[0:1]], axis=0)
    tapers = jnp.concatenate([lax.dynamic_slice_in_dim(taper_id, mine, 2 * per, 0), edge[1:2]], axis=0)

    anom_at, weight_at = places(blocks, at // 8, at % 8)
    late = 2
    early = own[:-late] + swapped[:-late]
    held_early, centred = pl.pallas_call(
        collect_kernel,
        out_shape=[
            jax.ShapeDtypeStruct((2, sum(v.shape[0] for v in own[:-late]), *packed.shape[1:]), BF16),
            jax.ShapeDtypeStruct((tiles, group * members, TILE), BF16),
        ],
        in_specs=[VMEM] * (1 + len(early)),
        out_specs=[VMEM] * 2,
        compiler_params=pltpu.CompilerParams(vmem_limit_bytes=18 << 20),
        name="collect",
    )(gathered, *early)
    increments = pl.pallas_call(
        analysis_kernel,
        out_shape=jax.ShapeDtypeStruct((group, tiles * members, TILE), BF16),
        in_specs=[SMEM] * 3 + [VMEM] * (3 + 2 * late),
        out_specs=VMEM,
        scratch_shapes=[pltpu.VMEM((2, sum(v.shape[0] for v in own[-late:]), *packed.shape[1:]), BF16)],
        compiler_params=pltpu.CompilerParams(vmem_limit_bytes=18 << 20),
        name="analysis",
    )(anom_at, weight_at, tapers, jnp.swapaxes(taper_table, 1, 2), centred, held_early, *own[-late:], *swapped[-late:])
    returned = lax.all_to_all(increments, "mem", split_axis=0, concat_axis=0, tiled=True)

    return pl.pallas_call(
        final_kernel,
        grid=(rows // 8,),
        out_shape=jax.ShapeDtypeStruct((members, rows, columns), F32),
        in_specs=[VMEM] * 2 + [pl.BlockSpec((8, columns), lambda i: (i, 0))],
        out_specs=pl.BlockSpec((members, 8, columns), lambda i: (0, i, 0)),
        scratch_shapes=[pltpu.VMEM((10, members, columns), F32)],
        compiler_params=pltpu.CompilerParams(vmem_limit_bytes=10 << 20),
        name="final_step",
    )(prior, returned, spreading_coefficient)


def solution(mesh):
    placed = (
        P("mem", "state", None),
        P("state", None),
        P("state", None, None),
        P("state", None, None),
        P(),
        P("state", None),
        P("state", None),
    )
    return jax.shard_map(
        body, mesh=mesh, in_specs=placed, out_specs=P("mem", "state", None), check_vma=False
    )
```

```python
import jax
import jax.numpy as jnp
from jax import lax
from jax.experimental import pallas as pl
from jax.experimental.pallas import tpu as pltpu
from jax.sharding import PartitionSpec as P

F32, BF16 = jnp.float32, jnp.bfloat16
TILE = 128
SLOTS = 4
FSTEPS = 4
HALO = FSTEPS + 1
VMEM = pl.BlockSpec(memory_space=pltpu.VMEM)
SMEM = pl.BlockSpec(memory_space=pltpu.SMEM)
HBM = pl.BlockSpec(memory_space=pltpu.HBM)


def pack_obs(anom_ref, weight_ref, out_ref):
    members = anom_ref.shape[2]
    core = lax.rem(lax.axis_index("mem"), 2)

    @pl.when(core == 0)
    def _():
        for q in range(members // TILE):
            out_ref[0, q * TILE : (q + 1) * TILE, :] = anom_ref[0, :, q * TILE : (q + 1) * TILE]

    @pl.when(core == 1)
    def _():
        for q in range(members // TILE):
            out_ref[0, q * TILE : (q + 1) * TILE, :] = weight_ref[0, :, q * TILE : (q + 1) * TILE].T


def pack_kernel(first_ref, last_ref, coef_ref, block_ref, taper_ref, anom_ref, weight_ref, up_ref, down_ref, own_ref):
    pack_obs(anom_ref, weight_ref, own_ref)
    members, depth, columns = first_ref.shape
    rows = coef_ref.shape[0]
    tiles = block_ref.shape[1]
    lane = lax.broadcasted_iota(jnp.int32, (8, columns), 1)
    for out_ref, x_ref, start, row0, tile0 in (
        (up_ref, first_ref, 0, 0, 0),
        (down_ref, last_ref, depth - HALO, rows - HALO, tiles - 2),
    ):
        for r in range(HALO):
            out_ref[r * members : (r + 1) * members, :] = x_ref[:, start + r, :]
        ids = jnp.zeros((8, columns), jnp.int32)
        for t in range(2):
            for k in range(SLOTS):
                ids = jnp.where(lane == t * SLOTS + k, block_ref[k, tile0 + t], ids)
                ids = jnp.where(lane == 8 + t * SLOTS + k, taper_ref[k, tile0 + t], ids)
        out_ref[HALO * members :, :] = ids.astype(F32)
        out_ref[HALO * members : HALO * members + HALO, :] = coef_ref[row0 : row0 + HALO, :]


def stepped(mid, one_side, other_side, coef):
    chunk, columns = mid.shape
    beside = one_side + other_side + pltpu.roll(mid, 1, 1) + pltpu.roll(mid, columns - 1, 1)
    delta = (beside - 4.0 * mid).reshape(chunk // 8, 8, columns)
    return mid + (coef[None] * delta).reshape(chunk, columns)


def split_tile(value, slot, members, pay_ref, mean_ref):
    mean = jnp.sum(value, axis=0, keepdims=True) * (1.0 / members)
    pay_ref[slot * members : (slot + 1) * members, :] = (value - mean).astype(BF16)
    high = mean.astype(BF16).astype(F32)
    middle = (mean - high).astype(BF16).astype(F32)
    mean_ref[3 * slot : 3 * slot + 1, :] = high
    mean_ref[3 * slot + 1 : 3 * slot + 2, :] = middle
    mean_ref[3 * slot + 2 : 3 * slot + 3, :] = mean - high - middle


def interior_kernel(x_ref, coef_ref, taper_ref, token_ref, prior_ref, out_ref, edge_ref, mean_ref, turned_ref, a_ref, b_ref, c_ref, pay_ref, sems):
    members, rows, columns = x_ref.shape
    group = out_ref.shape[0]
    per = rows // group
    for r in range(rows):
        c_ref[r] = jnp.broadcast_to(coef_ref[r : r + 1, :], (8, columns))
    chunk = 16

    def advance(number, carry):
        here = pl.ds(pl.multiple_of(number * chunk, chunk), chunk)
        for r in range(rows):
            a_ref[r, here, :] = x_ref[here, r, :]
        src, dst = a_ref, b_ref
        for step in range(1, FSTEPS + 1):
            done = step - 1
            for i, r in enumerate((done, done + 1, rows - 1 - done, rows - 2 - done)):
                edge_ref[4 * done + i, here, :] = src[r, here, :]
            for r in range(step, rows - step):
                dst[r, here, :] = stepped(src[r, here, :], src[r - 1, here, :], src[r + 1, here, :], c_ref[r])
            src, dst = dst, src
        return carry

    lax.fori_loop(0, members // chunk, advance, 0)
    src = a_ref if FSTEPS % 2 == 0 else b_ref
    inner = rows - 2 * FSTEPS
    copies = [pltpu.make_async_copy(src.at[pl.ds(FSTEPS, inner)], prior_ref.at[pl.ds(FSTEPS + 1, inner)], sems.at[0])]
    copies[0].start()
    mean_ref[...] = jnp.zeros_like(mean_ref)
    for j in range(1, group - 1):
        for i in range(per):
            for half in range(2):
                value = src[j * per + i, :, half * TILE : (half + 1) * TILE]
                split_tile(value, 2 * i + half, members, pay_ref.at[j], mean_ref.at[j])
        copies.append(pltpu.make_async_copy(pay_ref.at[j], out_ref.at[j, pl.ds(0, 2 * per * members)], sems.at[j]))
        copies[-1].start()
    for i in range(taper_ref.shape[0]):
        turned_ref[i] = taper_ref[i].T
    for copy in copies:
        copy.wait()


def edge_kernel(above_ref, below_ref, coef_ref, edge_ref, mean_ref, prior_in, pay_in, prior_ref, out_ref, token_ref, a_ref, b_ref, c_ref, pay_ref, m_ref, last_ref, sems):
    rows, columns = coef_ref.shape
    members = last_ref.shape[2]
    group, size, _ = out_ref.shape
    per = rows // group
    tiles = 2 * per + 1
    halos = (above_ref, below_ref)
    for side in range(2):
        for t in range(HALO + FSTEPS):
            if t < HALO:
                r = HALO * members + (t if side == 0 else HALO - 1 - t)
                row = halos[side][r : r + 1, :]
            else:
                r = t - HALO if side == 0 else rows - 1 - (t - HALO)
                row = coef_ref[r : r + 1, :]
            c_ref[side, t] = jnp.broadcast_to(row, (8, columns))
    chunk = 16

    def advance(number, carry):
        here = pl.ds(pl.multiple_of(number * chunk, chunk), chunk)
        for side in range(2):

            def value(step, t, side=side):
                if t > step + HALO - 1:
                    return edge_ref[4 * step + 2 * side + t - step - HALO, here, :]
                if step == 0:
                    r = t if side == 0 else HALO - 1 - t
                    return halos[side][pl.ds(pl.multiple_of(r * members + number * chunk, chunk), chunk), :]
                return (a_ref, b_ref)[step % 2][side, t, here, :]

            for step in range(1, FSTEPS + 1):
                for t in range(step, step + HALO):
                    new = stepped(value(step - 1, t), value(step - 1, t - 1), value(step - 1, t + 1), c_ref[side, t])
                    if step < FSTEPS:
                        (a_ref, b_ref)[step % 2][side, t, here, :] = new
                    else:
                        last_ref[side, t - FSTEPS if side == 0 else 2 * FSTEPS - t, here, :] = new
        return carry

    lax.fori_loop(0, members // chunk, advance, 0)
    copies = [
        pltpu.make_async_copy(last_ref.at[0], prior_ref.at[pl.ds(0, HALO)], sems.at[0]),
        pltpu.make_async_copy(last_ref.at[1], prior_ref.at[pl.ds(rows + 2 - HALO, HALO)], sems.at[1]),
    ]
    for copy in copies:
        copy.start()
    m_ref[...] = mean_ref[...]
    extra = tiles - 1
    for j in range(group):
        if j in (0, group - 1):
            for i in range(per):
                for half in range(2):
                    row = last_ref[0, i + 1] if j == 0 else last_ref[1, i]
                    split_tile(row[:, half * TILE : (half + 1) * TILE], 2 * i + half, members, pay_ref.at[j], m_ref.at[j])
        if j < 4:
            row = last_ref[0, 0] if j < 2 else last_ref[1, HALO - 1]
            split_tile(row[:, (j % 2) * TILE : (j % 2 + 1) * TILE], extra, members, pay_ref.at[j], m_ref.at[j])
        else:
            pay_ref[j, extra * members : tiles * members, :] = jnp.zeros((members, TILE), BF16)
        pay_ref[j, tiles * members :, :] = m_ref[j].astype(BF16)
        first = 0 if j in (0, group - 1) else extra * members
        part = pl.ds(first, size - first)
        copies.append(pltpu.make_async_copy(pay_ref.at[j, part], out_ref.at[j, part], sems.at[2 + j]))
        copies[-1].start()
    for copy in copies:
        copy.wait()


def fill(pieces, obs_ref):
    core = lax.rem(lax.axis_index("mem"), 2)
    for side in range(2):
        start = 0
        kind = core if side == 0 else 1 - core
        for piece in pieces[side * len(pieces) // 2 : (side + 1) * len(pieces) // 2]:

            def keep(i, carry, piece=piece, start=start, kind=kind):
                obs_ref[kind, start + i] = piece[i]
                return carry

            lax.fori_loop(0, piece.shape[0], keep, 0)
            start += piece.shape[0]


def collect_kernel(recv_ref, *rest):
    pieces, (obs_ref, centred_ref) = rest[:-2], rest[-2:]
    group, size, _ = recv_ref.shape
    tiles, members, _ = centred_ref.shape
    count = members // group
    fill(pieces, obs_ref)
    parts = recv_ref[:, size - 32 :, :].astype(F32)
    for t in range(tiles):
        own = parts[:, 3 * t, :] + parts[:, 3 * t + 1, :] + parts[:, 3 * t + 2, :]
        delta = own - jnp.mean(own, axis=0, keepdims=True)
        local = recv_ref[:, t * count : (t + 1) * count, :].astype(F32)
        centred_ref[t] = (local + delta[:, None, :]).astype(BF16).reshape(members, TILE)


def analysis_kernel(anom_at_ref, weight_at_ref, tapers_ref, taper_ref, centred_ref, early_ref, *rest):
    pieces, (ret_ref, late_ref) = rest[:-2], rest[-2:]
    tiles, members, _ = centred_ref.shape
    group = ret_ref.shape[0]
    count = members // group
    early = early_ref.shape[1]
    fill(pieces, late_ref)

    def block(kind, at):
        near = early_ref[kind, jnp.minimum(at, early - 1)]
        far = late_ref[kind, jnp.maximum(at - early, 0)]
        return jnp.where(at < early, near, far)

    def one(t, carry):
        anoms, weights = [], []
        for k in range(SLOTS):
            anom = block(0, anom_at_ref[t, k])
            anoms.append(jnp.concatenate([anom[q * TILE : (q + 1) * TILE] for q in range(members // TILE)], axis=1))
            weights.append(block(1, weight_at_ref[t, k]))
        cov = jnp.dot(jnp.concatenate(anoms, axis=0), centred_ref[t], preferred_element_type=F32) * (1.0 / (members - 1.0))
        tapered = [
            (taper_ref[tapers_ref[t, k]] * cov[k * TILE : (k + 1) * TILE]).astype(BF16) for k in range(SLOTS)
        ]
        total = jnp.dot(jnp.concatenate(weights, axis=1), jnp.concatenate(tapered, axis=0), preferred_element_type=F32)
        here = pl.ds(pl.multiple_of(t * count, count), count)
        ret_ref[:, here, :] = total.astype(BF16).reshape(group, count, TILE)
        return carry

    lax.fori_loop(0, tiles, one, 0, unroll=3)


def final_kernel(prior_ref, inc_ref, coef_ref, out_ref, v_ref):
    members, depth, columns = out_ref.shape
    group, size, _ = inc_ref.shape
    rows = prior_ref.shape[0] - 2
    per = rows // group
    extra = size // members - 1
    i, steps = pl.program_id(0), pl.num_programs(0)

    def put(index, j, slot, half):
        lanes = slice(half * TILE, (half + 1) * TILE)
        here = pl.ds(pl.multiple_of(slot * members, members), members)
        v_ref[index, :, lanes] = prior_ref[i * depth + index, :, lanes] + inc_ref[j, here, :].astype(F32)

    first = i * (depth // per)
    for half in range(2):
        top, bottom = i == 0, i == steps - 1
        put(0, jnp.where(top, half, first - 1), jnp.where(top, extra, 2 * (per - 1) + half), half)
        put(depth + 1, jnp.where(bottom, 2 + half, first + depth // per), jnp.where(bottom, extra, half), half)
        for r in range(depth):
            put(r + 1, first + r // per, 2 * (r % per) + half, half)
    coef = coef_ref[...]
    for r in range(depth):
        mid = v_ref[r + 1]
        beside = v_ref[r] + v_ref[r + 2] + pltpu.roll(mid, 1, 1) + pltpu.roll(mid, columns - 1, 1)
        out_ref[:, r, :] = mid + coef[r : r + 1, :] * (beside - 4.0 * mid)


AXES = ("mem", "state")


def fetch(value, mesh, source):
    xs, ys, zs = mesh
    pairs = []
    for x in range(xs):
        for c in range(2):
            for y in range(ys):
                for z in range(zs):
                    a, b, d, e = source(x, c, y, z)
                    pairs.append((((a * 2 + b) * ys + d % ys) * zs + e % zs, ((x * 2 + c) * ys + y) * zs + z))
    return lax.ppermute(value, AXES, pairs)


def ring(first, step):
    return lambda x, c, y, z: (x, c, y + step, z) if (c == 0) == first else (x, c, y, z + step)


def other_core(x, c, y, z):
    return (x, 1 - c, y, z)


TOKEN = jax.ShapeDtypeStruct((8, TILE), F32)


def join(operands, name, after):
    count = len(operands)
    flat = [v for pair in operands for v in (pair if isinstance(pair, tuple) else (pair,))]

    def kernel(*refs):
        outs = refs[len(flat) + len(after) :]
        core = lax.rem(lax.axis_index("mem"), 2)
        halves = [[], []]
        at = 0
        for pair in operands:
            for i in range(2):
                halves[i].append((refs[at + i], 0) if isinstance(pair, tuple) else (refs[at], i))
            at += 2 if isinstance(pair, tuple) else 1
        for i in range(2):
            for a, (ref, block) in enumerate(halves[i]):
                outs[0][i * count + a] = ref[block]
                if i == 0:
                    outs[1][a] = ref[block]

            @pl.when(core == i)
            def _(i=i):
                for a, (ref, block) in enumerate(halves[i]):
                    outs[2][a] = ref[block]

    shapes = [(n, *flat[0].shape[1:]) for n in (2 * count, count, count)]
    return pl.pallas_call(
        kernel,
        out_shape=[jax.ShapeDtypeStruct(shape, BF16) for shape in shapes],
        in_specs=[VMEM] * len(flat) + [HBM] * len(after),
        out_specs=[VMEM] * len(shapes),
        compiler_params=pltpu.CompilerParams(vmem_limit_bytes=6 << 20),
        name=name,
    )(*flat, *after)


def join_two_kernel(own_ref, far_ref, held_ref, other_ref, token_ref):
    core = lax.rem(lax.axis_index("mem"), 2)
    held_ref[0] = own_ref[0]
    held_ref[1] = far_ref[0]

    @pl.when(core == 0)
    def _():
        other_ref[0] = far_ref[0]

    @pl.when(core == 1)
    def _():
        other_ref[0] = own_ref[0]


def gather_first(own, mesh):
    far = fetch(own, mesh, lambda x, c, y, z: (x, c, y, z + 4))
    return pl.pallas_call(
        join_two_kernel,
        out_shape=[jax.ShapeDtypeStruct((n, *own.shape[1:]), BF16) for n in (2, 1)] + [TOKEN],
        in_specs=[VMEM] * 2,
        out_specs=[VMEM] * 2 + [HBM],
        compiler_params=pltpu.CompilerParams(vmem_limit_bytes=6 << 20),
        name="join_two",
    )(own, far)


def gather_second(own, held, alternate, mesh, after):
    p, m = (fetch(held, mesh, ring(True, step)) for step in (1, -1))
    near = fetch(own, mesh, ring(True, 2))
    far = fetch(alternate, mesh, ring(True, -2))
    return join([held, p, m, (near, far)], "join_eight", after)


def gather_rest(held, first, second, mesh):
    p, m = (fetch(held, mesh, ring(False, step)) for step in (1, -1))
    q = fetch(first, mesh, ring(False, 2))
    r = fetch(second, mesh, ring(False, -2))
    own = [held, p, m, q, r]
    return own, [fetch(v, mesh, other_core) for v in own]


def places(block, y, z):
    dy, dz = (block // 8 - y) % 4, (block % 8 - z) % 8
    low = dz % 4
    gray_y, gray_z = dy ^ (dy >> 1), low ^ (low >> 1)
    high = 4 * ((dz // 4) ^ (low == 3).astype(jnp.int32))
    return 8 * gray_z + high + gray_y, 8 * gray_y + high + gray_z


def body(ensemble, spreading_coefficient, obs_anom, obs_weight, taper_table, obs_block, taper_id):
    members, rows, columns = ensemble.shape
    group = lax.axis_size("mem")
    states = lax.axis_size("state")
    per = rows // group
    tiles = 2 * per + 1
    size = tiles * members + 32

    j, at = lax.axis_index("mem"), lax.axis_index("state")
    chips = (group // 2, states // 8, 8)
    up, down, packed = pl.pallas_call(
        pack_kernel,
        grid=(1,),
        out_shape=[jax.ShapeDtypeStruct((HALO * members + 8, columns), F32)] * 2
        + [jax.ShapeDtypeStruct((1, obs_anom.shape[2], TILE), BF16)],
        in_specs=[
            pl.BlockSpec((members, 8, columns), lambda i: (0, 0, 0)),
            pl.BlockSpec((members, 8, columns), lambda i: (0, rows // 8 - 1, 0)),
            VMEM,
            SMEM,
            SMEM,
            VMEM,
            VMEM,
        ],
        out_specs=[VMEM] * 3,
        name="pack",
    )(ensemble, ensemble, spreading_coefficient, obs_block.T, taper_id.T, obs_anom, obs_weight)
    below = lax.ppermute(up, "state", [(i + 1, i) for i in range(states - 1)])
    above = lax.ppermute(down, "state", [(i, i + 1) for i in range(states - 1)])

    held, alternate, started = gather_first(packed, chips)
    row = (members, columns)
    prior, payload, edges, means, turned = pl.pallas_call(
        interior_kernel,
        out_shape=[
            jax.ShapeDtypeStruct((rows + 2, *row), F32),
            jax.ShapeDtypeStruct((group, size, TILE), BF16),
            jax.ShapeDtypeStruct((4 * FSTEPS, *row), F32),
            jax.ShapeDtypeStruct((group, 32, TILE), F32),
            jax.ShapeDtypeStruct(taper_table.shape, F32),
        ],
        in_specs=[VMEM] * 3 + [HBM],
        out_specs=[HBM] * 2 + [VMEM] * 3,
        scratch_shapes=[
            pltpu.VMEM((rows, *row), F32),
            pltpu.VMEM((rows, *row), F32),
            pltpu.VMEM((rows, 8, columns), F32),
            pltpu.VMEM((group, 2 * per * members, TILE), BF16),
            pltpu.SemaphoreType.DMA((group,)),
        ],
        compiler_params=pltpu.CompilerParams(vmem_limit_bytes=14 << 20),
        name="forecast_interior",
    )(ensemble, spreading_coefficient, taper_table, started)
    prior, payload, forecast_done = pl.pallas_call(
        edge_kernel,
        out_shape=[prior, payload, TOKEN],
        in_specs=[VMEM] * 5 + [HBM] * 2,
        out_specs=[HBM] * 3,
        input_output_aliases={5: 0, 6: 1},
        scratch_shapes=[
            pltpu.VMEM((2, HALO + FSTEPS, *row), F32),
            pltpu.VMEM((2, HALO + FSTEPS, *row), F32),
            pltpu.VMEM((2, HALO + FSTEPS, 8, columns), F32),
            pltpu.VMEM((group, size, TILE), BF16),
            pltpu.VMEM((group, 32, TILE), F32),
            pltpu.VMEM((2, HALO, *row), F32),
            pltpu.SemaphoreType.DMA((group + 2,)),
        ],
        compiler_params=pltpu.CompilerParams(vmem_limit_bytes=14 << 20),
        name="forecast_edges",
    )(above, below, spreading_coefficient, edges, means, prior, payload)
    held, first, second = gather_second(packed, held, alternate, chips, [forecast_done])
    own, swapped = gather_rest(held, first, second, chips)
    gathered = lax.all_to_all(payload, "mem", split_axis=0, concat_axis=0, tiled=True)

    edge = jnp.where(j < 2, above[-1, :16], below[-1, :16])
    edge = jnp.where(j % 2 == 0, edge.reshape(-1, 4)[:3:2], edge.reshape(-1, 4)[1:4:2]).astype(jnp.int32)
    mine = 2 * per * j
    blocks = jnp.concatenate([lax.dynamic_slice_in_dim(obs_block, mine, 2 * per, 0), edge[0:1]], axis=0)
    tapers = jnp.concatenate([lax.dynamic_slice_in_dim(taper_id, mine, 2 * per, 0), edge[1:2]], axis=0)

    anom_at, weight_at = places(blocks, at // 8, at % 8)
    late = 2
    early = own[:-late] + swapped[:-late]
    held_early, centred = pl.pallas_call(
        collect_kernel,
        out_shape=[
            jax.ShapeDtypeStruct((2, sum(v.shape[0] for v in own[:-late]), *packed.shape[1:]), BF16),
            jax.ShapeDtypeStruct((tiles, group * members, TILE), BF16),
        ],
        in_specs=[VMEM] * (1 + len(early)),
        out_specs=[VMEM] * 2,
        compiler_params=pltpu.CompilerParams(vmem_limit_bytes=18 << 20),
        name="collect",
    )(gathered, *early)
    increments = pl.pallas_call(
        analysis_kernel,
        out_shape=jax.ShapeDtypeStruct((group, tiles * members, TILE), BF16),
        in_specs=[SMEM] * 3 + [VMEM] * (3 + 2 * late),
        out_specs=VMEM,
        scratch_shapes=[pltpu.VMEM((2, sum(v.shape[0] for v in own[-late:]), *packed.shape[1:]), BF16)],
        compiler_params=pltpu.CompilerParams(vmem_limit_bytes=18 << 20),
        name="analysis",
    )(anom_at, weight_at, tapers, turned, centred, held_early, *own[-late:], *swapped[-late:])
    returned = lax.all_to_all(increments, "mem", split_axis=0, concat_axis=0, tiled=True)

    return pl.pallas_call(
        final_kernel,
        grid=(rows // 8,),
        out_shape=jax.ShapeDtypeStruct((members, rows, columns), F32),
        in_specs=[VMEM] * 2 + [pl.BlockSpec((8, columns), lambda i: (i, 0))],
        out_specs=pl.BlockSpec((members, 8, columns), lambda i: (0, i, 0)),
        scratch_shapes=[pltpu.VMEM((10, members, columns), F32)],
        compiler_params=pltpu.CompilerParams(vmem_limit_bytes=10 << 20),
        name="final_step",
    )(prior, returned, spreading_coefficient)


def solution(mesh):
    placed = (
        P("mem", "state", None),
        P("state", None),
        P("state", None, None),
        P("state", None, None),
        P(),
        P("state", None),
        P("state", None),
    )
    return jax.shard_map(
        body, mesh=mesh, in_specs=placed, out_specs=P("mem", "state", None), check_vma=False
    )
```

```python
import jax
import jax.numpy as jnp
from jax import lax
from jax.experimental import pallas as pl
from jax.experimental.pallas import tpu as pltpu
from jax.sharding import PartitionSpec as P

F32, BF16 = jnp.float32, jnp.bfloat16
TILE = 128
SLOTS = 4
FSTEPS = 4
HALO = FSTEPS + 1
VMEM = pl.BlockSpec(memory_space=pltpu.VMEM)
SMEM = pl.BlockSpec(memory_space=pltpu.SMEM)
HBM = pl.BlockSpec(memory_space=pltpu.HBM)


def pack_obs_kernel(anom_ref, weight_ref, out_ref, token_ref):
    members = anom_ref.shape[2]
    core = lax.rem(lax.axis_index("mem"), 2)

    @pl.when(core == 0)
    def _():
        for q in range(members // TILE):
            out_ref[0, q * TILE : (q + 1) * TILE, :] = anom_ref[0, :, q * TILE : (q + 1) * TILE]

    @pl.when(core == 1)
    def _():
        for q in range(members // TILE):
            out_ref[0, q * TILE : (q + 1) * TILE, :] = weight_ref[0, :, q * TILE : (q + 1) * TILE].T


def pack_halo_kernel(first_ref, last_ref, coef_ref, block_ref, taper_ref, after_ref, up_ref, down_ref, token_ref):
    members, depth, columns = first_ref.shape
    rows = coef_ref.shape[0]
    tiles = block_ref.shape[1]
    lane = lax.broadcasted_iota(jnp.int32, (8, columns), 1)
    for out_ref, x_ref, start, row0, tile0 in (
        (up_ref, first_ref, 0, 0, 0),
        (down_ref, last_ref, depth - HALO, rows - HALO, tiles - 2),
    ):
        for r in range(HALO):
            out_ref[r * members : (r + 1) * members, :] = x_ref[:, start + r, :]
        ids = jnp.zeros((8, columns), jnp.int32)
        for t in range(2):
            for k in range(SLOTS):
                ids = jnp.where(lane == t * SLOTS + k, block_ref[k, tile0 + t], ids)
                ids = jnp.where(lane == 8 + t * SLOTS + k, taper_ref[k, tile0 + t], ids)
        out_ref[HALO * members :, :] = ids.astype(F32)
        out_ref[HALO * members : HALO * members + HALO, :] = coef_ref[row0 : row0 + HALO, :]


def stepped(mid, one_side, other_side, coef):
    chunk, columns = mid.shape
    beside = one_side + other_side + pltpu.roll(mid, 1, 1) + pltpu.roll(mid, columns - 1, 1)
    delta = (beside - 4.0 * mid).reshape(chunk // 8, 8, columns)
    return mid + (coef[None] * delta).reshape(chunk, columns)


def split_tile(value, slot, members, pay_ref, mean_ref):
    mean = jnp.sum(value, axis=0, keepdims=True) * (1.0 / members)
    pay_ref[slot * members : (slot + 1) * members, :] = (value - mean).astype(BF16)
    high = mean.astype(BF16).astype(F32)
    middle = (mean - high).astype(BF16).astype(F32)
    mean_ref[3 * slot : 3 * slot + 1, :] = high
    mean_ref[3 * slot + 1 : 3 * slot + 2, :] = middle
    mean_ref[3 * slot + 2 : 3 * slot + 3, :] = mean - high - middle


def interior_kernel(x_ref, coef_ref, taper_ref, token_ref, prior_ref, out_ref, edge_ref, mean_ref, turned_ref, a_ref, b_ref, c_ref, pay_ref, sems):
    members, rows, columns = x_ref.shape
    group = out_ref.shape[0]
    per = rows // group
    for r in range(rows):
        c_ref[r] = jnp.broadcast_to(coef_ref[r : r + 1, :], (8, columns))
    chunk = 16

    def advance(number, carry):
        here = pl.ds(pl.multiple_of(number * chunk, chunk), chunk)
        for r in range(rows):
            a_ref[r, here, :] = x_ref[here, r, :]
        src, dst = a_ref, b_ref
        for step in range(1, FSTEPS + 1):
            done = step - 1
            for i, r in enumerate((done, done + 1, rows - 1 - done, rows - 2 - done)):
                edge_ref[4 * done + i, here, :] = src[r, here, :]
            for r in range(step, rows - step):
                dst[r, here, :] = stepped(src[r, here, :], src[r - 1, here, :], src[r + 1, here, :], c_ref[r])
            src, dst = dst, src
        return carry

    lax.fori_loop(0, members // chunk, advance, 0)
    src = a_ref if FSTEPS % 2 == 0 else b_ref
    inner = rows - 2 * FSTEPS
    copies = [pltpu.make_async_copy(src.at[pl.ds(FSTEPS, inner)], prior_ref.at[pl.ds(FSTEPS + 1, inner)], sems.at[0])]
    copies[0].start()
    mean_ref[...] = jnp.zeros_like(mean_ref)
    for j in range(1, group - 1):
        for i in range(per):
            for half in range(2):
                value = src[j * per + i, :, half * TILE : (half + 1) * TILE]
                split_tile(value, 2 * i + half, members, pay_ref.at[j], mean_ref.at[j])
        copies.append(pltpu.make_async_copy(pay_ref.at[j], out_ref.at[j, pl.ds(0, 2 * per * members)], sems.at[j]))
        copies[-1].start()
    for i in range(taper_ref.shape[0]):
        turned_ref[i] = taper_ref[i].T
    for copy in copies:
        copy.wait()


def edge_kernel(above_ref, below_ref, coef_ref, edge_ref, mean_ref, prior_in, pay_in, prior_ref, out_ref, token_ref, a_ref, b_ref, c_ref, pay_ref, m_ref, last_ref, sems):
    rows, columns = coef_ref.shape
    members = last_ref.shape[2]
    group, size, _ = out_ref.shape
    per = rows // group
    tiles = 2 * per + 1
    halos = (above_ref, below_ref)
    for side in range(2):
        for t in range(HALO + FSTEPS):
            if t < HALO:
                r = HALO * members + (t if side == 0 else HALO - 1 - t)
                row = halos[side][r : r + 1, :]
            else:
                r = t - HALO if side == 0 else rows - 1 - (t - HALO)
                row = coef_ref[r : r + 1, :]
            c_ref[side, t] = jnp.broadcast_to(row, (8, columns))
    chunk = 16

    def advance(number, carry):
        here = pl.ds(pl.multiple_of(number * chunk, chunk), chunk)
        for side in range(2):

            def value(step, t, side=side):
                if t > step + HALO - 1:
                    return edge_ref[4 * step + 2 * side + t - step - HALO, here, :]
                if step == 0:
                    r = t if side == 0 else HALO - 1 - t
                    return halos[side][pl.ds(pl.multiple_of(r * members + number * chunk, chunk), chunk), :]
                return (a_ref, b_ref)[step % 2][side, t, here, :]

            for step in range(1, FSTEPS + 1):
                for t in range(step, step + HALO):
                    new = stepped(value(step - 1, t), value(step - 1, t - 1), value(step - 1, t + 1), c_ref[side, t])
                    if step < FSTEPS:
                        (a_ref, b_ref)[step % 2][side, t, here, :] = new
                    else:
                        last_ref[side, t - FSTEPS if side == 0 else 2 * FSTEPS - t, here, :] = new
        return carry

    lax.fori_loop(0, members // chunk, advance, 0)
    copies = [
        pltpu.make_async_copy(last_ref.at[0], prior_ref.at[pl.ds(0, HALO)], sems.at[0]),
        pltpu.make_async_copy(last_ref.at[1], prior_ref.at[pl.ds(rows + 2 - HALO, HALO)], sems.at[1]),
    ]
    for copy in copies:
        copy.start()
    m_ref[...] = mean_ref[...]
    extra = tiles - 1
    for j in range(group):
        if j in (0, group - 1):
            for i in range(per):
                for half in range(2):
                    row = last_ref[0, i + 1] if j == 0 else last_ref[1, i]
                    split_tile(row[:, half * TILE : (half + 1) * TILE], 2 * i + half, members, pay_ref.at[j], m_ref.at[j])
        if j < 4:
            row = last_ref[0, 0] if j < 2 else last_ref[1, HALO - 1]
            split_tile(row[:, (j % 2) * TILE : (j % 2 + 1) * TILE], extra, members, pay_ref.at[j], m_ref.at[j])
        else:
            pay_ref[j, extra * members : tiles * members, :] = jnp.zeros((members, TILE), BF16)
        pay_ref[j, tiles * members :, :] = m_ref[j].astype(BF16)
        first = 0 if j in (0, group - 1) else extra * members
        part = pl.ds(first, size - first)
        copies.append(pltpu.make_async_copy(pay_ref.at[j, part], out_ref.at[j, part], sems.at[2 + j]))
        copies[-1].start()
    for copy in copies:
        copy.wait()


def fill(pieces, obs_ref):
    core = lax.rem(lax.axis_index("mem"), 2)
    for side in range(2):
        start = 0
        kind = core if side == 0 else 1 - core
        for piece in pieces[side * len(pieces) // 2 : (side + 1) * len(pieces) // 2]:

            def keep(i, carry, piece=piece, start=start, kind=kind):
                obs_ref[kind, start + i] = piece[i]
                return carry

            lax.fori_loop(0, piece.shape[0], keep, 0)
            start += piece.shape[0]


def collect_kernel(recv_ref, *rest):
    pieces, (obs_ref, centred_ref) = rest[:-2], rest[-2:]
    group, size, _ = recv_ref.shape
    tiles, members, _ = centred_ref.shape
    count = members // group
    fill(pieces, obs_ref)
    parts = recv_ref[:, size - 32 :, :].astype(F32)
    for t in range(tiles):
        own = parts[:, 3 * t, :] + parts[:, 3 * t + 1, :] + parts[:, 3 * t + 2, :]
        delta = own - jnp.mean(own, axis=0, keepdims=True)
        local = recv_ref[:, t * count : (t + 1) * count, :].astype(F32)
        centred_ref[t] = (local + delta[:, None, :]).astype(BF16).reshape(members, TILE)


def analysis_kernel(anom_at_ref, weight_at_ref, tapers_ref, taper_ref, centred_ref, early_ref, *rest):
    pieces, (ret_ref, late_ref) = rest[:-2], rest[-2:]
    tiles, members, _ = centred_ref.shape
    group = ret_ref.shape[0]
    count = members // group
    early = early_ref.shape[1]
    fill(pieces, late_ref)

    def block(kind, at):
        near = early_ref[kind, jnp.minimum(at, early - 1)]
        far = late_ref[kind, jnp.maximum(at - early, 0)]
        return jnp.where(at < early, near, far)

    def one(t, carry):
        anoms, weights = [], []
        for k in range(SLOTS):
            anom = block(0, anom_at_ref[t, k])
            anoms.append(jnp.concatenate([anom[q * TILE : (q + 1) * TILE] for q in range(members // TILE)], axis=1))
            weights.append(block(1, weight_at_ref[t, k]))
        cov = jnp.dot(jnp.concatenate(anoms, axis=0), centred_ref[t], preferred_element_type=F32) * (1.0 / (members - 1.0))
        tapered = [
            (taper_ref[tapers_ref[t, k]] * cov[k * TILE : (k + 1) * TILE]).astype(BF16) for k in range(SLOTS)
        ]
        total = jnp.dot(jnp.concatenate(weights, axis=1), jnp.concatenate(tapered, axis=0), preferred_element_type=F32)
        here = pl.ds(pl.multiple_of(t * count, count), count)
        ret_ref[:, here, :] = total.astype(BF16).reshape(group, count, TILE)
        return carry

    lax.fori_loop(0, tiles, one, 0, unroll=3)


def final_kernel(prior_ref, inc_ref, coef_ref, out_ref, v_ref):
    members, depth, columns = out_ref.shape
    group, size, _ = inc_ref.shape
    rows = prior_ref.shape[0] - 2
    per = rows // group
    extra = size // members - 1
    i, steps = pl.program_id(0), pl.num_programs(0)

    def put(index, j, slot, half):
        lanes = slice(half * TILE, (half + 1) * TILE)
        here = pl.ds(pl.multiple_of(slot * members, members), members)
        v_ref[index, :, lanes] = prior_ref[i * depth + index, :, lanes] + inc_ref[j, here, :].astype(F32)

    first = i * (depth // per)
    for half in range(2):
        top, bottom = i == 0, i == steps - 1
        put(0, jnp.where(top, half, first - 1), jnp.where(top, extra, 2 * (per - 1) + half), half)
        put(depth + 1, jnp.where(bottom, 2 + half, first + depth // per), jnp.where(bottom, extra, half), half)
        for r in range(depth):
            put(r + 1, first + r // per, 2 * (r % per) + half, half)
    coef = coef_ref[...]
    for r in range(depth):
        mid = v_ref[r + 1]
        beside = v_ref[r] + v_ref[r + 2] + pltpu.roll(mid, 1, 1) + pltpu.roll(mid, columns - 1, 1)
        out_ref[:, r, :] = mid + coef[r : r + 1, :] * (beside - 4.0 * mid)


AXES = ("mem", "state")


def fetch(value, mesh, source):
    xs, ys, zs = mesh
    pairs = []
    for x in range(xs):
        for c in range(2):
            for y in range(ys):
                for z in range(zs):
                    a, b, d, e = source(x, c, y, z)
                    pairs.append((((a * 2 + b) * ys + d % ys) * zs + e % zs, ((x * 2 + c) * ys + y) * zs + z))
    return lax.ppermute(value, AXES, pairs)


def ring(first, step):
    return lambda x, c, y, z: (x, c, y + step, z) if (c == 0) == first else (x, c, y, z + step)


def other_core(x, c, y, z):
    return (x, 1 - c, y, z)


TOKEN = jax.ShapeDtypeStruct((8, TILE), F32)


def join(operands, name, after):
    count = len(operands)

    def kernel(*refs):
        outs = refs[count + len(after) :]
        core = lax.rem(lax.axis_index("mem"), 2)
        for a in range(count):
            for i in range(2):
                outs[0][i * count + a] = refs[a][i]
            outs[1][a] = refs[a][0]
            outs[2][a] = refs[a][core]

    shapes = [(n, *operands[0].shape[1:]) for n in (2 * count, count, count)]
    return pl.pallas_call(
        kernel,
        out_shape=[jax.ShapeDtypeStruct(shape, BF16) for shape in shapes],
        in_specs=[VMEM] * count + [HBM] * len(after),
        out_specs=[VMEM] * len(shapes),
        compiler_params=pltpu.CompilerParams(vmem_limit_bytes=6 << 20),
        name=name,
    )(*operands, *after)


def join_two_kernel(own_ref, far_ref, after_ref, held_ref, token_ref):
    held_ref[0] = own_ref[0]
    held_ref[1] = far_ref[0]


def gather_first(own, mesh, after):
    far = fetch(own, mesh, lambda x, c, y, z: (x, c, y, z + 4))
    return pl.pallas_call(
        join_two_kernel,
        out_shape=[jax.ShapeDtypeStruct((2, *own.shape[1:]), BF16), TOKEN],
        in_specs=[VMEM] * 2 + [HBM],
        out_specs=[VMEM, HBM],
        compiler_params=pltpu.CompilerParams(vmem_limit_bytes=6 << 20),
        name="join_two",
    )(own, far, after)


def gather_second(held, mesh, after):
    p, m, q = (fetch(held, mesh, ring(True, step)) for step in (1, -1, 2))
    return join([held, p, m, q], "join_eight", after)


def gather_rest(held, first, second, mesh):
    p, m = (fetch(held, mesh, ring(False, step)) for step in (1, -1))
    q = fetch(first, mesh, ring(False, 2))
    r = fetch(second, mesh, ring(False, -2))
    own = [held, p, m, q, r]
    return own, [fetch(v, mesh, other_core) for v in own]


def places(block, y, z):
    dy, dz = (block // 8 - y) % 4, (block % 8 - z) % 8
    low = dz % 4
    gray_y, gray_z = dy ^ (dy >> 1), low ^ (low >> 1)
    high = 4 * ((dz // 4) ^ (low == 3).astype(jnp.int32))
    return 8 * gray_z + high + gray_y, 8 * gray_y + high + gray_z


def body(ensemble, spreading_coefficient, obs_anom, obs_weight, taper_table, obs_block, taper_id):
    members, rows, columns = ensemble.shape
    group = lax.axis_size("mem")
    states = lax.axis_size("state")
    per = rows // group
    tiles = 2 * per + 1
    size = tiles * members + 32

    j, at = lax.axis_index("mem"), lax.axis_index("state")
    chips = (group // 2, states // 8, 8)
    packed, obs_packed = pl.pallas_call(
        pack_obs_kernel,
        out_shape=[jax.ShapeDtypeStruct((1, obs_anom.shape[2], TILE), BF16), TOKEN],
        in_specs=[VMEM] * 2,
        out_specs=[VMEM, HBM],
        compiler_params=pltpu.CompilerParams(vmem_limit_bytes=6 << 20),
        name="pack_obs",
    )(obs_anom, obs_weight)
    up, down, halo_packed = pl.pallas_call(
        pack_halo_kernel,
        grid=(1,),
        out_shape=[jax.ShapeDtypeStruct((HALO * members + 8, columns), F32)] * 2 + [TOKEN],
        in_specs=[
            pl.BlockSpec((members, 8, columns), lambda i: (0, 0, 0)),
            pl.BlockSpec((members, 8, columns), lambda i: (0, rows // 8 - 1, 0)),
            VMEM,
            SMEM,
            SMEM,
            HBM,
        ],
        out_specs=[VMEM] * 2 + [HBM],
        name="pack_halo",
    )(ensemble, ensemble, spreading_coefficient, obs_block.T, taper_id.T, obs_packed)
    below = lax.ppermute(up, "state", [(i + 1, i) for i in range(states - 1)])
    above = lax.ppermute(down, "state", [(i, i + 1) for i in range(states - 1)])

    held, started = gather_first(packed, chips, halo_packed)
    row = (members, columns)
    prior, payload, edges, means, turned = pl.pallas_call(
        interior_kernel,
        out_shape=[
            pltpu.HBM((rows + 2, *row), F32),
            pltpu.HBM((group, size, TILE), BF16),
            jax.ShapeDtypeStruct((4 * FSTEPS, *row), F32),
            jax.ShapeDtypeStruct((group, 32, TILE), F32),
            jax.ShapeDtypeStruct(taper_table.shape, F32),
        ],
        in_specs=[VMEM] * 3 + [HBM],
        out_specs=[HBM] * 2 + [VMEM] * 3,
        scratch_shapes=[
            pltpu.VMEM((rows, *row), F32),
            pltpu.VMEM((rows, *row), F32),
            pltpu.VMEM((rows, 8, columns), F32),
            pltpu.VMEM((group, 2 * per * members, TILE), BF16),
            pltpu.SemaphoreType.DMA((group,)),
        ],
        compiler_params=pltpu.CompilerParams(vmem_limit_bytes=14 << 20),
        name="forecast_interior",
    )(ensemble, spreading_coefficient, taper_table, started)
    prior, payload, forecast_done = pl.pallas_call(
        edge_kernel,
        out_shape=[pltpu.HBM(prior.shape, F32), pltpu.HBM(payload.shape, BF16), TOKEN],
        in_specs=[VMEM] * 5 + [HBM] * 2,
        out_specs=[HBM] * 3,
        input_output_aliases={5: 0, 6: 1},
        scratch_shapes=[
            pltpu.VMEM((2, HALO + FSTEPS, *row), F32),
            pltpu.VMEM((2, HALO + FSTEPS, *row), F32),
            pltpu.VMEM((2, HALO + FSTEPS, 8, columns), F32),
            pltpu.VMEM((group, size, TILE), BF16),
            pltpu.VMEM((group, 32, TILE), F32),
            pltpu.VMEM((2, HALO, *row), F32),
            pltpu.SemaphoreType.DMA((group + 2,)),
        ],
        compiler_params=pltpu.CompilerParams(vmem_limit_bytes=14 << 20),
        name="forecast_edges",
    )(above, below, spreading_coefficient, edges, means, prior, payload)
    held, first, second = gather_second(held, chips, [forecast_done])
    own, swapped = gather_rest(held, first, second, chips)
    gathered = lax.all_to_all(payload, "mem", split_axis=0, concat_axis=0, tiled=True)

    edge = jnp.where(j < 2, above[-1, :16], below[-1, :16])
    edge = jnp.where(j % 2 == 0, edge.reshape(-1, 4)[:3:2], edge.reshape(-1, 4)[1:4:2]).astype(jnp.int32)
    mine = 2 * per * j
    blocks = jnp.concatenate([lax.dynamic_slice_in_dim(obs_block, mine, 2 * per, 0), edge[0:1]], axis=0)
    tapers = jnp.concatenate([lax.dynamic_slice_in_dim(taper_id, mine, 2 * per, 0), edge[1:2]], axis=0)

    anom_at, weight_at = places(blocks, at // 8, at % 8)
    late = 2
    early = own[:-late] + swapped[:-late]
    held_early, centred = pl.pallas_call(
        collect_kernel,
        out_shape=[
            jax.ShapeDtypeStruct((2, sum(v.shape[0] for v in own[:-late]), *packed.shape[1:]), BF16),
            jax.ShapeDtypeStruct((tiles, group * members, TILE), BF16),
        ],
        in_specs=[VMEM] * (1 + len(early)),
        out_specs=[VMEM] * 2,
        compiler_params=pltpu.CompilerParams(vmem_limit_bytes=18 << 20),
        name="collect",
    )(gathered, *early)
    increments = pl.pallas_call(
        analysis_kernel,
        out_shape=jax.ShapeDtypeStruct((group, tiles * members, TILE), BF16),
        in_specs=[SMEM] * 3 + [VMEM] * (3 + 2 * late),
        out_specs=VMEM,
        scratch_shapes=[pltpu.VMEM((2, sum(v.shape[0] for v in own[-late:]), *packed.shape[1:]), BF16)],
        compiler_params=pltpu.CompilerParams(vmem_limit_bytes=18 << 20),
        name="analysis",
    )(anom_at, weight_at, tapers, turned, centred, held_early, *own[-late:], *swapped[-late:])
    returned = lax.all_to_all(increments, "mem", split_axis=0, concat_axis=0, tiled=True)

    return pl.pallas_call(
        final_kernel,
        grid=(rows // 8,),
        out_shape=jax.ShapeDtypeStruct((members, rows, columns), F32),
        in_specs=[VMEM] * 2 + [pl.BlockSpec((8, columns), lambda i: (i, 0))],
        out_specs=pl.BlockSpec((members, 8, columns), lambda i: (0, i, 0)),
        scratch_shapes=[pltpu.VMEM((10, members, columns), F32)],
        compiler_params=pltpu.CompilerParams(vmem_limit_bytes=10 << 20),
        name="final_step",
    )(prior, returned, spreading_coefficient)


def solution(mesh):
    placed = (
        P("mem", "state", None),
        P("state", None),
        P("state", None, None),
        P("state", None, None),
        P(),
        P("state", None),
        P("state", None),
    )
    return jax.shard_map(
        body, mesh=mesh, in_specs=placed, out_specs=P("mem", "state", None), check_vma=False
    )
```

```python
import jax
import jax.numpy as jnp
from jax import lax
from jax.experimental import pallas as pl
from jax.experimental.pallas import tpu as pltpu
from jax.sharding import PartitionSpec as P

F32, BF16 = jnp.float32, jnp.bfloat16
TILE = 128
SLOTS = 4
FSTEPS = 4
HALO = FSTEPS + 1
VMEM = pl.BlockSpec(memory_space=pltpu.VMEM)
SMEM = pl.BlockSpec(memory_space=pltpu.SMEM)
HBM = pl.BlockSpec(memory_space=pltpu.HBM)


def pack_obs_kernel(anom_ref, weight_ref, out_ref, token_ref, held_ref, sem):
    members = anom_ref.shape[2]
    core = lax.rem(lax.axis_index("mem"), 2)
    for kind, ref in enumerate((anom_ref, weight_ref)):

        @pl.when(core == kind)
        def _(kind=kind, ref=ref):
            copy = pltpu.make_async_copy(ref.at[0], held_ref, sem.at[kind])
            copy.start()
            copy.wait()
            for q in range(members // TILE):
                part = held_ref[:, q * TILE : (q + 1) * TILE]
                out_ref[0, q * TILE : (q + 1) * TILE, :] = part if kind == 0 else part.T


def pack_halo_kernel(first_ref, last_ref, coef_ref, block_ref, taper_ref, after_ref, up_ref, down_ref):
    members, depth, columns = first_ref.shape
    rows = coef_ref.shape[0]
    tiles = block_ref.shape[1]
    lane = lax.broadcasted_iota(jnp.int32, (8, columns), 1)
    for out_ref, x_ref, start, row0, tile0 in (
        (up_ref, first_ref, 0, 0, 0),
        (down_ref, last_ref, depth - HALO, rows - HALO, tiles - 2),
    ):
        for r in range(HALO):
            out_ref[r * members : (r + 1) * members, :] = x_ref[:, start + r, :]
        ids = jnp.zeros((8, columns), jnp.int32)
        for t in range(2):
            for k in range(SLOTS):
                ids = jnp.where(lane == t * SLOTS + k, block_ref[k, tile0 + t], ids)
                ids = jnp.where(lane == 8 + t * SLOTS + k, taper_ref[k, tile0 + t], ids)
        out_ref[HALO * members :, :] = ids.astype(F32)
        out_ref[HALO * members : HALO * members + HALO, :] = coef_ref[row0 : row0 + HALO, :]


def stepped(mid, one_side, other_side, coef):
    chunk, columns = mid.shape
    beside = one_side + other_side + pltpu.roll(mid, 1, 1) + pltpu.roll(mid, columns - 1, 1)
    delta = (beside - 4.0 * mid).reshape(chunk // 8, 8, columns)
    return mid + (coef[None] * delta).reshape(chunk, columns)


def split_tile(value, slot, members, pay_ref, mean_ref):
    mean = jnp.sum(value, axis=0, keepdims=True) * (1.0 / members)
    pay_ref[slot * members : (slot + 1) * members, :] = (value - mean).astype(BF16)
    high = mean.astype(BF16).astype(F32)
    middle = (mean - high).astype(BF16).astype(F32)
    mean_ref[3 * slot : 3 * slot + 1, :] = high
    mean_ref[3 * slot + 1 : 3 * slot + 2, :] = middle
    mean_ref[3 * slot + 2 : 3 * slot + 3, :] = mean - high - middle


def interior_kernel(x_ref, coef_ref, taper_ref, token_ref, prior_ref, out_ref, edge_ref, mean_ref, turned_out, a_ref, b_ref, c_ref, pay_ref, turned_ref, sems):
    members, rows, columns = x_ref.shape
    group = out_ref.shape[0]
    per = rows // group
    for r in range(rows):
        c_ref[r] = jnp.broadcast_to(coef_ref[r : r + 1, :], (8, columns))
    chunk = 16

    def advance(number, carry):
        here = pl.ds(pl.multiple_of(number * chunk, chunk), chunk)
        for r in range(rows):
            a_ref[r, here, :] = x_ref[here, r, :]
        src, dst = a_ref, b_ref
        for step in range(1, FSTEPS + 1):
            done = step - 1
            for i, r in enumerate((done, done + 1, rows - 1 - done, rows - 2 - done)):
                edge_ref[4 * done + i, here, :] = src[r, here, :]
            for r in range(step, rows - step):
                dst[r, here, :] = stepped(src[r, here, :], src[r - 1, here, :], src[r + 1, here, :], c_ref[r])
            src, dst = dst, src
        return carry

    lax.fori_loop(0, members // chunk, advance, 0)
    src = a_ref if FSTEPS % 2 == 0 else b_ref
    inner = rows - 2 * FSTEPS
    copies = [pltpu.make_async_copy(src.at[pl.ds(FSTEPS, inner)], prior_ref.at[pl.ds(FSTEPS + 1, inner)], sems.at[0])]
    copies[0].start()
    mean_ref[...] = jnp.zeros_like(mean_ref)
    for j in range(1, group - 1):
        for i in range(per):
            for half in range(2):
                value = src[j * per + i, :, half * TILE : (half + 1) * TILE]
                split_tile(value, 2 * i + half, members, pay_ref.at[j], mean_ref.at[j])
        copies.append(pltpu.make_async_copy(pay_ref.at[j], out_ref.at[j, pl.ds(0, 2 * per * members)], sems.at[j]))
        copies[-1].start()
    for i in range(taper_ref.shape[0]):
        turned_ref[i] = taper_ref[i].T
    copies.append(pltpu.make_async_copy(turned_ref, turned_out, sems.at[group]))
    copies[-1].start()
    for copy in copies:
        copy.wait()


def edge_kernel(above_ref, below_ref, coef_ref, edge_ref, mean_ref, prior_in, pay_in, prior_ref, out_ref, token_ref, a_ref, b_ref, c_ref, pay_ref, m_ref, last_ref, sems):
    rows, columns = coef_ref.shape
    members = last_ref.shape[2]
    group, size, _ = out_ref.shape
    per = rows // group
    tiles = 2 * per + 1
    halos = (above_ref, below_ref)
    for side in range(2):
        for t in range(HALO + FSTEPS):
            if t < HALO:
                r = HALO * members + (t if side == 0 else HALO - 1 - t)
                row = halos[side][r : r + 1, :]
            else:
                r = t - HALO if side == 0 else rows - 1 - (t - HALO)
                row = coef_ref[r : r + 1, :]
            c_ref[side, t] = jnp.broadcast_to(row, (8, columns))
    chunk = 16

    def advance(number, carry):
        here = pl.ds(pl.multiple_of(number * chunk, chunk), chunk)
        for side in range(2):

            def value(step, t, side=side):
                if t > step + HALO - 1:
                    return edge_ref[4 * step + 2 * side + t - step - HALO, here, :]
                if step == 0:
                    r = t if side == 0 else HALO - 1 - t
                    return halos[side][pl.ds(pl.multiple_of(r * members + number * chunk, chunk), chunk), :]
                return (a_ref, b_ref)[step % 2][side, t, here, :]

            for step in range(1, FSTEPS + 1):
                for t in range(step, step + HALO):
                    new = stepped(value(step - 1, t), value(step - 1, t - 1), value(step - 1, t + 1), c_ref[side, t])
                    if step < FSTEPS:
                        (a_ref, b_ref)[step % 2][side, t, here, :] = new
                    else:
                        last_ref[side, t - FSTEPS if side == 0 else 2 * FSTEPS - t, here, :] = new
        return carry

    lax.fori_loop(0, members // chunk, advance, 0)
    copies = [
        pltpu.make_async_copy(last_ref.at[0], prior_ref.at[pl.ds(0, HALO)], sems.at[0]),
        pltpu.make_async_copy(last_ref.at[1], prior_ref.at[pl.ds(rows + 2 - HALO, HALO)], sems.at[1]),
    ]
    for copy in copies:
        copy.start()
    m_ref[...] = mean_ref[...]
    extra = tiles - 1
    for j in range(group):
        if j in (0, group - 1):
            for i in range(per):
                for half in range(2):
                    row = last_ref[0, i + 1] if j == 0 else last_ref[1, i]
                    split_tile(row[:, half * TILE : (half + 1) * TILE], 2 * i + half, members, pay_ref.at[j], m_ref.at[j])
        if j < 4:
            row = last_ref[0, 0] if j < 2 else last_ref[1, HALO - 1]
            split_tile(row[:, (j % 2) * TILE : (j % 2 + 1) * TILE], extra, members, pay_ref.at[j], m_ref.at[j])
        else:
            pay_ref[j, extra * members : tiles * members, :] = jnp.zeros((members, TILE), BF16)
        pay_ref[j, tiles * members :, :] = m_ref[j].astype(BF16)
        first = 0 if j in (0, group - 1) else extra * members
        part = pl.ds(first, size - first)
        copies.append(pltpu.make_async_copy(pay_ref.at[j, part], out_ref.at[j, part], sems.at[2 + j]))
        copies[-1].start()
    for copy in copies:
        copy.wait()


def fill(pieces, obs_ref):
    core = lax.rem(lax.axis_index("mem"), 2)
    for side in range(2):
        start = 0
        kind = core if side == 0 else 1 - core
        for piece in pieces[side * len(pieces) // 2 : (side + 1) * len(pieces) // 2]:

            def keep(i, carry, piece=piece, start=start, kind=kind):
                obs_ref[kind, start + i] = piece[i]
                return carry

            lax.fori_loop(0, piece.shape[0], keep, 0)
            start += piece.shape[0]


def collect_kernel(recv_ref, *rest):
    pieces, (obs_ref, centred_ref) = rest[:-2], rest[-2:]
    group, size, _ = recv_ref.shape
    tiles, members, _ = centred_ref.shape
    count = members // group
    fill(pieces, obs_ref)
    parts = recv_ref[:, size - 32 :, :].astype(F32)
    for t in range(tiles):
        own = parts[:, 3 * t, :] + parts[:, 3 * t + 1, :] + parts[:, 3 * t + 2, :]
        delta = own - jnp.mean(own, axis=0, keepdims=True)
        local = recv_ref[:, t * count : (t + 1) * count, :].astype(F32)
        centred_ref[t] = (local + delta[:, None, :]).astype(BF16).reshape(members, TILE)


def analysis_kernel(anom_at_ref, weight_at_ref, tapers_ref, taper_ref, centred_ref, early_ref, *rest):
    pieces, (ret_ref, late_ref) = rest[:-2], rest[-2:]
    tiles, members, _ = centred_ref.shape
    group = ret_ref.shape[0]
    count = members // group
    early = early_ref.shape[1]
    fill(pieces, late_ref)

    def block(kind, at):
        near = early_ref[kind, jnp.minimum(at, early - 1)]
        far = late_ref[kind, jnp.maximum(at - early, 0)]
        return jnp.where(at < early, near, far)

    def one(t, carry):
        anoms, weights = [], []
        for k in range(SLOTS):
            anom = block(0, anom_at_ref[t, k])
            anoms.append(jnp.concatenate([anom[q * TILE : (q + 1) * TILE] for q in range(members // TILE)], axis=1))
            weights.append(block(1, weight_at_ref[t, k]))
        cov = jnp.dot(jnp.concatenate(anoms, axis=0), centred_ref[t], preferred_element_type=F32) * (1.0 / (members - 1.0))
        tapered = [
            (taper_ref[tapers_ref[t, k]] * cov[k * TILE : (k + 1) * TILE]).astype(BF16) for k in range(SLOTS)
        ]
        total = jnp.dot(jnp.concatenate(weights, axis=1), jnp.concatenate(tapered, axis=0), preferred_element_type=F32)
        here = pl.ds(pl.multiple_of(t * count, count), count)
        ret_ref[:, here, :] = total.astype(BF16).reshape(group, count, TILE)
        return carry

    lax.fori_loop(0, tiles, one, 0, unroll=3)


def final_kernel(prior_ref, inc_ref, coef_ref, out_ref, v_ref):
    members, depth, columns = out_ref.shape
    group, size, _ = inc_ref.shape
    rows = prior_ref.shape[0] - 2
    per = rows // group
    extra = size // members - 1
    i, steps = pl.program_id(0), pl.num_programs(0)

    def put(index, j, slot, half):
        lanes = slice(half * TILE, (half + 1) * TILE)
        here = pl.ds(pl.multiple_of(slot * members, members), members)
        v_ref[index, :, lanes] = prior_ref[i * depth + index, :, lanes] + inc_ref[j, here, :].astype(F32)

    first = i * (depth // per)
    for half in range(2):
        top, bottom = i == 0, i == steps - 1
        put(0, jnp.where(top, half, first - 1), jnp.where(top, extra, 2 * (per - 1) + half), half)
        put(depth + 1, jnp.where(bottom, 2 + half, first + depth // per), jnp.where(bottom, extra, half), half)
        for r in range(depth):
            put(r + 1, first + r // per, 2 * (r % per) + half, half)
    coef = coef_ref[...]
    for r in range(depth):
        mid = v_ref[r + 1]
        beside = v_ref[r] + v_ref[r + 2] + pltpu.roll(mid, 1, 1) + pltpu.roll(mid, columns - 1, 1)
        out_ref[:, r, :] = mid + coef[r : r + 1, :] * (beside - 4.0 * mid)


AXES = ("mem", "state")


def fetch(value, mesh, source):
    xs, ys, zs = mesh
    pairs = []
    for x in range(xs):
        for c in range(2):
            for y in range(ys):
                for z in range(zs):
                    a, b, d, e = source(x, c, y, z)
                    pairs.append((((a * 2 + b) * ys + d % ys) * zs + e % zs, ((x * 2 + c) * ys + y) * zs + z))
    return lax.ppermute(value, AXES, pairs)


def ring(first, step):
    return lambda x, c, y, z: (x, c, y + step, z) if (c == 0) == first else (x, c, y, z + step)


def other_core(x, c, y, z):
    return (x, 1 - c, y, z)


TOKEN = pltpu.HBM((8, TILE), F32)


def join(operands, name, after):
    count = len(operands)

    def kernel(*refs):
        outs = refs[count + len(after) :]
        core = lax.rem(lax.axis_index("mem"), 2)
        for a in range(count):
            for i in range(2):
                outs[0][i * count + a] = refs[a][i]
            outs[1][a] = refs[a][0]
            outs[2][a] = refs[a][core]

    shapes = [(n, *operands[0].shape[1:]) for n in (2 * count, count, count)]
    return pl.pallas_call(
        kernel,
        out_shape=[jax.ShapeDtypeStruct(shape, BF16) for shape in shapes],
        in_specs=[VMEM] * count + [HBM] * len(after),
        out_specs=[VMEM] * len(shapes),
        compiler_params=pltpu.CompilerParams(vmem_limit_bytes=6 << 20),
        name=name,
    )(*operands, *after)


def join_two_kernel(own_ref, far_ref, held_ref, token_ref):
    held_ref[0] = own_ref[0]
    held_ref[1] = far_ref[0]


def gather_first(own, mesh):
    far = fetch(own, mesh, lambda x, c, y, z: (x, c, y, z + 4))
    return pl.pallas_call(
        join_two_kernel,
        out_shape=[jax.ShapeDtypeStruct((2, *own.shape[1:]), BF16), TOKEN],
        in_specs=[VMEM] * 2,
        out_specs=[VMEM, HBM],
        compiler_params=pltpu.CompilerParams(vmem_limit_bytes=6 << 20),
        name="join_two",
    )(own, far)


def gather_second(held, mesh, after):
    p, m, q = (fetch(held, mesh, ring(True, step)) for step in (1, -1, 2))
    return join([held, p, m, q], "join_eight", after)


def gather_rest(held, first, second, mesh):
    p, m = (fetch(held, mesh, ring(False, step)) for step in (1, -1))
    q = fetch(first, mesh, ring(False, 2))
    r = fetch(second, mesh, ring(False, -2))
    own = [held, p, m, q, r]
    return own, [fetch(v, mesh, other_core) for v in own]


def places(block, y, z):
    dy, dz = (block // 8 - y) % 4, (block % 8 - z) % 8
    low = dz % 4
    gray_y, gray_z = dy ^ (dy >> 1), low ^ (low >> 1)
    high = 4 * ((dz // 4) ^ (low == 3).astype(jnp.int32))
    return 8 * gray_z + high + gray_y, 8 * gray_y + high + gray_z


def body(ensemble, spreading_coefficient, obs_anom, obs_weight, taper_table, obs_block, taper_id):
    members, rows, columns = ensemble.shape
    group = lax.axis_size("mem")
    states = lax.axis_size("state")
    per = rows // group
    tiles = 2 * per + 1
    size = tiles * members + 32

    j, at = lax.axis_index("mem"), lax.axis_index("state")
    chips = (group // 2, states // 8, 8)
    packed, obs_packed = pl.pallas_call(
        pack_obs_kernel,
        out_shape=[jax.ShapeDtypeStruct((1, obs_anom.shape[2], TILE), BF16), TOKEN],
        in_specs=[HBM] * 2,
        out_specs=[VMEM, HBM],
        scratch_shapes=[pltpu.VMEM(obs_anom.shape[1:], BF16), pltpu.SemaphoreType.DMA((2,))],
        name="pack_obs",
    )(obs_anom, obs_weight)
    up, down = pl.pallas_call(
        pack_halo_kernel,
        grid=(1,),
        out_shape=[jax.ShapeDtypeStruct((HALO * members + 8, columns), F32)] * 2,
        in_specs=[
            pl.BlockSpec((members, 8, columns), lambda i: (0, 0, 0)),
            pl.BlockSpec((members, 8, columns), lambda i: (0, rows // 8 - 1, 0)),
            VMEM,
            SMEM,
            SMEM,
            HBM,
        ],
        out_specs=[VMEM] * 2,
        name="pack_halo",
    )(ensemble, ensemble, spreading_coefficient, obs_block.T, taper_id.T, obs_packed)
    below = lax.ppermute(up, "state", [(i + 1, i) for i in range(states - 1)])
    above = lax.ppermute(down, "state", [(i, i + 1) for i in range(states - 1)])

    held, started = gather_first(packed, chips)
    row = (members, columns)
    prior, payload, edges, means, turned = pl.pallas_call(
        interior_kernel,
        out_shape=[
            pltpu.HBM((rows + 2, *row), F32),
            pltpu.HBM((group, size, TILE), BF16),
            jax.ShapeDtypeStruct((4 * FSTEPS, *row), F32),
            jax.ShapeDtypeStruct((group, 32, TILE), F32),
            pltpu.HBM(taper_table.shape, F32),
        ],
        in_specs=[VMEM] * 3 + [HBM],
        out_specs=[HBM] * 2 + [VMEM] * 2 + [HBM],
        scratch_shapes=[
            pltpu.VMEM((rows, *row), F32),
            pltpu.VMEM((rows, *row), F32),
            pltpu.VMEM((rows, 8, columns), F32),
            pltpu.VMEM((group, 2 * per * members, TILE), BF16),
            pltpu.VMEM(taper_table.shape, F32),
            pltpu.SemaphoreType.DMA((group + 1,)),
        ],
        compiler_params=pltpu.CompilerParams(vmem_limit_bytes=14 << 20),
        name="forecast_interior",
    )(ensemble, spreading_coefficient, taper_table, started)
    prior, payload, forecast_done = pl.pallas_call(
        edge_kernel,
        out_shape=[pltpu.HBM(prior.shape, F32), pltpu.HBM(payload.shape, BF16), TOKEN],
        in_specs=[VMEM] * 5 + [HBM] * 2,
        out_specs=[HBM] * 3,
        input_output_aliases={5: 0, 6: 1},
        scratch_shapes=[
            pltpu.VMEM((2, HALO + FSTEPS, *row), F32),
            pltpu.VMEM((2, HALO + FSTEPS, *row), F32),
            pltpu.VMEM((2, HALO + FSTEPS, 8, columns), F32),
            pltpu.VMEM((group, size, TILE), BF16),
            pltpu.VMEM((group, 32, TILE), F32),
            pltpu.VMEM((2, HALO, *row), F32),
            pltpu.SemaphoreType.DMA((group + 2,)),
        ],
        compiler_params=pltpu.CompilerParams(vmem_limit_bytes=14 << 20),
        name="forecast_edges",
    )(above, below, spreading_coefficient, edges, means, prior, payload)
    held, first, second = gather_second(held, chips, [forecast_done])
    own, swapped = gather_rest(held, first, second, chips)
    gathered = lax.all_to_all(payload, "mem", split_axis=0, concat_axis=0, tiled=True)

    edge = jnp.where(j < 2, above[-1, :16], below[-1, :16])
    edge = jnp.where(j % 2 == 0, edge.reshape(-1, 4)[:3:2], edge.reshape(-1, 4)[1:4:2]).astype(jnp.int32)
    mine = 2 * per * j
    blocks = jnp.concatenate([lax.dynamic_slice_in_dim(obs_block, mine, 2 * per, 0), edge[0:1]], axis=0)
    tapers = jnp.concatenate([lax.dynamic_slice_in_dim(taper_id, mine, 2 * per, 0), edge[1:2]], axis=0)

    anom_at, weight_at = places(blocks, at // 8, at % 8)
    late = 2
    early = own[:-late] + swapped[:-late]
    held_early, centred = pl.pallas_call(
        collect_kernel,
        out_shape=[
            jax.ShapeDtypeStruct((2, sum(v.shape[0] for v in own[:-late]), *packed.shape[1:]), BF16),
            jax.ShapeDtypeStruct((tiles, group * members, TILE), BF16),
        ],
        in_specs=[VMEM] * (1 + len(early)),
        out_specs=[VMEM] * 2,
        compiler_params=pltpu.CompilerParams(vmem_limit_bytes=18 << 20),
        name="collect",
    )(gathered, *early)
    increments = pl.pallas_call(
        analysis_kernel,
        out_shape=jax.ShapeDtypeStruct((group, tiles * members, TILE), BF16),
        in_specs=[SMEM] * 3 + [VMEM] * (3 + 2 * late),
        out_specs=VMEM,
        scratch_shapes=[pltpu.VMEM((2, sum(v.shape[0] for v in own[-late:]), *packed.shape[1:]), BF16)],
        compiler_params=pltpu.CompilerParams(vmem_limit_bytes=18 << 20),
        name="analysis",
    )(anom_at, weight_at, tapers, turned, centred, held_early, *own[-late:], *swapped[-late:])
    returned = lax.all_to_all(increments, "mem", split_axis=0, concat_axis=0, tiled=True)

    return pl.pallas_call(
        final_kernel,
        grid=(rows // 8,),
        out_shape=jax.ShapeDtypeStruct((members, rows, columns), F32),
        in_specs=[VMEM] * 2 + [pl.BlockSpec((8, columns), lambda i: (i, 0))],
        out_specs=pl.BlockSpec((members, 8, columns), lambda i: (0, i, 0)),
        scratch_shapes=[pltpu.VMEM((10, members, columns), F32)],
        compiler_params=pltpu.CompilerParams(vmem_limit_bytes=10 << 20),
        name="final_step",
    )(prior, returned, spreading_coefficient)


def solution(mesh):
    placed = (
        P("mem", "state", None),
        P("state", None),
        P("state", None, None),
        P("state", None, None),
        P(),
        P("state", None),
        P("state", None),
    )
    return jax.shard_map(
        body, mesh=mesh, in_specs=placed, out_specs=P("mem", "state", None), check_vma=False
    )
```

```python
import jax
import jax.numpy as jnp
from jax import lax
from jax.experimental import pallas as pl
from jax.experimental.pallas import tpu as pltpu
from jax.sharding import PartitionSpec as P

F32, BF16 = jnp.float32, jnp.bfloat16
TILE = 128
SLOTS = 4
FSTEPS = 4
HALO = FSTEPS + 1
VMEM = pl.BlockSpec(memory_space=pltpu.VMEM)
SMEM = pl.BlockSpec(memory_space=pltpu.SMEM)
HBM = pl.BlockSpec(memory_space=pltpu.HBM)


def pack_obs_kernel(anom_ref, weight_ref, out_ref, token_ref, held_ref, sem):
    members = anom_ref.shape[2]
    core = lax.rem(lax.axis_index("mem"), 2)
    for kind, ref in enumerate((anom_ref, weight_ref)):

        @pl.when(core == kind)
        def _(kind=kind, ref=ref):
            copy = pltpu.make_async_copy(ref.at[0], held_ref, sem.at[kind])
            copy.start()
            copy.wait()
            for q in range(members // TILE):
                part = held_ref[:, q * TILE : (q + 1) * TILE]
                out_ref[0, q * TILE : (q + 1) * TILE, :] = part if kind == 0 else part.T


def pack_halo_kernel(first_ref, last_ref, coef_ref, block_ref, taper_ref, after_ref, up_ref, down_ref):
    members, depth, columns = first_ref.shape
    rows = coef_ref.shape[0]
    tiles = block_ref.shape[1]
    lane = lax.broadcasted_iota(jnp.int32, (8, columns), 1)
    for out_ref, x_ref, start, row0, tile0 in (
        (up_ref, first_ref, 0, 0, 0),
        (down_ref, last_ref, depth - HALO, rows - HALO, tiles - 2),
    ):
        for r in range(HALO):
            out_ref[r * members : (r + 1) * members, :] = x_ref[:, start + r, :]
        ids = jnp.zeros((8, columns), jnp.int32)
        for t in range(2):
            for k in range(SLOTS):
                ids = jnp.where(lane == t * SLOTS + k, block_ref[k, tile0 + t], ids)
                ids = jnp.where(lane == 8 + t * SLOTS + k, taper_ref[k, tile0 + t], ids)
        out_ref[HALO * members :, :] = ids.astype(F32)
        out_ref[HALO * members : HALO * members + HALO, :] = coef_ref[row0 : row0 + HALO, :]


def stepped(mid, one_side, other_side, coef):
    chunk, columns = mid.shape
    beside = one_side + other_side + pltpu.roll(mid, 1, 1) + pltpu.roll(mid, columns - 1, 1)
    delta = (beside - 4.0 * mid).reshape(chunk // 8, 8, columns)
    return mid + (coef[None] * delta).reshape(chunk, columns)


def split_tile(value, slot, members, pay_ref, mean_ref):
    mean = jnp.sum(value, axis=0, keepdims=True) * (1.0 / members)
    pay_ref[slot * members : (slot + 1) * members, :] = (value - mean).astype(BF16)
    high = mean.astype(BF16).astype(F32)
    middle = (mean - high).astype(BF16).astype(F32)
    mean_ref[3 * slot : 3 * slot + 1, :] = high
    mean_ref[3 * slot + 1 : 3 * slot + 2, :] = middle
    mean_ref[3 * slot + 2 : 3 * slot + 3, :] = mean - high - middle


def interior_kernel(x_ref, coef_ref, taper_ref, token_ref, prior_ref, out_ref, edge_ref, mean_ref, turned_out, a_ref, b_ref, c_ref, pay_ref, turned_ref, sems):
    members, rows, columns = x_ref.shape
    group = out_ref.shape[0]
    per = rows // group
    for r in range(rows):
        c_ref[r] = jnp.broadcast_to(coef_ref[r : r + 1, :], (8, columns))
    chunk = 16

    def advance(number, carry):
        here = pl.ds(pl.multiple_of(number * chunk, chunk), chunk)
        for r in range(rows):
            a_ref[r, here, :] = x_ref[here, r, :]
        src, dst = a_ref, b_ref
        for step in range(1, FSTEPS + 1):
            done = step - 1
            for i, r in enumerate((done, done + 1, rows - 1 - done, rows - 2 - done)):
                edge_ref[4 * done + i, here, :] = src[r, here, :]
            for r in range(step, rows - step):
                dst[r, here, :] = stepped(src[r, here, :], src[r - 1, here, :], src[r + 1, here, :], c_ref[r])
            src, dst = dst, src
        return carry

    lax.fori_loop(0, members // chunk, advance, 0)
    src = a_ref if FSTEPS % 2 == 0 else b_ref
    inner = rows - 2 * FSTEPS
    copies = [pltpu.make_async_copy(src.at[pl.ds(FSTEPS, inner)], prior_ref.at[pl.ds(FSTEPS + 1, inner)], sems.at[0])]
    copies[0].start()
    mean_ref[...] = jnp.zeros_like(mean_ref)
    for j in range(1, group - 1):
        for i in range(per):
            for half in range(2):
                value = src[j * per + i, :, half * TILE : (half + 1) * TILE]
                split_tile(value, 2 * i + half, members, pay_ref.at[j], mean_ref.at[j])
        copies.append(pltpu.make_async_copy(pay_ref.at[j], out_ref.at[j, pl.ds(0, 2 * per * members)], sems.at[j]))
        copies[-1].start()
    for i in range(taper_ref.shape[0]):
        turned_ref[i] = taper_ref[i].T
    copies.append(pltpu.make_async_copy(turned_ref, turned_out, sems.at[group]))
    copies[-1].start()
    for copy in copies:
        copy.wait()


def edge_kernel(above_ref, below_ref, coef_ref, edge_ref, mean_ref, prior_in, pay_in, prior_ref, out_ref, ids_ref, token_ref, a_ref, b_ref, c_ref, pay_ref, m_ref, last_ref, sems):
    rows, columns = coef_ref.shape
    members = last_ref.shape[2]
    group, size, _ = out_ref.shape
    per = rows // group
    tiles = 2 * per + 1
    halos = (above_ref, below_ref)
    sides = [ref[HALO * members :, 0:TILE].astype(jnp.int32) for ref in halos]
    ids_ref[...] = jnp.where(lax.axis_index("mem") < 2, sides[0], sides[1])
    for side in range(2):
        for t in range(HALO + FSTEPS):
            if t < HALO:
                r = HALO * members + (t if side == 0 else HALO - 1 - t)
                row = halos[side][r : r + 1, :]
            else:
                r = t - HALO if side == 0 else rows - 1 - (t - HALO)
                row = coef_ref[r : r + 1, :]
            c_ref[side, t] = jnp.broadcast_to(row, (8, columns))
    chunk = 16

    def advance(number, carry):
        here = pl.ds(pl.multiple_of(number * chunk, chunk), chunk)
        for side in range(2):

            def value(step, t, side=side):
                if t > step + HALO - 1:
                    return edge_ref[4 * step + 2 * side + t - step - HALO, here, :]
                if step == 0:
                    r = t if side == 0 else HALO - 1 - t
                    return halos[side][pl.ds(pl.multiple_of(r * members + number * chunk, chunk), chunk), :]
                return (a_ref, b_ref)[step % 2][side, t, here, :]

            for step in range(1, FSTEPS + 1):
                for t in range(step, step + HALO):
                    new = stepped(value(step - 1, t), value(step - 1, t - 1), value(step - 1, t + 1), c_ref[side, t])
                    if step < FSTEPS:
                        (a_ref, b_ref)[step % 2][side, t, here, :] = new
                    else:
                        last_ref[side, t - FSTEPS if side == 0 else 2 * FSTEPS - t, here, :] = new
        return carry

    lax.fori_loop(0, members // chunk, advance, 0)
    copies = [
        pltpu.make_async_copy(last_ref.at[0], prior_ref.at[pl.ds(0, HALO)], sems.at[0]),
        pltpu.make_async_copy(last_ref.at[1], prior_ref.at[pl.ds(rows + 2 - HALO, HALO)], sems.at[1]),
    ]
    for copy in copies:
        copy.start()
    m_ref[...] = mean_ref[...]
    extra = tiles - 1
    for j in range(group):
        if j in (0, group - 1):
            for i in range(per):
                for half in range(2):
                    row = last_ref[0, i + 1] if j == 0 else last_ref[1, i]
                    split_tile(row[:, half * TILE : (half + 1) * TILE], 2 * i + half, members, pay_ref.at[j], m_ref.at[j])
        if j < 4:
            row = last_ref[0, 0] if j < 2 else last_ref[1, HALO - 1]
            split_tile(row[:, (j % 2) * TILE : (j % 2 + 1) * TILE], extra, members, pay_ref.at[j], m_ref.at[j])
        else:
            pay_ref[j, extra * members : tiles * members, :] = jnp.zeros((members, TILE), BF16)
        pay_ref[j, tiles * members :, :] = m_ref[j].astype(BF16)
        first = 0 if j in (0, group - 1) else extra * members
        part = pl.ds(first, size - first)
        copies.append(pltpu.make_async_copy(pay_ref.at[j, part], out_ref.at[j, part], sems.at[2 + j]))
        copies[-1].start()
    for copy in copies:
        copy.wait()


def fill(pieces, obs_ref):
    core = lax.rem(lax.axis_index("mem"), 2)
    for side in range(2):
        start = 0
        kind = core if side == 0 else 1 - core
        for piece in pieces[side * len(pieces) // 2 : (side + 1) * len(pieces) // 2]:

            def keep(i, carry, piece=piece, start=start, kind=kind):
                obs_ref[kind, start + i] = piece[i]
                return carry

            lax.fori_loop(0, piece.shape[0], keep, 0)
            start += piece.shape[0]


def collect_kernel(recv_ref, *rest):
    pieces, (obs_ref, centred_ref) = rest[:-2], rest[-2:]
    group, size, _ = recv_ref.shape
    tiles, members, _ = centred_ref.shape
    count = members // group
    fill(pieces, obs_ref)
    parts = recv_ref[:, size - 32 :, :].astype(F32)
    for t in range(tiles):
        own = parts[:, 3 * t, :] + parts[:, 3 * t + 1, :] + parts[:, 3 * t + 2, :]
        delta = own - jnp.mean(own, axis=0, keepdims=True)
        local = recv_ref[:, t * count : (t + 1) * count, :].astype(F32)
        centred_ref[t] = (local + delta[:, None, :]).astype(BF16).reshape(members, TILE)


def analysis_kernel(block_ref, pattern_ref, edge_ref, taper_ref, centred_ref, early_ref, *rest):
    pieces, (ret_ref, late_ref) = rest[:-2], rest[-2:]
    tiles, members, _ = centred_ref.shape
    group = ret_ref.shape[0]
    count = members // group
    early = early_ref.shape[1]
    fill(pieces, late_ref)
    slab, state = lax.axis_index("mem"), lax.axis_index("state")
    y, z, half = state // 8, lax.rem(state, 8), lax.rem(slab, 2)

    def number(ref, t, k, first):
        usual = ref[k, slab * (tiles - 1) + jnp.minimum(t, tiles - 2)]
        return jnp.where(t < tiles - 1, usual, edge_ref[7, first + half * SLOTS + k])

    def block(kind, at):
        near = early_ref[kind, jnp.minimum(at, early - 1)]
        far = late_ref[kind, jnp.maximum(at - early, 0)]
        return jnp.where(at < early, near, far)

    def one(t, carry):
        anoms, weights = [], []
        for k in range(SLOTS):
            anom_at, weight_at = places(number(block_ref, t, k, 0), y, z)
            anom = block(0, anom_at)
            anoms.append(jnp.concatenate([anom[q * TILE : (q + 1) * TILE] for q in range(members // TILE)], axis=1))
            weights.append(block(1, weight_at))
        cov = jnp.dot(jnp.concatenate(anoms, axis=0), centred_ref[t], preferred_element_type=F32) * (1.0 / (members - 1.0))
        tapered = [
            (taper_ref[number(pattern_ref, t, k, 2 * SLOTS)] * cov[k * TILE : (k + 1) * TILE]).astype(BF16) for k in range(SLOTS)
        ]
        total = jnp.dot(jnp.concatenate(weights, axis=1), jnp.concatenate(tapered, axis=0), preferred_element_type=F32)
        here = pl.ds(pl.multiple_of(t * count, count), count)
        ret_ref[:, here, :] = total.astype(BF16).reshape(group, count, TILE)
        return carry

    lax.fori_loop(0, tiles, one, 0, unroll=3)


def final_kernel(prior_ref, inc_ref, coef_ref, out_ref, v_ref):
    members, depth, columns = out_ref.shape
    group, size, _ = inc_ref.shape
    rows = prior_ref.shape[0] - 2
    per = rows // group
    extra = size // members - 1
    i, steps = pl.program_id(0), pl.num_programs(0)

    def put(index, j, slot, half):
        lanes = slice(half * TILE, (half + 1) * TILE)
        here = pl.ds(pl.multiple_of(slot * members, members), members)
        v_ref[index, :, lanes] = prior_ref[i * depth + index, :, lanes] + inc_ref[j, here, :].astype(F32)

    first = i * (depth // per)
    for half in range(2):
        top, bottom = i == 0, i == steps - 1
        put(0, jnp.where(top, half, first - 1), jnp.where(top, extra, 2 * (per - 1) + half), half)
        put(depth + 1, jnp.where(bottom, 2 + half, first + depth // per), jnp.where(bottom, extra, half), half)
        for r in range(depth):
            put(r + 1, first + r // per, 2 * (r % per) + half, half)
    coef = coef_ref[...]
    for r in range(depth):
        mid = v_ref[r + 1]
        beside = v_ref[r] + v_ref[r + 2] + pltpu.roll(mid, 1, 1) + pltpu.roll(mid, columns - 1, 1)
        out_ref[:, r, :] = mid + coef[r : r + 1, :] * (beside - 4.0 * mid)


AXES = ("mem", "state")


def fetch(value, mesh, source):
    xs, ys, zs = mesh
    pairs = []
    for x in range(xs):
        for c in range(2):
            for y in range(ys):
                for z in range(zs):
                    a, b, d, e = source(x, c, y, z)
                    pairs.append((((a * 2 + b) * ys + d % ys) * zs + e % zs, ((x * 2 + c) * ys + y) * zs + z))
    return lax.ppermute(value, AXES, pairs)


def ring(first, step):
    return lambda x, c, y, z: (x, c, y + step, z) if (c == 0) == first else (x, c, y, z + step)


def other_core(x, c, y, z):
    return (x, 1 - c, y, z)


TOKEN = jax.ShapeDtypeStruct((8, TILE), F32)


def join(operands, name, after):
    count = len(operands)

    def kernel(*refs):
        outs, sems = refs[count + len(after) : -1], refs[-1]
        core = lax.rem(lax.axis_index("mem"), 2)
        copies = []
        for a in range(count):
            copies.append(pltpu.make_async_copy(refs[a].at[0], outs[1].at[a], sems.at[2 * a]))
            copies.append(pltpu.make_async_copy(refs[a].at[core], outs[2].at[a], sems.at[2 * a + 1]))
        for copy in copies:
            copy.start()
        for a in range(count):
            for i in range(2):
                outs[0][i * count + a] = refs[a][i]
        for copy in copies:
            copy.wait()

    block = operands[0].shape[1:]
    return pl.pallas_call(
        kernel,
        out_shape=[jax.ShapeDtypeStruct((2 * count, *block), BF16)] + [pltpu.HBM((count, *block), BF16)] * 2,
        in_specs=[VMEM] * count + [HBM] * len(after),
        out_specs=[VMEM] + [HBM] * 2,
        scratch_shapes=[pltpu.SemaphoreType.DMA((2 * count,))],
        compiler_params=pltpu.CompilerParams(vmem_limit_bytes=6 << 20),
        name=name,
    )(*operands, *after)


def join_two_kernel(own_ref, far_ref, held_ref, token_ref):
    held_ref[0] = own_ref[0]
    held_ref[1] = far_ref[0]


def gather_first(own, mesh):
    far = fetch(own, mesh, lambda x, c, y, z: (x, c, y, z + 4))
    return pl.pallas_call(
        join_two_kernel,
        out_shape=[jax.ShapeDtypeStruct((2, *own.shape[1:]), BF16), TOKEN],
        in_specs=[VMEM] * 2,
        out_specs=[VMEM, HBM],
        compiler_params=pltpu.CompilerParams(vmem_limit_bytes=6 << 20),
        name="join_two",
    )(own, far)


def gather_second(held, mesh, after):
    p, m, q = (fetch(held, mesh, ring(True, step)) for step in (1, -1, 2))
    return join([held, p, m, q], "join_eight", after)


def gather_rest(held, first, second, mesh):
    p, m = (fetch(held, mesh, ring(False, step)) for step in (1, -1))
    q = fetch(first, mesh, ring(False, 2))
    r = fetch(second, mesh, ring(False, -2))
    own = [held, p, m, q, r]
    return own, [fetch(v, mesh, other_core) for v in own]


def places(block, y, z):
    dy, dz = (block // 8 - y) & 3, (block - z) & 7
    low = dz & 3
    gray_y, gray_z = dy ^ (dy >> 1), low ^ (low >> 1)
    high = 4 * ((dz >> 2) ^ jnp.where(low == 3, 1, 0))
    return 8 * gray_z + high + gray_y, 8 * gray_y + high + gray_z


def body(ensemble, spreading_coefficient, obs_anom, obs_weight, taper_table, obs_block, taper_id):
    members, rows, columns = ensemble.shape
    group = lax.axis_size("mem")
    states = lax.axis_size("state")
    per = rows // group
    tiles = 2 * per + 1
    size = tiles * members + 32

    chips = (group // 2, states // 8, 8)
    packed, obs_packed = pl.pallas_call(
        pack_obs_kernel,
        out_shape=[jax.ShapeDtypeStruct((1, obs_anom.shape[2], TILE), BF16), TOKEN],
        in_specs=[HBM] * 2,
        out_specs=[VMEM, HBM],
        scratch_shapes=[pltpu.VMEM(obs_anom.shape[1:], BF16), pltpu.SemaphoreType.DMA((2,))],
        name="pack_obs",
    )(obs_anom, obs_weight)
    up, down = pl.pallas_call(
        pack_halo_kernel,
        grid=(1,),
        out_shape=[jax.ShapeDtypeStruct((HALO * members + 8, columns), F32)] * 2,
        in_specs=[
            pl.BlockSpec((members, 8, columns), lambda i: (0, 0, 0)),
            pl.BlockSpec((members, 8, columns), lambda i: (0, rows // 8 - 1, 0)),
            VMEM,
            SMEM,
            SMEM,
            HBM,
        ],
        out_specs=[VMEM] * 2,
        name="pack_halo",
    )(ensemble, ensemble, spreading_coefficient, obs_block.T, taper_id.T, obs_packed)
    below = lax.ppermute(up, "state", [(i + 1, i) for i in range(states - 1)])
    above = lax.ppermute(down, "state", [(i, i + 1) for i in range(states - 1)])

    held, started = gather_first(packed, chips)
    row = (members, columns)
    prior, payload, edges, means, turned = pl.pallas_call(
        interior_kernel,
        out_shape=[
            pltpu.HBM((rows + 2, *row), F32),
            pltpu.HBM((group, size, TILE), BF16),
            jax.ShapeDtypeStruct((4 * FSTEPS, *row), F32),
            jax.ShapeDtypeStruct((group, 32, TILE), F32),
            pltpu.HBM(taper_table.shape, F32),
        ],
        in_specs=[VMEM] * 3 + [HBM],
        out_specs=[HBM] * 2 + [VMEM] * 2 + [HBM],
        scratch_shapes=[
            pltpu.VMEM((rows, *row), F32),
            pltpu.VMEM((rows, *row), F32),
            pltpu.VMEM((rows, 8, columns), F32),
            pltpu.VMEM((group, 2 * per * members, TILE), BF16),
            pltpu.VMEM(taper_table.shape, F32),
            pltpu.SemaphoreType.DMA((group + 1,)),
        ],
        compiler_params=pltpu.CompilerParams(vmem_limit_bytes=14 << 20),
        name="forecast_interior",
    )(ensemble, spreading_coefficient, taper_table, started)
    prior, payload, edge_ids, forecast_done = pl.pallas_call(
        edge_kernel,
        out_shape=[pltpu.HBM(prior.shape, F32), pltpu.HBM(payload.shape, BF16), jax.ShapeDtypeStruct((8, TILE), jnp.int32), TOKEN],
        in_specs=[VMEM] * 5 + [HBM] * 2,
        out_specs=[HBM] * 2 + [VMEM, HBM],
        input_output_aliases={5: 0, 6: 1},
        scratch_shapes=[
            pltpu.VMEM((2, HALO + FSTEPS, *row), F32),
            pltpu.VMEM((2, HALO + FSTEPS, *row), F32),
            pltpu.VMEM((2, HALO + FSTEPS, 8, columns), F32),
            pltpu.VMEM((group, size, TILE), BF16),
            pltpu.VMEM((group, 32, TILE), F32),
            pltpu.VMEM((2, HALO, *row), F32),
            pltpu.SemaphoreType.DMA((group + 2,)),
        ],
        compiler_params=pltpu.CompilerParams(vmem_limit_bytes=14 << 20),
        name="forecast_edges",
    )(above, below, spreading_coefficient, edges, means, prior, payload)
    held, first, second = gather_second(held, chips, [forecast_done])
    own, swapped = gather_rest(held, first, second, chips)
    gathered = lax.all_to_all(payload, "mem", split_axis=0, concat_axis=0, tiled=True)

    late = 2
    early = own[:-late] + swapped[:-late]
    held_early, centred = pl.pallas_call(
        collect_kernel,
        out_shape=[
            jax.ShapeDtypeStruct((2, sum(v.shape[0] for v in own[:-late]), *packed.shape[1:]), BF16),
            jax.ShapeDtypeStruct((tiles, group * members, TILE), BF16),
        ],
        in_specs=[VMEM] * (1 + len(early)),
        out_specs=[VMEM] * 2,
        compiler_params=pltpu.CompilerParams(vmem_limit_bytes=18 << 20),
        name="collect",
    )(gathered, *early)
    increments = pl.pallas_call(
        analysis_kernel,
        out_shape=jax.ShapeDtypeStruct((group, tiles * members, TILE), BF16),
        in_specs=[SMEM] * 3 + [VMEM] * (3 + 2 * late),
        out_specs=VMEM,
        scratch_shapes=[pltpu.VMEM((2, sum(v.shape[0] for v in own[-late:]), *packed.shape[1:]), BF16)],
        compiler_params=pltpu.CompilerParams(vmem_limit_bytes=18 << 20),
        name="analysis",
    )(obs_block.T, taper_id.T, edge_ids, turned, centred, held_early, *own[-late:], *swapped[-late:])
    returned = lax.all_to_all(increments, "mem", split_axis=0, concat_axis=0, tiled=True)

    return pl.pallas_call(
        final_kernel,
        grid=(rows // 8,),
        out_shape=jax.ShapeDtypeStruct((members, rows, columns), F32),
        in_specs=[VMEM] * 2 + [pl.BlockSpec((8, columns), lambda i: (i, 0))],
        out_specs=pl.BlockSpec((members, 8, columns), lambda i: (0, i, 0)),
        scratch_shapes=[pltpu.VMEM((10, members, columns), F32)],
        compiler_params=pltpu.CompilerParams(vmem_limit_bytes=10 << 20),
        name="final_step",
    )(prior, returned, spreading_coefficient)


def solution(mesh):
    placed = (
        P("mem", "state", None),
        P("state", None),
        P("state", None, None),
        P("state", None, None),
        P(),
        P("state", None),
        P("state", None),
    )
    return jax.shard_map(
        body, mesh=mesh, in_specs=placed, out_specs=P("mem", "state", None), check_vma=False
    )
```

```python
import jax
import jax.numpy as jnp
from jax import lax
from jax.experimental import pallas as pl
from jax.experimental.pallas import tpu as pltpu
from jax.sharding import PartitionSpec as P

F32, BF16 = jnp.float32, jnp.bfloat16
TILE = 128
SLOTS = 4
FSTEPS = 4
HALO = FSTEPS + 1
VMEM = pl.BlockSpec(memory_space=pltpu.VMEM)
SMEM = pl.BlockSpec(memory_space=pltpu.SMEM)
HBM = pl.BlockSpec(memory_space=pltpu.HBM)


def pack_obs_kernel(anom_ref, weight_ref, out_ref, token_ref, held_ref, sem):
    members = anom_ref.shape[2]
    core = lax.rem(lax.axis_index("mem"), 2)
    for kind, ref in enumerate((anom_ref, weight_ref)):

        @pl.when(core == kind)
        def _(kind=kind, ref=ref):
            copy = pltpu.make_async_copy(ref.at[0], held_ref, sem.at[kind])
            copy.start()
            copy.wait()
            for q in range(members // TILE):
                part = held_ref[:, q * TILE : (q + 1) * TILE]
                out_ref[0, q * TILE : (q + 1) * TILE, :] = part if kind == 0 else part.T


def pack_halo_kernel(first_ref, last_ref, coef_ref, block_ref, taper_ref, after_ref, up_ref, down_ref):
    members, depth, columns = first_ref.shape
    rows = coef_ref.shape[0]
    tiles = block_ref.shape[1]
    lane = lax.broadcasted_iota(jnp.int32, (8, columns), 1)
    for out_ref, x_ref, start, row0, tile0 in (
        (up_ref, first_ref, 0, 0, 0),
        (down_ref, last_ref, depth - HALO, rows - HALO, tiles - 2),
    ):
        for r in range(HALO):
            out_ref[r * members : (r + 1) * members, :] = x_ref[:, start + r, :]
        ids = jnp.zeros((8, columns), jnp.int32)
        for t in range(2):
            for k in range(SLOTS):
                ids = jnp.where(lane == t * SLOTS + k, block_ref[k, tile0 + t], ids)
                ids = jnp.where(lane == 8 + t * SLOTS + k, taper_ref[k, tile0 + t], ids)
        out_ref[HALO * members :, :] = ids.astype(F32)
        out_ref[HALO * members : HALO * members + HALO, :] = coef_ref[row0 : row0 + HALO, :]


def stepped(mid, one_side, other_side, coef):
    chunk, columns = mid.shape
    beside = one_side + other_side + pltpu.roll(mid, 1, 1) + pltpu.roll(mid, columns - 1, 1)
    delta = (beside - 4.0 * mid).reshape(chunk // 8, 8, columns)
    return mid + (coef[None] * delta).reshape(chunk, columns)


def split_tile(value, slot, members, pay_ref, mean_ref):
    mean = jnp.sum(value, axis=0, keepdims=True) * (1.0 / members)
    pay_ref[slot * members : (slot + 1) * members, :] = (value - mean).astype(BF16)
    high = mean.astype(BF16).astype(F32)
    middle = (mean - high).astype(BF16).astype(F32)
    mean_ref[3 * slot : 3 * slot + 1, :] = high
    mean_ref[3 * slot + 1 : 3 * slot + 2, :] = middle
    mean_ref[3 * slot + 2 : 3 * slot + 3, :] = mean - high - middle


def interior_kernel(x_ref, coef_ref, taper_ref, token_ref, prior_ref, out_ref, edge_ref, mean_ref, turned_out, a_ref, b_ref, c_ref, pay_ref, turned_ref, sems):
    members, rows, columns = x_ref.shape
    group = out_ref.shape[0]
    per = rows // group
    for r in range(rows):
        c_ref[r] = jnp.broadcast_to(coef_ref[r : r + 1, :], (8, columns))
    chunk = 16

    def advance(number, carry):
        here = pl.ds(pl.multiple_of(number * chunk, chunk), chunk)
        for r in range(rows):
            a_ref[r, here, :] = x_ref[here, r, :]
        src, dst = a_ref, b_ref
        for step in range(1, FSTEPS + 1):
            done = step - 1
            for i, r in enumerate((done, done + 1, rows - 1 - done, rows - 2 - done)):
                edge_ref[4 * done + i, here, :] = src[r, here, :]
            for r in range(step, rows - step):
                dst[r, here, :] = stepped(src[r, here, :], src[r - 1, here, :], src[r + 1, here, :], c_ref[r])
            src, dst = dst, src
        return carry

    lax.fori_loop(0, members // chunk, advance, 0)
    src = a_ref if FSTEPS % 2 == 0 else b_ref
    inner = rows - 2 * FSTEPS
    copies = [pltpu.make_async_copy(src.at[pl.ds(FSTEPS, inner)], prior_ref.at[pl.ds(FSTEPS + 1, inner)], sems.at[0])]
    copies[0].start()
    mean_ref[...] = jnp.zeros_like(mean_ref)
    for j in range(1, group - 1):
        for i in range(per):
            for half in range(2):
                value = src[j * per + i, :, half * TILE : (half + 1) * TILE]
                split_tile(value, 2 * i + half, members, pay_ref.at[j], mean_ref.at[j])
        copies.append(pltpu.make_async_copy(pay_ref.at[j], out_ref.at[j, pl.ds(0, 2 * per * members)], sems.at[j]))
        copies[-1].start()
    for i in range(taper_ref.shape[0]):
        turned_ref[i] = taper_ref[i].T
    copies.append(pltpu.make_async_copy(turned_ref, turned_out, sems.at[group]))
    copies[-1].start()
    for copy in copies:
        copy.wait()


def edge_kernel(above_ref, below_ref, coef_ref, edge_ref, mean_ref, prior_in, pay_in, prior_ref, out_ref, token_ref, a_ref, b_ref, c_ref, pay_ref, m_ref, last_ref, sems):
    rows, columns = coef_ref.shape
    members = last_ref.shape[2]
    group, size, _ = out_ref.shape
    per = rows // group
    tiles = 2 * per + 1
    halos = (above_ref, below_ref)
    for side in range(2):
        for t in range(HALO + FSTEPS):
            if t < HALO:
                r = HALO * members + (t if side == 0 else HALO - 1 - t)
                row = halos[side][r : r + 1, :]
            else:
                r = t - HALO if side == 0 else rows - 1 - (t - HALO)
                row = coef_ref[r : r + 1, :]
            c_ref[side, t] = jnp.broadcast_to(row, (8, columns))
    chunk = 16

    def advance(number, carry):
        here = pl.ds(pl.multiple_of(number * chunk, chunk), chunk)
        for side in range(2):

            def value(step, t, side=side):
                if t > step + HALO - 1:
                    return edge_ref[4 * step + 2 * side + t - step - HALO, here, :]
                if step == 0:
                    r = t if side == 0 else HALO - 1 - t
                    return halos[side][pl.ds(pl.multiple_of(r * members + number * chunk, chunk), chunk), :]
                return (a_ref, b_ref)[step % 2][side, t, here, :]

            for step in range(1, FSTEPS + 1):
                for t in range(step, step + HALO):
                    new = stepped(value(step - 1, t), value(step - 1, t - 1), value(step - 1, t + 1), c_ref[side, t])
                    if step < FSTEPS:
                        (a_ref, b_ref)[step % 2][side, t, here, :] = new
                    else:
                        last_ref[side, t - FSTEPS if side == 0 else 2 * FSTEPS - t, here, :] = new
        return carry

    lax.fori_loop(0, members // chunk, advance, 0)
    copies = [
        pltpu.make_async_copy(last_ref.at[0], prior_ref.at[pl.ds(0, HALO)], sems.at[0]),
        pltpu.make_async_copy(last_ref.at[1], prior_ref.at[pl.ds(rows + 2 - HALO, HALO)], sems.at[1]),
    ]
    for copy in copies:
        copy.start()
    m_ref[...] = mean_ref[...]
    extra = tiles - 1
    for j in range(group):
        if j in (0, group - 1):
            for i in range(per):
                for half in range(2):
                    row = last_ref[0, i + 1] if j == 0 else last_ref[1, i]
                    split_tile(row[:, half * TILE : (half + 1) * TILE], 2 * i + half, members, pay_ref.at[j], m_ref.at[j])
        if j < 4:
            row = last_ref[0, 0] if j < 2 else last_ref[1, HALO - 1]
            split_tile(row[:, (j % 2) * TILE : (j % 2 + 1) * TILE], extra, members, pay_ref.at[j], m_ref.at[j])
        else:
            pay_ref[j, extra * members : tiles * members, :] = jnp.zeros((members, TILE), BF16)
        pay_ref[j, tiles * members :, :] = m_ref[j].astype(BF16)
        first = 0 if j in (0, group - 1) else extra * members
        part = pl.ds(first, size - first)
        copies.append(pltpu.make_async_copy(pay_ref.at[j, part], out_ref.at[j, part], sems.at[2 + j]))
        copies[-1].start()
    for copy in copies:
        copy.wait()


def fill(pieces, obs_ref):
    core = lax.rem(lax.axis_index("mem"), 2)
    for side in range(2):
        start = 0
        kind = core if side == 0 else 1 - core
        for piece in pieces[side * len(pieces) // 2 : (side + 1) * len(pieces) // 2]:

            def keep(i, carry, piece=piece, start=start, kind=kind):
                obs_ref[kind, start + i] = piece[i]
                return carry

            lax.fori_loop(0, piece.shape[0], keep, 0)
            start += piece.shape[0]


def collect_kernel(recv_ref, *rest):
    pieces, (obs_ref, centred_ref) = rest[:-2], rest[-2:]
    group, size, _ = recv_ref.shape
    tiles, members, _ = centred_ref.shape
    count = members // group
    fill(pieces, obs_ref)
    parts = recv_ref[:, size - 32 :, :].astype(F32)
    for t in range(tiles):
        own = parts[:, 3 * t, :] + parts[:, 3 * t + 1, :] + parts[:, 3 * t + 2, :]
        delta = own - jnp.mean(own, axis=0, keepdims=True)
        local = recv_ref[:, t * count : (t + 1) * count, :].astype(F32)
        centred_ref[t] = (local + delta[:, None, :]).astype(BF16).reshape(members, TILE)


def analysis_kernel(anom_at_ref, weight_at_ref, tapers_ref, taper_ref, centred_ref, early_ref, *rest):
    pieces, (ret_ref, late_ref) = rest[:-2], rest[-2:]
    tiles, members, _ = centred_ref.shape
    group = ret_ref.shape[0]
    count = members // group
    early = early_ref.shape[1]
    fill(pieces, late_ref)

    def block(kind, at):
        near = early_ref[kind, jnp.minimum(at, early - 1)]
        far = late_ref[kind, jnp.maximum(at - early, 0)]
        return jnp.where(at < early, near, far)

    def one(t, carry):
        anoms, weights = [], []
        for k in range(SLOTS):
            anom = block(0, anom_at_ref[t, k])
            anoms.append(jnp.concatenate([anom[q * TILE : (q + 1) * TILE] for q in range(members // TILE)], axis=1))
            weights.append(block(1, weight_at_ref[t, k]))
        cov = jnp.dot(jnp.concatenate(anoms, axis=0), centred_ref[t], preferred_element_type=F32) * (1.0 / (members - 1.0))
        tapered = [
            (taper_ref[tapers_ref[t, k]] * cov[k * TILE : (k + 1) * TILE]).astype(BF16) for k in range(SLOTS)
        ]
        total = jnp.dot(jnp.concatenate(weights, axis=1), jnp.concatenate(tapered, axis=0), preferred_element_type=F32)
        here = pl.ds(pl.multiple_of(t * count, count), count)
        ret_ref[:, here, :] = total.astype(BF16).reshape(group, count, TILE)
        return carry

    lax.fori_loop(0, tiles, one, 0, unroll=3)


def final_kernel(prior_ref, inc_ref, coef_ref, out_ref, v_ref):
    members, depth, columns = out_ref.shape
    group, size, _ = inc_ref.shape
    rows = prior_ref.shape[0] - 2
    per = rows // group
    extra = size // members - 1
    i, steps = pl.program_id(0), pl.num_programs(0)

    def put(index, j, slot, half):
        lanes = slice(half * TILE, (half + 1) * TILE)
        here = pl.ds(pl.multiple_of(slot * members, members), members)
        v_ref[index, :, lanes] = prior_ref[i * depth + index, :, lanes] + inc_ref[j, here, :].astype(F32)

    first = i * (depth // per)
    for half in range(2):
        top, bottom = i == 0, i == steps - 1
        put(0, jnp.where(top, half, first - 1), jnp.where(top, extra, 2 * (per - 1) + half), half)
        put(depth + 1, jnp.where(bottom, 2 + half, first + depth // per), jnp.where(bottom, extra, half), half)
        for r in range(depth):
            put(r + 1, first + r // per, 2 * (r % per) + half, half)
    coef = coef_ref[...]
    for r in range(depth):
        mid = v_ref[r + 1]
        beside = v_ref[r] + v_ref[r + 2] + pltpu.roll(mid, 1, 1) + pltpu.roll(mid, columns - 1, 1)
        out_ref[:, r, :] = mid + coef[r : r + 1, :] * (beside - 4.0 * mid)


AXES = ("mem", "state")


def fetch(value, mesh, source):
    xs, ys, zs = mesh
    pairs = []
    for x in range(xs):
        for c in range(2):
            for y in range(ys):
                for z in range(zs):
                    a, b, d, e = source(x, c, y, z)
                    pairs.append((((a * 2 + b) * ys + d % ys) * zs + e % zs, ((x * 2 + c) * ys + y) * zs + z))
    return lax.ppermute(value, AXES, pairs)


def ring(first, step):
    return lambda x, c, y, z: (x, c, y + step, z) if (c == 0) == first else (x, c, y, z + step)


def other_core(x, c, y, z):
    return (x, 1 - c, y, z)


TOKEN = jax.ShapeDtypeStruct((8, TILE), F32)


def join(operands, name, after):
    count = len(operands)

    def kernel(*refs):
        outs = refs[count + len(after) :]
        core = lax.rem(lax.axis_index("mem"), 2)
        for a in range(count):
            for i in range(2):
                outs[0][i * count + a] = refs[a][i]
            outs[1][a] = refs[a][0]
            outs[2][a] = refs[a][core]

    shapes = [(n, *operands[0].shape[1:]) for n in (2 * count, count, count)]
    return pl.pallas_call(
        kernel,
        out_shape=[jax.ShapeDtypeStruct(shape, BF16) for shape in shapes],
        in_specs=[VMEM] * count + [HBM] * len(after),
        out_specs=[VMEM] * len(shapes),
        compiler_params=pltpu.CompilerParams(vmem_limit_bytes=6 << 20),
        name=name,
    )(*operands, *after)


def join_two_kernel(own_ref, far_ref, held_ref, token_ref):
    held_ref[0] = own_ref[0]
    held_ref[1] = far_ref[0]


def gather_first(own, mesh):
    far = fetch(own, mesh, lambda x, c, y, z: (x, c, y, z + 4))
    return pl.pallas_call(
        join_two_kernel,
        out_shape=[jax.ShapeDtypeStruct((2, *own.shape[1:]), BF16), TOKEN],
        in_specs=[VMEM] * 2,
        out_specs=[VMEM, HBM],
        compiler_params=pltpu.CompilerParams(vmem_limit_bytes=6 << 20),
        name="join_two",
    )(own, far)


def gather_second(held, mesh, after):
    p, m, q = (fetch(held, mesh, ring(True, step)) for step in (1, -1, 2))
    return join([held, p, m, q], "join_eight", after)


def gather_rest(held, first, second, mesh):
    p, m = (fetch(held, mesh, ring(False, step)) for step in (1, -1))
    q = fetch(first, mesh, ring(False, 2))
    r = fetch(second, mesh, ring(False, -2))
    own = [held, p, m, q, r]
    return own, [fetch(v, mesh, other_core) for v in own]


def places(block, y, z):
    dy, dz = (block // 8 - y) % 4, (block % 8 - z) % 8
    low = dz % 4
    gray_y, gray_z = dy ^ (dy >> 1), low ^ (low >> 1)
    high = 4 * ((dz // 4) ^ (low == 3).astype(jnp.int32))
    return 8 * gray_z + high + gray_y, 8 * gray_y + high + gray_z


def body(ensemble, spreading_coefficient, obs_anom, obs_weight, taper_table, obs_block, taper_id):
    members, rows, columns = ensemble.shape
    group = lax.axis_size("mem")
    states = lax.axis_size("state")
    per = rows // group
    tiles = 2 * per + 1
    size = tiles * members + 32

    j, at = lax.axis_index("mem"), lax.axis_index("state")
    chips = (group // 2, states // 8, 8)
    packed, obs_packed = pl.pallas_call(
        pack_obs_kernel,
        out_shape=[jax.ShapeDtypeStruct((1, obs_anom.shape[2], TILE), BF16), TOKEN],
        in_specs=[HBM] * 2,
        out_specs=[VMEM, HBM],
        scratch_shapes=[pltpu.VMEM(obs_anom.shape[1:], BF16), pltpu.SemaphoreType.DMA((2,))],
        name="pack_obs",
    )(obs_anom, obs_weight)
    up, down = pl.pallas_call(
        pack_halo_kernel,
        grid=(1,),
        out_shape=[jax.ShapeDtypeStruct((HALO * members + 8, columns), F32)] * 2,
        in_specs=[
            pl.BlockSpec((members, 8, columns), lambda i: (0, 0, 0)),
            pl.BlockSpec((members, 8, columns), lambda i: (0, rows // 8 - 1, 0)),
            VMEM,
            SMEM,
            SMEM,
            HBM,
        ],
        out_specs=[VMEM] * 2,
        name="pack_halo",
    )(ensemble, ensemble, spreading_coefficient, obs_block.T, taper_id.T, obs_packed)
    below = lax.ppermute(up, "state", [(i + 1, i) for i in range(states - 1)])
    above = lax.ppermute(down, "state", [(i, i + 1) for i in range(states - 1)])

    held, started = gather_first(packed, chips)
    row = (members, columns)
    prior, payload, edges, means, turned = pl.pallas_call(
        interior_kernel,
        out_shape=[
            pltpu.HBM((rows + 2, *row), F32),
            pltpu.HBM((group, size, TILE), BF16),
            jax.ShapeDtypeStruct((4 * FSTEPS, *row), F32),
            jax.ShapeDtypeStruct((group, 32, TILE), F32),
            pltpu.HBM(taper_table.shape, F32),
        ],
        in_specs=[VMEM] * 3 + [HBM],
        out_specs=[HBM] * 2 + [VMEM] * 2 + [HBM],
        scratch_shapes=[
            pltpu.VMEM((rows, *row), F32),
            pltpu.VMEM((rows, *row), F32),
            pltpu.VMEM((rows, 8, columns), F32),
            pltpu.VMEM((group, 2 * per * members, TILE), BF16),
            pltpu.VMEM(taper_table.shape, F32),
            pltpu.SemaphoreType.DMA((group + 1,)),
        ],
        compiler_params=pltpu.CompilerParams(vmem_limit_bytes=14 << 20),
        name="forecast_interior",
    )(ensemble, spreading_coefficient, taper_table, started)
    prior, payload, forecast_done = pl.pallas_call(
        edge_kernel,
        out_shape=[pltpu.HBM(prior.shape, F32), pltpu.HBM(payload.shape, BF16), TOKEN],
        in_specs=[VMEM] * 5 + [HBM] * 2,
        out_specs=[HBM] * 3,
        input_output_aliases={5: 0, 6: 1},
        scratch_shapes=[
            pltpu.VMEM((2, HALO + FSTEPS, *row), F32),
            pltpu.VMEM((2, HALO + FSTEPS, *row), F32),
            pltpu.VMEM((2, HALO + FSTEPS, 8, columns), F32),
            pltpu.VMEM((group, size, TILE), BF16),
            pltpu.VMEM((group, 32, TILE), F32),
            pltpu.VMEM((2, HALO, *row), F32),
            pltpu.SemaphoreType.DMA((group + 2,)),
        ],
        compiler_params=pltpu.CompilerParams(vmem_limit_bytes=14 << 20),
        name="forecast_edges",
    )(above, below, spreading_coefficient, edges, means, prior, payload)
    held, first, second = gather_second(held, chips, [forecast_done])
    own, swapped = gather_rest(held, first, second, chips)
    gathered = lax.all_to_all(payload, "mem", split_axis=0, concat_axis=0, tiled=True)

    edge = jnp.where(j < 2, above[-1, :16], below[-1, :16])
    edge = jnp.where(j % 2 == 0, edge.reshape(-1, 4)[:3:2], edge.reshape(-1, 4)[1:4:2]).astype(jnp.int32)
    mine = 2 * per * j
    blocks = jnp.concatenate([lax.dynamic_slice_in_dim(obs_block, mine, 2 * per, 0), edge[0:1]], axis=0)
    tapers = jnp.concatenate([lax.dynamic_slice_in_dim(taper_id, mine, 2 * per, 0), edge[1:2]], axis=0)

    anom_at, weight_at = places(blocks, at // 8, at % 8)
    late = 2
    early = own[:-late] + swapped[:-late]
    held_early, centred = pl.pallas_call(
        collect_kernel,
        out_shape=[
            jax.ShapeDtypeStruct((2, sum(v.shape[0] for v in own[:-late]), *packed.shape[1:]), BF16),
            jax.ShapeDtypeStruct((tiles, group * members, TILE), BF16),
        ],
        in_specs=[VMEM] * (1 + len(early)),
        out_specs=[VMEM] * 2,
        compiler_params=pltpu.CompilerParams(vmem_limit_bytes=18 << 20),
        name="collect",
    )(gathered, *early)
    increments = pl.pallas_call(
        analysis_kernel,
        out_shape=jax.ShapeDtypeStruct((group, tiles * members, TILE), BF16),
        in_specs=[SMEM] * 3 + [VMEM] * (3 + 2 * late),
        out_specs=VMEM,
        scratch_shapes=[pltpu.VMEM((2, sum(v.shape[0] for v in own[-late:]), *packed.shape[1:]), BF16)],
        compiler_params=pltpu.CompilerParams(vmem_limit_bytes=18 << 20),
        name="analysis",
    )(anom_at, weight_at, tapers, turned, centred, held_early, *own[-late:], *swapped[-late:])
    returned = lax.all_to_all(increments, "mem", split_axis=0, concat_axis=0, tiled=True)

    return pl.pallas_call(
        final_kernel,
        grid=(rows // 8,),
        out_shape=jax.ShapeDtypeStruct((members, rows, columns), F32),
        in_specs=[VMEM] * 2 + [pl.BlockSpec((8, columns), lambda i: (i, 0))],
        out_specs=pl.BlockSpec((members, 8, columns), lambda i: (0, i, 0)),
        scratch_shapes=[pltpu.VMEM((10, members, columns), F32)],
        compiler_params=pltpu.CompilerParams(vmem_limit_bytes=10 << 20),
        name="final_step",
    )(prior, returned, spreading_coefficient)


def solution(mesh):
    placed = (
        P("mem", "state", None),
        P("state", None),
        P("state", None, None),
        P("state", None, None),
        P(),
        P("state", None),
        P("state", None),
    )
    return jax.shard_map(
        body, mesh=mesh, in_specs=placed, out_specs=P("mem", "state", None), check_vma=False
    )
```

```python
import jax
import jax.numpy as jnp
from jax import lax
from jax.experimental import pallas as pl
from jax.experimental.pallas import tpu as pltpu
from jax.sharding import PartitionSpec as P

F32, BF16 = jnp.float32, jnp.bfloat16
TILE = 128
SLOTS = 4
FSTEPS = 4
HALO = FSTEPS + 1
VMEM = pl.BlockSpec(memory_space=pltpu.VMEM)
SMEM = pl.BlockSpec(memory_space=pltpu.SMEM)
HBM = pl.BlockSpec(memory_space=pltpu.HBM)


def pack_obs_kernel(anom_ref, weight_ref, out_ref, token_ref, held_ref, sem):
    members = anom_ref.shape[2]
    core = lax.rem(lax.axis_index("mem"), 2)
    for kind, ref in enumerate((anom_ref, weight_ref)):

        @pl.when(core == kind)
        def _(kind=kind, ref=ref):
            copy = pltpu.make_async_copy(ref.at[0], held_ref, sem.at[kind])
            copy.start()
            copy.wait()
            for q in range(members // TILE):
                part = held_ref[:, q * TILE : (q + 1) * TILE]
                out_ref[0, q * TILE : (q + 1) * TILE, :] = part if kind == 0 else part.T


def pack_halo_kernel(first_ref, last_ref, coef_ref, block_ref, taper_ref, after_ref, up_ref, down_ref):
    members, depth, columns = first_ref.shape
    rows = coef_ref.shape[0]
    tiles = block_ref.shape[1]
    lane = lax.broadcasted_iota(jnp.int32, (8, columns), 1)
    for out_ref, x_ref, start, row0, tile0 in (
        (up_ref, first_ref, 0, 0, 0),
        (down_ref, last_ref, depth - HALO, rows - HALO, tiles - 2),
    ):
        for r in range(HALO):
            out_ref[r * members : (r + 1) * members, :] = x_ref[:, start + r, :]
        ids = jnp.zeros((8, columns), jnp.int32)
        for t in range(2):
            for k in range(SLOTS):
                ids = jnp.where(lane == t * SLOTS + k, block_ref[k, tile0 + t], ids)
                ids = jnp.where(lane == 8 + t * SLOTS + k, taper_ref[k, tile0 + t], ids)
        out_ref[HALO * members :, :] = ids.astype(F32)
        out_ref[HALO * members : HALO * members + HALO, :] = coef_ref[row0 : row0 + HALO, :]


def stepped(mid, one_side, other_side, coef):
    chunk, columns = mid.shape
    beside = one_side + other_side + pltpu.roll(mid, 1, 1) + pltpu.roll(mid, columns - 1, 1)
    delta = (beside - 4.0 * mid).reshape(chunk // 8, 8, columns)
    return mid + (coef[None] * delta).reshape(chunk, columns)


def split_tile(value, slot, members, pay_ref, mean_ref):
    mean = jnp.sum(value, axis=0, keepdims=True) * (1.0 / members)
    pay_ref[slot * members : (slot + 1) * members, :] = (value - mean).astype(BF16)
    high = mean.astype(BF16).astype(F32)
    middle = (mean - high).astype(BF16).astype(F32)
    mean_ref[3 * slot : 3 * slot + 1, :] = high
    mean_ref[3 * slot + 1 : 3 * slot + 2, :] = middle
    mean_ref[3 * slot + 2 : 3 * slot + 3, :] = mean - high - middle


def interior_kernel(x_ref, coef_ref, taper_ref, token_ref, prior_ref, out_ref, edge_ref, mean_ref, turned_out, a_ref, b_ref, c_ref, pay_ref, turned_ref, sems):
    members, rows, columns = x_ref.shape
    group = out_ref.shape[0]
    per = rows // group
    for r in range(rows):
        c_ref[r] = jnp.broadcast_to(coef_ref[r : r + 1, :], (8, columns))
    chunk = 16

    def advance(number, carry):
        here = pl.ds(pl.multiple_of(number * chunk, chunk), chunk)
        for r in range(rows):
            a_ref[r, here, :] = x_ref[here, r, :]
        src, dst = a_ref, b_ref
        for step in range(1, FSTEPS + 1):
            done = step - 1
            for i, r in enumerate((done, done + 1, rows - 1 - done, rows - 2 - done)):
                edge_ref[4 * done + i, here, :] = src[r, here, :]
            for r in range(step, rows - step):
                dst[r, here, :] = stepped(src[r, here, :], src[r - 1, here, :], src[r + 1, here, :], c_ref[r])
            src, dst = dst, src
        return carry

    lax.fori_loop(0, members // chunk, advance, 0)
    src = a_ref if FSTEPS % 2 == 0 else b_ref
    inner = rows - 2 * FSTEPS
    copies = [pltpu.make_async_copy(src.at[pl.ds(FSTEPS, inner)], prior_ref.at[pl.ds(FSTEPS + 1, inner)], sems.at[0])]
    copies[0].start()
    mean_ref[...] = jnp.zeros_like(mean_ref)
    for j in range(1, group - 1):
        for i in range(per):
            for half in range(2):
                value = src[j * per + i, :, half * TILE : (half + 1) * TILE]
                split_tile(value, 2 * i + half, members, pay_ref.at[j], mean_ref.at[j])
        copies.append(pltpu.make_async_copy(pay_ref.at[j], out_ref.at[j, pl.ds(0, 2 * per * members)], sems.at[j]))
        copies[-1].start()
    for i in range(taper_ref.shape[0]):
        turned_ref[i] = taper_ref[i].T
    copies.append(pltpu.make_async_copy(turned_ref, turned_out, sems.at[group]))
    copies[-1].start()
    for copy in copies:
        copy.wait()


def edge_kernel(above_ref, below_ref, coef_ref, edge_ref, mean_ref, prior_in, pay_in, prior_ref, out_ref, token_ref, a_ref, b_ref, c_ref, pay_ref, m_ref, last_ref, sems):
    rows, columns = coef_ref.shape
    members = last_ref.shape[2]
    group, size, _ = out_ref.shape
    per = rows // group
    tiles = 2 * per + 1
    halos = (above_ref, below_ref)
    for side in range(2):
        for t in range(HALO + FSTEPS):
            if t < HALO:
                r = HALO * members + (t if side == 0 else HALO - 1 - t)
                row = halos[side][r : r + 1, :]
            else:
                r = t - HALO if side == 0 else rows - 1 - (t - HALO)
                row = coef_ref[r : r + 1, :]
            c_ref[side, t] = jnp.broadcast_to(row, (8, columns))
    chunk = 16

    def advance(number, carry):
        here = pl.ds(pl.multiple_of(number * chunk, chunk), chunk)
        for side in range(2):

            def value(step, t, side=side):
                if t > step + HALO - 1:
                    return edge_ref[4 * step + 2 * side + t - step - HALO, here, :]
                if step == 0:
                    r = t if side == 0 else HALO - 1 - t
                    return halos[side][pl.ds(pl.multiple_of(r * members + number * chunk, chunk), chunk), :]
                return (a_ref, b_ref)[step % 2][side, t, here, :]

            for step in range(1, FSTEPS + 1):
                for t in range(step, step + HALO):
                    new = stepped(value(step - 1, t), value(step - 1, t - 1), value(step - 1, t + 1), c_ref[side, t])
                    if step < FSTEPS:
                        (a_ref, b_ref)[step % 2][side, t, here, :] = new
                    else:
                        last_ref[side, t - FSTEPS if side == 0 else 2 * FSTEPS - t, here, :] = new
        return carry

    lax.fori_loop(0, members // chunk, advance, 0)
    copies = [
        pltpu.make_async_copy(last_ref.at[0], prior_ref.at[pl.ds(0, HALO)], sems.at[0]),
        pltpu.make_async_copy(last_ref.at[1], prior_ref.at[pl.ds(rows + 2 - HALO, HALO)], sems.at[1]),
    ]
    for copy in copies:
        copy.start()
    m_ref[...] = mean_ref[...]
    extra = tiles - 1
    for j in range(group):
        if j in (0, group - 1):
            for i in range(per):
                for half in range(2):
                    row = last_ref[0, i + 1] if j == 0 else last_ref[1, i]
                    split_tile(row[:, half * TILE : (half + 1) * TILE], 2 * i + half, members, pay_ref.at[j], m_ref.at[j])
        if j < 4:
            row = last_ref[0, 0] if j < 2 else last_ref[1, HALO - 1]
            split_tile(row[:, (j % 2) * TILE : (j % 2 + 1) * TILE], extra, members, pay_ref.at[j], m_ref.at[j])
        else:
            pay_ref[j, extra * members : tiles * members, :] = jnp.zeros((members, TILE), BF16)
        pay_ref[j, tiles * members :, :] = m_ref[j].astype(BF16)
        first = 0 if j in (0, group - 1) else extra * members
        part = pl.ds(first, size - first)
        copies.append(pltpu.make_async_copy(pay_ref.at[j, part], out_ref.at[j, part], sems.at[2 + j]))
        copies[-1].start()
    for copy in copies:
        copy.wait()


def fill(pieces, obs_ref):
    core = lax.rem(lax.axis_index("mem"), 2)
    for side in range(2):
        start = 0
        kind = core if side == 0 else 1 - core
        for piece in pieces[side * len(pieces) // 2 : (side + 1) * len(pieces) // 2]:

            def keep(i, carry, piece=piece, start=start, kind=kind):
                obs_ref[kind, start + i] = piece[i]
                return carry

            lax.fori_loop(0, piece.shape[0], keep, 0)
            start += piece.shape[0]


def collect_kernel(recv_ref, *rest):
    pieces, (obs_ref, centred_ref) = rest[:-2], rest[-2:]
    group, size, _ = recv_ref.shape
    tiles, members, _ = centred_ref.shape
    count = members // group
    fill(pieces, obs_ref)
    parts = recv_ref[:, size - 32 :, :].astype(F32)
    for t in range(tiles):
        own = parts[:, 3 * t, :] + parts[:, 3 * t + 1, :] + parts[:, 3 * t + 2, :]
        delta = own - jnp.mean(own, axis=0, keepdims=True)
        local = recv_ref[:, t * count : (t + 1) * count, :].astype(F32)
        centred_ref[t] = (local + delta[:, None, :]).astype(BF16).reshape(members, TILE)


def analysis_kernel(anom_at_ref, weight_at_ref, tapers_ref, taper_ref, centred_ref, early_ref, *rest):
    pieces, (ret_ref, late_ref) = rest[:-2], rest[-2:]
    tiles, members, _ = centred_ref.shape
    group = ret_ref.shape[0]
    count = members // group
    early = early_ref.shape[1]
    fill(pieces, late_ref)

    def block(kind, at):
        near = early_ref[kind, jnp.minimum(at, early - 1)]
        far = late_ref[kind, jnp.maximum(at - early, 0)]
        return jnp.where(at < early, near, far)

    def one(t, carry):
        anoms, weights = [], []
        for k in range(SLOTS):
            anom = block(0, anom_at_ref[t, k])
            anoms.append(jnp.concatenate([anom[q * TILE : (q + 1) * TILE] for q in range(members // TILE)], axis=1))
            weights.append(block(1, weight_at_ref[t, k]))
        cov = jnp.dot(jnp.concatenate(anoms, axis=0), centred_ref[t], preferred_element_type=F32) * (1.0 / (members - 1.0))
        tapered = [
            (taper_ref[tapers_ref[t, k]] * cov[k * TILE : (k + 1) * TILE]).astype(BF16) for k in range(SLOTS)
        ]
        total = jnp.dot(jnp.concatenate(weights, axis=1), jnp.concatenate(tapered, axis=0), preferred_element_type=F32)
        here = pl.ds(pl.multiple_of(t * count, count), count)
        ret_ref[:, here, :] = total.astype(BF16).reshape(group, count, TILE)
        return carry

    lax.fori_loop(0, tiles, one, 0, unroll=3)


def final_kernel(prior_ref, inc_ref, coef_ref, out_ref, v_ref):
    members, depth, columns = out_ref.shape
    group, size, _ = inc_ref.shape
    rows = prior_ref.shape[0] - 2
    per = rows // group
    extra = size // members - 1
    i, steps = pl.program_id(0), pl.num_programs(0)

    def put(index, j, slot, half):
        lanes = slice(half * TILE, (half + 1) * TILE)
        here = pl.ds(pl.multiple_of(slot * members, members), members)
        v_ref[index, :, lanes] = prior_ref[i * depth + index, :, lanes] + inc_ref[j, here, :].astype(F32)

    first = i * (depth // per)
    for half in range(2):
        top, bottom = i == 0, i == steps - 1
        put(0, jnp.where(top, half, first - 1), jnp.where(top, extra, 2 * (per - 1) + half), half)
        put(depth + 1, jnp.where(bottom, 2 + half, first + depth // per), jnp.where(bottom, extra, half), half)
        for r in range(depth):
            put(r + 1, first + r // per, 2 * (r % per) + half, half)
    coef = coef_ref[...]
    for r in range(depth):
        mid = v_ref[r + 1]
        beside = v_ref[r] + v_ref[r + 2] + pltpu.roll(mid, 1, 1) + pltpu.roll(mid, columns - 1, 1)
        out_ref[:, r, :] = mid + coef[r : r + 1, :] * (beside - 4.0 * mid)


AXES = ("mem", "state")


def fetch(value, mesh, source):
    xs, ys, zs = mesh
    pairs = []
    for x in range(xs):
        for c in range(2):
            for y in range(ys):
                for z in range(zs):
                    a, b, d, e = source(x, c, y, z)
                    pairs.append((((a * 2 + b) * ys + d % ys) * zs + e % zs, ((x * 2 + c) * ys + y) * zs + z))
    return lax.ppermute(value, AXES, pairs)


def ring(first, step):
    return lambda x, c, y, z: (x, c, y + step, z) if (c == 0) == first else (x, c, y, z + step)


def other_core(x, c, y, z):
    return (x, 1 - c, y, z)


TOKEN = jax.ShapeDtypeStruct((8, TILE), F32)


def join(operands, name, after):
    count = len(operands)

    def kernel(*refs):
        outs = refs[count + len(after) :]
        core = lax.rem(lax.axis_index("mem"), 2)
        for a in range(count):
            for i in range(2):
                outs[0][i * count + a] = refs[a][i]
            outs[1][a] = refs[a][0]
            outs[2][a] = refs[a][core]

    shapes = [(n, *operands[0].shape[1:]) for n in (2 * count, count, count)]
    return pl.pallas_call(
        kernel,
        out_shape=[jax.ShapeDtypeStruct(shape, BF16) for shape in shapes],
        in_specs=[VMEM] * count + [HBM] * len(after),
        out_specs=[VMEM] * len(shapes),
        compiler_params=pltpu.CompilerParams(vmem_limit_bytes=6 << 20),
        name=name,
    )(*operands, *after)


def join_two_kernel(own_ref, far_ref, held_ref, token_ref):
    held_ref[0] = own_ref[0]
    held_ref[1] = far_ref[0]


def gather_first(own, mesh):
    far = fetch(own, mesh, lambda x, c, y, z: (x, c, y, z + 4))
    return pl.pallas_call(
        join_two_kernel,
        out_shape=[jax.ShapeDtypeStruct((2, *own.shape[1:]), BF16), TOKEN],
        in_specs=[VMEM] * 2,
        out_specs=[VMEM, HBM],
        compiler_params=pltpu.CompilerParams(vmem_limit_bytes=6 << 20),
        name="join_two",
    )(own, far)


def gather_second(held, mesh, after):
    p, m = (fetch(held, mesh, ring(True, step)) for step in (1, -1))
    q = fetch(held, mesh, lambda x, c, y, z: (x, c, y + 2, z) if c == 0 else (x, c, y, z + 2 - 4 * (z % 2)))
    return join([held, p, m, q], "join_eight", after)


def gather_rest(held, first, second, mesh):
    p, m = (fetch(held, mesh, ring(False, step)) for step in (1, -1))
    q = fetch(first, mesh, ring(False, 2))
    r = fetch(second, mesh, ring(False, -2))
    own = [held, p, m, q, r]
    return own, [fetch(v, mesh, other_core) for v in own]


def places(block, y, z):
    dy, dz = (block // 8 - y) % 4, (block % 8 - z) % 8
    low = dz % 4
    gray_y, gray_z = dy ^ (dy >> 1), low ^ (low >> 1)
    high = (dz // 4) ^ (low == 3).astype(jnp.int32)
    turned = high ^ jnp.where(low == 2, z % 2, 0)
    return 8 * gray_z + 4 * high + gray_y, 8 * gray_y + 4 * turned + gray_z


def body(ensemble, spreading_coefficient, obs_anom, obs_weight, taper_table, obs_block, taper_id):
    members, rows, columns = ensemble.shape
    group = lax.axis_size("mem")
    states = lax.axis_size("state")
    per = rows // group
    tiles = 2 * per + 1
    size = tiles * members + 32

    j, at = lax.axis_index("mem"), lax.axis_index("state")
    chips = (group // 2, states // 8, 8)
    packed, obs_packed = pl.pallas_call(
        pack_obs_kernel,
        out_shape=[jax.ShapeDtypeStruct((1, obs_anom.shape[2], TILE), BF16), TOKEN],
        in_specs=[HBM] * 2,
        out_specs=[VMEM, HBM],
        scratch_shapes=[pltpu.VMEM(obs_anom.shape[1:], BF16), pltpu.SemaphoreType.DMA((2,))],
        name="pack_obs",
    )(obs_anom, obs_weight)
    up, down = pl.pallas_call(
        pack_halo_kernel,
        grid=(1,),
        out_shape=[jax.ShapeDtypeStruct((HALO * members + 8, columns), F32)] * 2,
        in_specs=[
            pl.BlockSpec((members, 8, columns), lambda i: (0, 0, 0)),
            pl.BlockSpec((members, 8, columns), lambda i: (0, rows // 8 - 1, 0)),
            VMEM,
            SMEM,
            SMEM,
            HBM,
        ],
        out_specs=[VMEM] * 2,
        name="pack_halo",
    )(ensemble, ensemble, spreading_coefficient, obs_block.T, taper_id.T, obs_packed)
    below = lax.ppermute(up, "state", [(i + 1, i) for i in range(states - 1)])
    above = lax.ppermute(down, "state", [(i, i + 1) for i in range(states - 1)])

    held, started = gather_first(packed, chips)
    row = (members, columns)
    prior, payload, edges, means, turned = pl.pallas_call(
        interior_kernel,
        out_shape=[
            pltpu.HBM((rows + 2, *row), F32),
            pltpu.HBM((group, size, TILE), BF16),
            jax.ShapeDtypeStruct((4 * FSTEPS, *row), F32),
            jax.ShapeDtypeStruct((group, 32, TILE), F32),
            pltpu.HBM(taper_table.shape, F32),
        ],
        in_specs=[VMEM] * 3 + [HBM],
        out_specs=[HBM] * 2 + [VMEM] * 2 + [HBM],
        scratch_shapes=[
            pltpu.VMEM((rows, *row), F32),
            pltpu.VMEM((rows, *row), F32),
            pltpu.VMEM((rows, 8, columns), F32),
            pltpu.VMEM((group, 2 * per * members, TILE), BF16),
            pltpu.VMEM(taper_table.shape, F32),
            pltpu.SemaphoreType.DMA((group + 1,)),
        ],
        compiler_params=pltpu.CompilerParams(vmem_limit_bytes=14 << 20),
        name="forecast_interior",
    )(ensemble, spreading_coefficient, taper_table, started)
    prior, payload, forecast_done = pl.pallas_call(
        edge_kernel,
        out_shape=[pltpu.HBM(prior.shape, F32), pltpu.HBM(payload.shape, BF16), TOKEN],
        in_specs=[VMEM] * 5 + [HBM] * 2,
        out_specs=[HBM] * 3,
        input_output_aliases={5: 0, 6: 1},
        scratch_shapes=[
            pltpu.VMEM((2, HALO + FSTEPS, *row), F32),
            pltpu.VMEM((2, HALO + FSTEPS, *row), F32),
            pltpu.VMEM((2, HALO + FSTEPS, 8, columns), F32),
            pltpu.VMEM((group, size, TILE), BF16),
            pltpu.VMEM((group, 32, TILE), F32),
            pltpu.VMEM((2, HALO, *row), F32),
            pltpu.SemaphoreType.DMA((group + 2,)),
        ],
        compiler_params=pltpu.CompilerParams(vmem_limit_bytes=14 << 20),
        name="forecast_edges",
    )(above, below, spreading_coefficient, edges, means, prior, payload)
    held, first, second = gather_second(held, chips, [forecast_done])
    own, swapped = gather_rest(held, first, second, chips)
    gathered = lax.all_to_all(payload, "mem", split_axis=0, concat_axis=0, tiled=True)

    edge = jnp.where(j < 2, above[-1, :16], below[-1, :16])
    edge = jnp.where(j % 2 == 0, edge.reshape(-1, 4)[:3:2], edge.reshape(-1, 4)[1:4:2]).astype(jnp.int32)
    mine = 2 * per * j
    blocks = jnp.concatenate([lax.dynamic_slice_in_dim(obs_block, mine, 2 * per, 0), edge[0:1]], axis=0)
    tapers = jnp.concatenate([lax.dynamic_slice_in_dim(taper_id, mine, 2 * per, 0), edge[1:2]], axis=0)

    anom_at, weight_at = places(blocks, at // 8, at % 8)
    late = 2
    early = own[:-late] + swapped[:-late]
    held_early, centred = pl.pallas_call(
        collect_kernel,
        out_shape=[
            jax.ShapeDtypeStruct((2, sum(v.shape[0] for v in own[:-late]), *packed.shape[1:]), BF16),
            jax.ShapeDtypeStruct((tiles, group * members, TILE), BF16),
        ],
        in_specs=[VMEM] * (1 + len(early)),
        out_specs=[VMEM] * 2,
        compiler_params=pltpu.CompilerParams(vmem_limit_bytes=18 << 20),
        name="collect",
    )(gathered, *early)
    increments = pl.pallas_call(
        analysis_kernel,
        out_shape=jax.ShapeDtypeStruct((group, tiles * members, TILE), BF16),
        in_specs=[SMEM] * 3 + [VMEM] * (3 + 2 * late),
        out_specs=VMEM,
        scratch_shapes=[pltpu.VMEM((2, sum(v.shape[0] for v in own[-late:]), *packed.shape[1:]), BF16)],
        compiler_params=pltpu.CompilerParams(vmem_limit_bytes=18 << 20),
        name="analysis",
    )(anom_at, weight_at, tapers, turned, centred, held_early, *own[-late:], *swapped[-late:])
    returned = lax.all_to_all(increments, "mem", split_axis=0, concat_axis=0, tiled=True)

    return pl.pallas_call(
        final_kernel,
        grid=(rows // 8,),
        out_shape=jax.ShapeDtypeStruct((members, rows, columns), F32),
        in_specs=[VMEM] * 2 + [pl.BlockSpec((8, columns), lambda i: (i, 0))],
        out_specs=pl.BlockSpec((members, 8, columns), lambda i: (0, i, 0)),
        scratch_shapes=[pltpu.VMEM((10, members, columns), F32)],
        compiler_params=pltpu.CompilerParams(vmem_limit_bytes=10 << 20),
        name="final_step",
    )(prior, returned, spreading_coefficient)


def solution(mesh):
    placed = (
        P("mem", "state", None),
        P("state", None),
        P("state", None, None),
        P("state", None, None),
        P(),
        P("state", None),
        P("state", None),
    )
    return jax.shard_map(
        body, mesh=mesh, in_specs=placed, out_specs=P("mem", "state", None), check_vma=False
    )
```

```python
import jax
import jax.numpy as jnp
from jax import lax
from jax.experimental import pallas as pl
from jax.experimental.pallas import tpu as pltpu
from jax.sharding import PartitionSpec as P

F32, BF16 = jnp.float32, jnp.bfloat16
TILE = 128
SLOTS = 4
FSTEPS = 4
HALO = FSTEPS + 1
VMEM = pl.BlockSpec(memory_space=pltpu.VMEM)
SMEM = pl.BlockSpec(memory_space=pltpu.SMEM)
HBM = pl.BlockSpec(memory_space=pltpu.HBM)


def pack_obs_kernel(anom_ref, weight_ref, out_ref, token_ref, held_ref, sem):
    members = anom_ref.shape[2]
    core = lax.rem(lax.axis_index("mem"), 2)
    for kind, ref in enumerate((anom_ref, weight_ref)):

        @pl.when(core == kind)
        def _(kind=kind, ref=ref):
            copy = pltpu.make_async_copy(ref.at[0], held_ref, sem.at[kind])
            copy.start()
            copy.wait()
            for q in range(members // TILE):
                part = held_ref[:, q * TILE : (q + 1) * TILE]
                out_ref[0, q * TILE : (q + 1) * TILE, :] = part if kind == 0 else part.T


def pack_halo_kernel(first_ref, last_ref, coef_ref, block_ref, taper_ref, after_ref, up_ref, down_ref):
    members, depth, columns = first_ref.shape
    rows = coef_ref.shape[0]
    tiles = block_ref.shape[1]
    lane = lax.broadcasted_iota(jnp.int32, (8, columns), 1)
    for out_ref, x_ref, start, row0, tile0 in (
        (up_ref, first_ref, 0, 0, 0),
        (down_ref, last_ref, depth - HALO, rows - HALO, tiles - 2),
    ):
        for r in range(HALO):
            out_ref[r * members : (r + 1) * members, :] = x_ref[:, start + r, :]
        ids = jnp.zeros((8, columns), jnp.int32)
        for t in range(2):
            for k in range(SLOTS):
                ids = jnp.where(lane == t * SLOTS + k, block_ref[k, tile0 + t], ids)
                ids = jnp.where(lane == 8 + t * SLOTS + k, taper_ref[k, tile0 + t], ids)
        out_ref[HALO * members :, :] = ids.astype(F32)
        out_ref[HALO * members : HALO * members + HALO, :] = coef_ref[row0 : row0 + HALO, :]


def stepped(mid, one_side, other_side, coef):
    chunk, columns = mid.shape
    beside = one_side + other_side + pltpu.roll(mid, 1, 1) + pltpu.roll(mid, columns - 1, 1)
    delta = (beside - 4.0 * mid).reshape(chunk // 8, 8, columns)
    return mid + (coef[None] * delta).reshape(chunk, columns)


def split_tile(value, slot, members, pay_ref, mean_ref):
    mean = jnp.sum(value, axis=0, keepdims=True) * (1.0 / members)
    pay_ref[slot * members : (slot + 1) * members, :] = (value - mean).astype(BF16)
    high = mean.astype(BF16).astype(F32)
    middle = (mean - high).astype(BF16).astype(F32)
    mean_ref[3 * slot : 3 * slot + 1, :] = high
    mean_ref[3 * slot + 1 : 3 * slot + 2, :] = middle
    mean_ref[3 * slot + 2 : 3 * slot + 3, :] = mean - high - middle


def interior_kernel(x_ref, coef_ref, taper_ref, token_ref, prior_ref, out_ref, edge_ref, mean_ref, turned_out, a_ref, b_ref, c_ref, pay_ref, turned_ref, sems):
    members, rows, columns = x_ref.shape
    group = out_ref.shape[0]
    per = rows // group
    for r in range(rows):
        c_ref[r] = jnp.broadcast_to(coef_ref[r : r + 1, :], (8, columns))
    chunk = 16

    def advance(number, carry):
        here = pl.ds(pl.multiple_of(number * chunk, chunk), chunk)
        for r in range(rows):
            a_ref[r, here, :] = x_ref[here, r, :]
        src, dst = a_ref, b_ref
        for step in range(1, FSTEPS + 1):
            done = step - 1
            for i, r in enumerate((done, done + 1, rows - 1 - done, rows - 2 - done)):
                edge_ref[4 * done + i, here, :] = src[r, here, :]
            for r in range(step, rows - step):
                dst[r, here, :] = stepped(src[r, here, :], src[r - 1, here, :], src[r + 1, here, :], c_ref[r])
            src, dst = dst, src
        return carry

    lax.fori_loop(0, members // chunk, advance, 0)
    src = a_ref if FSTEPS % 2 == 0 else b_ref
    inner = rows - 2 * FSTEPS
    copies = [pltpu.make_async_copy(src.at[pl.ds(FSTEPS, inner)], prior_ref.at[pl.ds(FSTEPS + 1, inner)], sems.at[0])]
    copies[0].start()
    mean_ref[...] = jnp.zeros_like(mean_ref)
    for j in range(1, group - 1):
        for i in range(per):
            for half in range(2):
                value = src[j * per + i, :, half * TILE : (half + 1) * TILE]
                split_tile(value, 2 * i + half, members, pay_ref.at[j], mean_ref.at[j])
        copies.append(pltpu.make_async_copy(pay_ref.at[j], out_ref.at[j, pl.ds(0, 2 * per * members)], sems.at[j]))
        copies[-1].start()
    for i in range(taper_ref.shape[0]):
        turned_ref[i] = taper_ref[i].T
    copies.append(pltpu.make_async_copy(turned_ref, turned_out, sems.at[group]))
    copies[-1].start()
    for copy in copies:
        copy.wait()


def edge_kernel(above_ref, below_ref, coef_ref, edge_ref, mean_ref, prior_in, pay_in, prior_ref, out_ref, token_ref, a_ref, b_ref, c_ref, pay_ref, m_ref, last_ref, sems):
    rows, columns = coef_ref.shape
    members = last_ref.shape[2]
    group, size, _ = out_ref.shape
    per = rows // group
    tiles = 2 * per + 1
    halos = (above_ref, below_ref)
    for side in range(2):
        for t in range(HALO + FSTEPS):
            if t < HALO:
                r = HALO * members + (t if side == 0 else HALO - 1 - t)
                row = halos[side][r : r + 1, :]
            else:
                r = t - HALO if side == 0 else rows - 1 - (t - HALO)
                row = coef_ref[r : r + 1, :]
            c_ref[side, t] = jnp.broadcast_to(row, (8, columns))
    chunk = 16

    def advance(number, carry):
        here = pl.ds(pl.multiple_of(number * chunk, chunk), chunk)
        for side in range(2):

            def value(step, t, side=side):
                if t > step + HALO - 1:
                    return edge_ref[4 * step + 2 * side + t - step - HALO, here, :]
                if step == 0:
                    r = t if side == 0 else HALO - 1 - t
                    return halos[side][pl.ds(pl.multiple_of(r * members + number * chunk, chunk), chunk), :]
                return (a_ref, b_ref)[step % 2][side, t, here, :]

            for step in range(1, FSTEPS + 1):
                for t in range(step, step + HALO):
                    new = stepped(value(step - 1, t), value(step - 1, t - 1), value(step - 1, t + 1), c_ref[side, t])
                    if step < FSTEPS:
                        (a_ref, b_ref)[step % 2][side, t, here, :] = new
                    else:
                        last_ref[side, t - FSTEPS if side == 0 else 2 * FSTEPS - t, here, :] = new
        return carry

    lax.fori_loop(0, members // chunk, advance, 0)
    copies = [
        pltpu.make_async_copy(last_ref.at[0], prior_ref.at[pl.ds(0, HALO)], sems.at[0]),
        pltpu.make_async_copy(last_ref.at[1], prior_ref.at[pl.ds(rows + 2 - HALO, HALO)], sems.at[1]),
    ]
    for copy in copies:
        copy.start()
    m_ref[...] = mean_ref[...]
    extra = tiles - 1
    for j in range(group):
        if j in (0, group - 1):
            for i in range(per):
                for half in range(2):
                    row = last_ref[0, i + 1] if j == 0 else last_ref[1, i]
                    split_tile(row[:, half * TILE : (half + 1) * TILE], 2 * i + half, members, pay_ref.at[j], m_ref.at[j])
        if j < 4:
            row = last_ref[0, 0] if j < 2 else last_ref[1, HALO - 1]
            split_tile(row[:, (j % 2) * TILE : (j % 2 + 1) * TILE], extra, members, pay_ref.at[j], m_ref.at[j])
        else:
            pay_ref[j, extra * members : tiles * members, :] = jnp.zeros((members, TILE), BF16)
        pay_ref[j, tiles * members :, :] = m_ref[j].astype(BF16)
        first = 0 if j in (0, group - 1) else extra * members
        part = pl.ds(first, size - first)
        copies.append(pltpu.make_async_copy(pay_ref.at[j, part], out_ref.at[j, part], sems.at[2 + j]))
        copies[-1].start()
    for copy in copies:
        copy.wait()


def fill(pieces, obs_ref):
    core = lax.rem(lax.axis_index("mem"), 2)
    for side in range(2):
        start = 0
        kind = core if side == 0 else 1 - core
        for piece in pieces[side * len(pieces) // 2 : (side + 1) * len(pieces) // 2]:

            def keep(i, carry, piece=piece, start=start, kind=kind):
                obs_ref[kind, start + i] = piece[i]
                return carry

            lax.fori_loop(0, piece.shape[0], keep, 0)
            start += piece.shape[0]


def collect_kernel(recv_ref, *rest):
    pieces, (obs_ref, centred_ref) = rest[:-2], rest[-2:]
    group, size, _ = recv_ref.shape
    tiles, members, _ = centred_ref.shape
    count = members // group
    fill(pieces, obs_ref)
    parts = recv_ref[:, size - 32 :, :].astype(F32)
    for t in range(tiles):
        own = parts[:, 3 * t, :] + parts[:, 3 * t + 1, :] + parts[:, 3 * t + 2, :]
        delta = own - jnp.mean(own, axis=0, keepdims=True)
        local = recv_ref[:, t * count : (t + 1) * count, :].astype(F32)
        centred_ref[t] = (local + delta[:, None, :]).astype(BF16).reshape(members, TILE)


def analysis_kernel(anom_at_ref, weight_at_ref, tapers_ref, taper_ref, centred_ref, early_ref, *rest):
    pieces, (ret_ref, late_ref) = rest[:-2], rest[-2:]
    tiles, members, _ = centred_ref.shape
    group = ret_ref.shape[0]
    count = members // group
    early = early_ref.shape[1]
    fill(pieces, late_ref)

    def block(kind, at):
        near = early_ref[kind, jnp.minimum(at, early - 1)]
        far = late_ref[kind, jnp.maximum(at - early, 0)]
        return jnp.where(at < early, near, far)

    def one(t, carry):
        anoms, weights = [], []
        for k in range(SLOTS):
            anom = block(0, anom_at_ref[t, k])
            anoms.append(jnp.concatenate([anom[q * TILE : (q + 1) * TILE] for q in range(members // TILE)], axis=1))
            weights.append(block(1, weight_at_ref[t, k]))
        cov = jnp.dot(jnp.concatenate(anoms, axis=0), centred_ref[t], preferred_element_type=F32) * (1.0 / (members - 1.0))
        tapered = [
            (taper_ref[tapers_ref[t, k]] * cov[k * TILE : (k + 1) * TILE]).astype(BF16) for k in range(SLOTS)
        ]
        total = jnp.dot(jnp.concatenate(weights, axis=1), jnp.concatenate(tapered, axis=0), preferred_element_type=F32)
        here = pl.ds(pl.multiple_of(t * count, count), count)
        ret_ref[:, here, :] = total.astype(BF16).reshape(group, count, TILE)
        return carry

    lax.fori_loop(0, tiles, one, 0, unroll=9)


def final_kernel(prior_ref, inc_ref, coef_ref, out_ref, v_ref):
    members, depth, columns = out_ref.shape
    group, size, _ = inc_ref.shape
    rows = prior_ref.shape[0] - 2
    per = rows // group
    extra = size // members - 1
    i, steps = pl.program_id(0), pl.num_programs(0)

    def put(index, j, slot, half):
        lanes = slice(half * TILE, (half + 1) * TILE)
        here = pl.ds(pl.multiple_of(slot * members, members), members)
        v_ref[index, :, lanes] = prior_ref[i * depth + index, :, lanes] + inc_ref[j, here, :].astype(F32)

    first = i * (depth // per)
    for half in range(2):
        top, bottom = i == 0, i == steps - 1
        put(0, jnp.where(top, half, first - 1), jnp.where(top, extra, 2 * (per - 1) + half), half)
        put(depth + 1, jnp.where(bottom, 2 + half, first + depth // per), jnp.where(bottom, extra, half), half)
        for r in range(depth):
            put(r + 1, first + r // per, 2 * (r % per) + half, half)
    coef = coef_ref[...]
    for r in range(depth):
        mid = v_ref[r + 1]
        beside = v_ref[r] + v_ref[r + 2] + pltpu.roll(mid, 1, 1) + pltpu.roll(mid, columns - 1, 1)
        out_ref[:, r, :] = mid + coef[r : r + 1, :] * (beside - 4.0 * mid)


AXES = ("mem", "state")


def fetch(value, mesh, source):
    xs, ys, zs = mesh
    pairs = []
    for x in range(xs):
        for c in range(2):
            for y in range(ys):
                for z in range(zs):
                    a, b, d, e = source(x, c, y, z)
                    pairs.append((((a * 2 + b) * ys + d % ys) * zs + e % zs, ((x * 2 + c) * ys + y) * zs + z))
    return lax.ppermute(value, AXES, pairs)


def ring(first, step):
    return lambda x, c, y, z: (x, c, y + step, z) if (c == 0) == first else (x, c, y, z + step)


def other_core(x, c, y, z):
    return (x, 1 - c, y, z)


TOKEN = jax.ShapeDtypeStruct((8, TILE), F32)


def join(operands, name, after):
    count = len(operands)

    def kernel(*refs):
        outs = refs[count + len(after) :]
        core = lax.rem(lax.axis_index("mem"), 2)
        for a in range(count):
            for i in range(2):
                outs[0][i * count + a] = refs[a][i]
            outs[1][a] = refs[a][0]
            outs[2][a] = refs[a][core]

    shapes = [(n, *operands[0].shape[1:]) for n in (2 * count, count, count)]
    return pl.pallas_call(
        kernel,
        out_shape=[jax.ShapeDtypeStruct(shape, BF16) for shape in shapes],
        in_specs=[VMEM] * count + [HBM] * len(after),
        out_specs=[VMEM] * len(shapes),
        compiler_params=pltpu.CompilerParams(vmem_limit_bytes=6 << 20),
        name=name,
    )(*operands, *after)


def join_two_kernel(own_ref, far_ref, held_ref, token_ref):
    held_ref[0] = own_ref[0]
    held_ref[1] = far_ref[0]


def gather_first(own, mesh):
    far = fetch(own, mesh, lambda x, c, y, z: (x, c, y, z + 4))
    return pl.pallas_call(
        join_two_kernel,
        out_shape=[jax.ShapeDtypeStruct((2, *own.shape[1:]), BF16), TOKEN],
        in_specs=[VMEM] * 2,
        out_specs=[VMEM, HBM],
        compiler_params=pltpu.CompilerParams(vmem_limit_bytes=6 << 20),
        name="join_two",
    )(own, far)


def gather_second(held, mesh, after):
    p, m = (fetch(held, mesh, ring(True, step)) for step in (1, -1))
    q = fetch(held, mesh, lambda x, c, y, z: (x, c, y + 2, z) if c == 0 else (x, c, y, z + 2 - 4 * (z % 2)))
    return join([held, p, m, q], "join_eight", after)


def gather_rest(held, first, second, mesh):
    p, m = (fetch(held, mesh, ring(False, step)) for step in (1, -1))
    q = fetch(first, mesh, ring(False, 2))
    r = fetch(second, mesh, ring(False, -2))
    own = [held, p, m, q, r]
    return own, [fetch(v, mesh, other_core) for v in own]


def places(block, y, z):
    dy, dz = (block // 8 - y) % 4, (block % 8 - z) % 8
    low = dz % 4
    gray_y, gray_z = dy ^ (dy >> 1), low ^ (low >> 1)
    high = (dz // 4) ^ (low == 3).astype(jnp.int32)
    turned = high ^ jnp.where(low == 2, z % 2, 0)
    return 8 * gray_z + 4 * high + gray_y, 8 * gray_y + 4 * turned + gray_z


def body(ensemble, spreading_coefficient, obs_anom, obs_weight, taper_table, obs_block, taper_id):
    members, rows, columns = ensemble.shape
    group = lax.axis_size("mem")
    states = lax.axis_size("state")
    per = rows // group
    tiles = 2 * per + 1
    size = tiles * members + 32

    j, at = lax.axis_index("mem"), lax.axis_index("state")
    chips = (group // 2, states // 8, 8)
    packed, obs_packed = pl.pallas_call(
        pack_obs_kernel,
        out_shape=[jax.ShapeDtypeStruct((1, obs_anom.shape[2], TILE), BF16), TOKEN],
        in_specs=[HBM] * 2,
        out_specs=[VMEM, HBM],
        scratch_shapes=[pltpu.VMEM(obs_anom.shape[1:], BF16), pltpu.SemaphoreType.DMA((2,))],
        name="pack_obs",
    )(obs_anom, obs_weight)
    up, down = pl.pallas_call(
        pack_halo_kernel,
        grid=(1,),
        out_shape=[jax.ShapeDtypeStruct((HALO * members + 8, columns), F32)] * 2,
        in_specs=[
            pl.BlockSpec((members, 8, columns), lambda i: (0, 0, 0)),
            pl.BlockSpec((members, 8, columns), lambda i: (0, rows // 8 - 1, 0)),
            VMEM,
            SMEM,
            SMEM,
            HBM,
        ],
        out_specs=[VMEM] * 2,
        name="pack_halo",
    )(ensemble, ensemble, spreading_coefficient, obs_block.T, taper_id.T, obs_packed)
    below = lax.ppermute(up, "state", [(i + 1, i) for i in range(states - 1)])
    above = lax.ppermute(down, "state", [(i, i + 1) for i in range(states - 1)])

    held, started = gather_first(packed, chips)
    row = (members, columns)
    prior, payload, edges, means, turned = pl.pallas_call(
        interior_kernel,
        out_shape=[
            pltpu.HBM((rows + 2, *row), F32),
            pltpu.HBM((group, size, TILE), BF16),
            jax.ShapeDtypeStruct((4 * FSTEPS, *row), F32),
            jax.ShapeDtypeStruct((group, 32, TILE), F32),
            pltpu.HBM(taper_table.shape, F32),
        ],
        in_specs=[VMEM] * 3 + [HBM],
        out_specs=[HBM] * 2 + [VMEM] * 2 + [HBM],
        scratch_shapes=[
            pltpu.VMEM((rows, *row), F32),
            pltpu.VMEM((rows, *row), F32),
            pltpu.VMEM((rows, 8, columns), F32),
            pltpu.VMEM((group, 2 * per * members, TILE), BF16),
            pltpu.VMEM(taper_table.shape, F32),
            pltpu.SemaphoreType.DMA((group + 1,)),
        ],
        compiler_params=pltpu.CompilerParams(vmem_limit_bytes=14 << 20),
        name="forecast_interior",
    )(ensemble, spreading_coefficient, taper_table, started)
    prior, payload, forecast_done = pl.pallas_call(
        edge_kernel,
        out_shape=[pltpu.HBM(prior.shape, F32), pltpu.HBM(payload.shape, BF16), TOKEN],
        in_specs=[VMEM] * 5 + [HBM] * 2,
        out_specs=[HBM] * 3,
        input_output_aliases={5: 0, 6: 1},
        scratch_shapes=[
            pltpu.VMEM((2, HALO + FSTEPS, *row), F32),
            pltpu.VMEM((2, HALO + FSTEPS, *row), F32),
            pltpu.VMEM((2, HALO + FSTEPS, 8, columns), F32),
            pltpu.VMEM((group, size, TILE), BF16),
            pltpu.VMEM((group, 32, TILE), F32),
            pltpu.VMEM((2, HALO, *row), F32),
            pltpu.SemaphoreType.DMA((group + 2,)),
        ],
        compiler_params=pltpu.CompilerParams(vmem_limit_bytes=14 << 20),
        name="forecast_edges",
    )(above, below, spreading_coefficient, edges, means, prior, payload)
    held, first, second = gather_second(held, chips, [forecast_done])
    own, swapped = gather_rest(held, first, second, chips)
    gathered = lax.all_to_all(payload, "mem", split_axis=0, concat_axis=0, tiled=True)

    edge = jnp.where(j < 2, above[-1, :16], below[-1, :16])
    edge = jnp.where(j % 2 == 0, edge.reshape(-1, 4)[:3:2], edge.reshape(-1, 4)[1:4:2]).astype(jnp.int32)
    mine = 2 * per * j
    blocks = jnp.concatenate([lax.dynamic_slice_in_dim(obs_block, mine, 2 * per, 0), edge[0:1]], axis=0)
    tapers = jnp.concatenate([lax.dynamic_slice_in_dim(taper_id, mine, 2 * per, 0), edge[1:2]], axis=0)

    anom_at, weight_at = places(blocks, at // 8, at % 8)
    late = 2
    early = own[:-late] + swapped[:-late]
    held_early, centred = pl.pallas_call(
        collect_kernel,
        out_shape=[
            jax.ShapeDtypeStruct((2, sum(v.shape[0] for v in own[:-late]), *packed.shape[1:]), BF16),
            jax.ShapeDtypeStruct((tiles, group * members, TILE), BF16),
        ],
        in_specs=[VMEM] * (1 + len(early)),
        out_specs=[VMEM] * 2,
        compiler_params=pltpu.CompilerParams(vmem_limit_bytes=18 << 20),
        name="collect",
    )(gathered, *early)
    increments = pl.pallas_call(
        analysis_kernel,
        out_shape=jax.ShapeDtypeStruct((group, tiles * members, TILE), BF16),
        in_specs=[SMEM] * 3 + [VMEM] * (3 + 2 * late),
        out_specs=VMEM,
        scratch_shapes=[pltpu.VMEM((2, sum(v.shape[0] for v in own[-late:]), *packed.shape[1:]), BF16)],
        compiler_params=pltpu.CompilerParams(vmem_limit_bytes=18 << 20),
        name="analysis",
    )(anom_at, weight_at, tapers, turned, centred, held_early, *own[-late:], *swapped[-late:])
    returned = lax.all_to_all(increments, "mem", split_axis=0, concat_axis=0, tiled=True)

    return pl.pallas_call(
        final_kernel,
        grid=(rows // 8,),
        out_shape=jax.ShapeDtypeStruct((members, rows, columns), F32),
        in_specs=[VMEM] * 2 + [pl.BlockSpec((8, columns), lambda i: (i, 0))],
        out_specs=pl.BlockSpec((members, 8, columns), lambda i: (0, i, 0)),
        scratch_shapes=[pltpu.VMEM((10, members, columns), F32)],
        compiler_params=pltpu.CompilerParams(vmem_limit_bytes=10 << 20),
        name="final_step",
    )(prior, returned, spreading_coefficient)


def solution(mesh):
    placed = (
        P("mem", "state", None),
        P("state", None),
        P("state", None, None),
        P("state", None, None),
        P(),
        P("state", None),
        P("state", None),
    )
    return jax.shard_map(
        body, mesh=mesh, in_specs=placed, out_specs=P("mem", "state", None), check_vma=False
    )
```
